32 devices in a mesh: grp: 2 (over y), mom: 16 (over z, x, core).
Axes of the slice: x: 2, y: 2, z: 4, core: 2. Of those that a mesh axis runs over, the one named last changes fastest.
Arguments:
- lesser: bfloat16 [4, 1, 64, 256, 512], P('grp', None, 'mom'), may hold values from -6 to 6
- greater: bfloat16 [4, 1, 64, 256, 512], P('grp', None, 'mom'), may hold values from -6 to 6
- coupling: float32 [4, 4, 64], replicated, may hold values from 0.002 to 0.2
- occupation: float32 [4], replicated, may hold values from 0.1 to 2
- shift: int32 [4], replicated, may hold values from 1 to 2, as said below
- region_map: int32 [1], replicated, may hold values from 0 to 3
Outputs:
- lesser_self: bfloat16 [4, 1, 64, 256, 512], P('grp', None, 'mom')
- greater_self: bfloat16 [4, 1, 64, 256, 512], P('grp', None, 'mom')
The draws below stay inside these ranges and needn't reach their ends.
Inputs may be any that keep to these rules, and one draw needn't show every extreme that they name: Some mode has shift 2.
All inputs are finite; a program needn't handle non-finite values.
Results may differ from the reference program's by a relative error of at most 0.0053.
Values may be sent and summed in bfloat16 or wider, within the bound.
No kernel may reach another device: no remote copies, remote signals or barrier semaphores. Data moves between devices by JAX's collectives and lax.ppermute only.
A program may use at most 128 MiB of HBM per device.

```python
import math
import jax
import jax.numpy as jnp
from jax import lax

B = 256
NK = 64
NBLK = 1
SMAX = 2
MODES = 4
REGIONS = 4
NE = 4


def draw_shift(key, part):
    key = jax.random.fold_in(key, 7)
    draw_key, pick_key = jax.random.split(key)
    values = jax.random.randint(draw_key, (MODES,), 1, SMAX + 1)
    chosen = jax.random.randint(pick_key, (), 0, MODES)
    return jnp.where(jnp.arange(MODES) == chosen, SMAX, values).astype(jnp.int32)


def steps_of(key, dims, cuts, least, high):
    level, own = 1.0, jax.random.fold_in(key, 6)
    for axis_at, shards_of in cuts:
        steps = jnp.exp(jax.random.uniform(jax.random.fold_in(own, axis_at), (shards_of,), jnp.float32, least / len(cuts), high / len(cuts)))
        level = level * jnp.repeat(steps, dims[axis_at] // shards_of).reshape([-1 if axis == axis_at else 1 for axis in range(len(dims))])
    return level


def centred(rng, shape, spread, bound, cuts=(), held_as=jnp.bfloat16):
    loudness = steps_of(rng, shape, cuts, -0.22, 0.18) if cuts else 1.0
    values = jax.random.normal(rng, shape, jnp.float32) * spread * loudness
    return jnp.minimum(jnp.maximum(values, -bound), bound).astype(held_as)


def setup_inputs(seed: int = 0) -> dict:
    key_of = jax.random.split(jax.random.key(seed), 7)
    lesser = centred(key_of[0], (NE, NBLK, NK, B, 2 * B), 1.0, 6.0, ((0, 2), (2, 16)))
    greater = centred(key_of[1], (NE, NBLK, NK, B, 2 * B), 1.0, 6.0, ((0, 2), (2, 16)))
    coupling = jnp.clip(jnp.exp(jax.random.uniform(key_of[2], (REGIONS, MODES, NK), jnp.float32, math.log(0.002), math.log(0.2))), 0.002, 0.2)
    occupation = jnp.clip(jnp.exp(jax.random.uniform(key_of[3], (MODES,), jnp.float32, math.log(0.1), math.log(2.0))), 0.1, 2.0)
    shift = draw_shift(jax.random.fold_in(key_of[6], 71), 0)
    region_map = jax.random.randint(key_of[5], (NBLK,), 0, REGIONS).astype(jnp.int32)
    return {"lesser": lesser, "greater": greater, "coupling": coupling, "occupation": occupation, "shift": shift, "region_map": region_map}


def dft_basis(points):
    row_index = lax.broadcasted_iota(jnp.int32, (points, points), 0)
    col_index = lax.broadcasted_iota(jnp.int32, (points, points), 1)
    angles = ((row_index * col_index) % points).astype(jnp.float32) * (2.0 * math.pi / points)
    return jnp.concatenate([jnp.cos(angles), jnp.sin(angles)], axis=0)


def forward(stacked, basis_low):
    points = stacked.shape[3]
    columns = stacked.shape[5] // 2
    mixture = jnp.einsum('pk,aebkxw->aebpxw', basis_low.astype(jnp.float32), stacked.astype(jnp.float32))
    cosine = mixture[:, :, :, :points]
    sine = mixture[:, :, :, points:]
    return cosine[..., :columns] + sine[..., columns:], cosine[..., columns:] - sine[..., :columns]


def combine(hat_real, hat_imag, spec_real, spec_imag, occupation, shift, energies):
    out_shape = (2, energies) + hat_real.shape[2:]
    sigma_real = jnp.zeros(out_shape, jnp.float32)
    sigma_imag = jnp.zeros(out_shape, jnp.float32)
    points = spec_real.shape[2]
    for phonon in range(occupation.shape[0]):
        offset = shift[phonon]
        filling = occupation[phonon]
        lower_real = lax.dynamic_slice_in_dim(hat_real, SMAX - offset, energies, 1)
        lower_imag = lax.dynamic_slice_in_dim(hat_imag, SMAX - offset, energies, 1)
        upper_real = lax.dynamic_slice_in_dim(hat_real, SMAX + offset, energies, 1)
        upper_imag = lax.dynamic_slice_in_dim(hat_imag, SMAX + offset, energies, 1)
        weight_low = jnp.stack([filling, filling + 1.0]).reshape(2, 1, 1, 1, 1, 1)
        weight_high = jnp.stack([filling + 1.0, filling]).reshape(2, 1, 1, 1, 1, 1)
        mixed_real = weight_low * lower_real + weight_high * upper_real
        mixed_imag = weight_low * lower_imag + weight_high * upper_imag
        factor_real = spec_real[:, phonon, :].reshape(1, 1, -1, points, 1, 1)
        factor_imag = spec_imag[:, phonon, :].reshape(1, 1, -1, points, 1, 1)
        sigma_real = sigma_real + factor_real * mixed_real - factor_imag * mixed_imag
        sigma_imag = sigma_imag + factor_real * mixed_imag + factor_imag * mixed_real
    return sigma_real, sigma_imag


def inverse(sigma_real, sigma_imag, basis_low):
    points = sigma_real.shape[3]
    columns = sigma_real.shape[5]
    spectral = jnp.concatenate([sigma_real, sigma_imag], axis=-1).astype(jnp.bfloat16)
    mixture = jnp.einsum('pk,aebkxw->aebpxw', basis_low.astype(jnp.float32), spectral.astype(jnp.float32))
    cosine = mixture[:, :, :, :points]
    sine = mixture[:, :, :, points:]
    real_part = cosine[..., :columns] - sine[..., columns:]
    imag_part = cosine[..., columns:] + sine[..., :columns]
    return (jnp.concatenate([real_part, imag_part], axis=-1) * (1.0 / points)).astype(jnp.bfloat16)


def reference(lesser, greater, coupling, occupation, shift, region_map):
    basis = dft_basis(NK)
    basis_low = basis.astype(jnp.bfloat16)
    chosen = coupling[region_map]
    spectrum = jnp.einsum('pq,bmq->bmp', basis, chosen, precision=lax.Precision.HIGHEST)
    spec_real = spectrum[:, :, :NK]
    spec_imag = -spectrum[:, :, NK:]
    row_span = min(8, B)

    def one_block(block_index):
        first_row = block_index * row_span
        row_slab = jnp.stack([lax.dynamic_slice_in_dim(lesser, first_row, row_span, 3),
                              lax.dynamic_slice_in_dim(greater, first_row, row_span, 3)])
        padded = jnp.pad(row_slab, ((0, 0), (SMAX, SMAX), (0, 0), (0, 0), (0, 0), (0, 0)))
        hat_real, hat_imag = forward(padded, basis_low)
        sigma_real, sigma_imag = combine(hat_real, hat_imag, spec_real, spec_imag, occupation, shift, NE)
        return inverse(sigma_real, sigma_imag, basis_low)

    pieces = lax.map(one_block, jnp.arange(B // row_span, dtype=jnp.int32))
    pieces = jnp.moveaxis(pieces, 0, 4).reshape(2, NE, NBLK, NK, B, 2 * B)
    return pieces[0], pieces[1]
```

```python
import functools
import math

import jax
import jax.numpy as jnp
import numpy as np
from jax import lax
from jax.experimental import pallas as pl
from jax.experimental.pallas import tpu as pltpu
from jax.sharding import PartitionSpec as P

SMAX = 2
TILE = 16
VMEM_BYTES = 40 * 1024 * 1024
APART = 1 << 16


def permutation(energies, momenta, rows):
    inner = energies * momenta
    size = inner * rows
    matrix = np.zeros((size, size), np.float32)
    for state in range(inner):
        for row in range(rows):
            matrix[row * inner + state, state * rows + row] = 1.0
    return matrix


def pack_kernel(perm_ref, lesser_ref, greater_ref, out_ref):
    for side, ref in enumerate((lesser_ref, greater_ref)):
        for piece in range(out_ref.shape[1]):
            rows = out_ref.shape[2] // (ref.shape[0] * ref.shape[2])
            block = ref[:, :, :, piece * rows : (piece + 1) * rows, :]
            block = block.reshape(out_ref.shape[2], out_ref.shape[3])
            moved = jnp.dot(perm_ref[...], block, preferred_element_type=jnp.float32)
            out_ref[side, piece] = moved.astype(out_ref.dtype)


def unpack_kernel(perm_ref, in_ref, lesser_ref, greater_ref):
    for side, ref in enumerate((lesser_ref, greater_ref)):
        for piece in range(in_ref.shape[1]):
            rows = in_ref.shape[2] // (ref.shape[0] * ref.shape[2])
            moved = jnp.dot(
                perm_ref[...], in_ref[side, piece], preferred_element_type=jnp.float32
            )
            moved = moved.astype(ref.dtype).reshape(
                ref.shape[0], 1, ref.shape[2], rows, ref.shape[4]
            )
            ref[:, :, :, piece * rows : (piece + 1) * rows, :] = moved


def mix_kernel(matrix_ref, in_ref, out_ref):
    devices, rows, columns = in_ref.shape
    block = in_ref[...].reshape(devices * rows, columns)
    mixed = jnp.dot(matrix_ref[...], block, preferred_element_type=jnp.float32)
    out_ref[...] = mixed.astype(out_ref.dtype).reshape(devices, rows, columns)


def build_kernel(
    region_ref, side_ref, shift_ref, occupation_ref, coupling_ref, pick_ref, down_ref, across_ref, out_ref
):
    points = pick_ref.shape[1]
    modes = coupling_ref.shape[1]
    chosen = coupling_ref[region_ref[0]]
    greater = side_ref[0].astype(jnp.float32)
    apart = down_ref[...] - across_ref[...]
    total = jnp.zeros(out_ref.shape, jnp.float32)
    for step in range(-SMAX, SMAX + 1):
        if step == 0:
            continue
        row = jnp.zeros((1, 2 * points), jnp.float32)
        for mode in range(modes):
            filling = occupation_ref[mode] + (greater if step > 0 else 1.0 - greater)
            weight = jnp.where(shift_ref[mode] == abs(step), filling, 0.0)
            row = row + weight * chosen[mode : mode + 1, :]
        wide = jnp.broadcast_to(row, (points, 2 * points))
        turned = pltpu.roll(wide, 0, 1, stride=1, stride_axis=0)[:, :points]
        half = jnp.dot(
            pick_ref[...], turned.astype(jnp.bfloat16), preferred_element_type=jnp.float32
        ).astype(jnp.bfloat16)
        full = lax.dot_general(
            pick_ref[...], half, (((1,), (1,)), ((), ())), preferred_element_type=jnp.float32
        )
        total = jnp.where(apart == step, full, total)
    out_ref[...] = total.astype(out_ref.dtype)


def params():
    return pltpu.CompilerParams(vmem_limit_bytes=VMEM_BYTES)


def build(coupling, occupation, shift, region_map, side, groups, shares, energies, momenta, fold):
    devices = groups * shares
    points = shares * momenta
    group, share, row, energy, momentum = np.unravel_index(
        np.arange(devices * fold * energies * momenta), (groups, shares, fold, energies, momenta)
    )
    code = (row * APART + group * energies + energy).astype(np.int32)
    pick = (share * momenta + momentum)[:, None] == np.arange(points)[None, :]
    size = code.size
    scalars = pl.BlockSpec(memory_space=pltpu.SMEM)
    vectors = pl.BlockSpec(memory_space=pltpu.VMEM)
    return pl.pallas_call(
        build_kernel,
        out_shape=jax.ShapeDtypeStruct((size, size), jnp.bfloat16),
        in_specs=[scalars] * 4 + [vectors] * 4,
        out_specs=vectors,
        compiler_params=params(),
        name="build",
    )(
        region_map,
        side.reshape(1),
        shift,
        occupation,
        jnp.concatenate([coupling, coupling], axis=2),
        jnp.asarray(pick, jnp.bfloat16),
        jnp.asarray(code[:, None]),
        jnp.asarray(code[None, :]),
    )


def pack(lesser, greater, pieces, rows, batch):
    energies, _, momenta, _, columns = lesser.shape
    size = energies * momenta * rows
    perm = jnp.asarray(permutation(energies, momenta, rows), jnp.bfloat16)
    slab = pl.BlockSpec((energies, 1, momenta, batch * rows, columns), lambda i: (0, 0, 0, i, 0))
    return pl.pallas_call(
        pack_kernel,
        grid=(pieces // batch,),
        out_shape=jax.ShapeDtypeStruct((2, pieces, size, columns), lesser.dtype),
        in_specs=[pl.BlockSpec((size, size), lambda i: (0, 0)), slab, slab],
        out_specs=pl.BlockSpec((2, batch, size, columns), lambda i: (0, i, 0, 0)),
        compiler_params=params(),
        name="pack",
    )(perm, lesser, greater)


def unpack(packed, shape, pieces, rows, batch):
    energies, _, momenta, _, columns = shape
    size = energies * momenta * rows
    perm = jnp.asarray(permutation(energies, momenta, rows).T, jnp.bfloat16)
    slab = pl.BlockSpec((energies, 1, momenta, batch * rows, columns), lambda i: (0, 0, 0, i, 0))
    out = jax.ShapeDtypeStruct(shape, packed.dtype)
    return pl.pallas_call(
        unpack_kernel,
        grid=(pieces // batch,),
        out_shape=(out, out),
        in_specs=[
            pl.BlockSpec((size, size), lambda i: (0, 0)),
            pl.BlockSpec((2, batch, size, columns), lambda i: (0, i, 0, 0)),
        ],
        out_specs=(slab, slab),
        compiler_params=params(),
        name="unpack",
    )(perm, packed)


def mix(matrix, received):
    devices, size, columns = received.shape
    block = pl.BlockSpec((devices, TILE, columns), lambda i: (0, i, 0))
    return pl.pallas_call(
        mix_kernel,
        grid=(size // TILE,),
        out_shape=jax.ShapeDtypeStruct(received.shape, received.dtype),
        in_specs=[pl.BlockSpec(matrix.shape, lambda i: (0, 0)), block],
        out_specs=block,
        compiler_params=params(),
        name="mix",
    )(matrix, received)


def by_rows(lesser, greater, coupling, occupation, shift, region_map, groups, shares):
    energies, _, momenta, height, columns = lesser.shape
    devices = groups * shares
    pieces = devices // 2
    rows = height // pieces
    batch = 2 if pieces % 2 == 0 else 1
    side = (lax.axis_index(("grp", "mom")) // pieces).astype(jnp.int32)
    fold = TILE // (energies * momenta)
    matrix = build(
        coupling, occupation, shift, region_map, side, groups, shares, energies, momenta, fold
    )
    sent = pack(lesser, greater, pieces, rows, batch)
    sent = sent.reshape((devices,) + sent.shape[2:])
    received = lax.all_to_all(sent, ("grp", "mom"), split_axis=0, concat_axis=0, tiled=True)
    mixed = mix(matrix, received)
    returned = lax.all_to_all(mixed, ("grp", "mom"), split_axis=0, concat_axis=0, tiled=True)
    returned = returned.reshape((2, pieces) + returned.shape[1:])
    return unpack(returned, lesser.shape, pieces, rows, batch)


def with_halo(shard, sides, width):
    for axis, dim in sides:
        size, length = (lax.axis_size(axis), shard.shape[dim])
        up = [(i, (i + 1) % size) for i in range(size - 1)]
        down = [(j, i) for i, j in up]
        last = lax.slice_in_dim(shard, length - width, length, axis=dim)
        first = lax.slice_in_dim(shard, 0, width, axis=dim)
        before = lax.ppermute(last, axis, up)
        after = lax.ppermute(first, axis, down)
        shard = jnp.concatenate([before, shard, after], axis=dim)
    return shard


def dft_basis(points):
    row_index = lax.broadcasted_iota(jnp.int32, (points, points), 0)
    col_index = lax.broadcasted_iota(jnp.int32, (points, points), 1)
    angles = (row_index * col_index % points).astype(jnp.float32) * (2.0 * math.pi / points)
    return jnp.concatenate([jnp.cos(angles), jnp.sin(angles)], axis=0)


def coupling_spectrum(coupling, region_map, basis):
    regions = coupling.shape[0]
    points = coupling.shape[2]
    onehot = (region_map[:, None] == jnp.arange(regions, dtype=jnp.int32)[None, :]).astype(
        jnp.float32
    )
    chosen = jnp.einsum("br,rmq->bmq", onehot, coupling, precision=lax.Precision.HIGHEST)
    spectrum = jnp.einsum("pq,bmq->bmp", basis, chosen, precision=lax.Precision.HIGHEST)
    return (spectrum[:, :, :points], -spectrum[:, :, points:])


def forward(stacked, basis_low):
    points = stacked.shape[3]
    columns = stacked.shape[5] // 2
    mixture = jnp.einsum(
        "pk,aebkxw->aebpxw", basis_low, stacked, preferred_element_type=jnp.float32
    )
    cosine = mixture[:, :, :, :points]
    sine = mixture[:, :, :, points:]
    return (
        cosine[..., :columns] + sine[..., columns:],
        cosine[..., columns:] - sine[..., :columns],
    )


def combine(hat_real, hat_imag, spec_real, spec_imag, occupation, shift, energies):
    out_shape = (2, energies) + hat_real.shape[2:]
    sigma_real = jnp.zeros(out_shape, jnp.float32)
    sigma_imag = jnp.zeros(out_shape, jnp.float32)
    points = spec_real.shape[2]
    for phonon in range(occupation.shape[0]):
        offset = shift[phonon]
        filling = occupation[phonon]
        lower_real = lax.dynamic_slice_in_dim(hat_real, SMAX - offset, energies, 1)
        lower_imag = lax.dynamic_slice_in_dim(hat_imag, SMAX - offset, energies, 1)
        upper_real = lax.dynamic_slice_in_dim(hat_real, SMAX + offset, energies, 1)
        upper_imag = lax.dynamic_slice_in_dim(hat_imag, SMAX + offset, energies, 1)
        weight_low = jnp.stack([filling, filling + 1.0]).reshape(2, 1, 1, 1, 1, 1)
        weight_high = jnp.stack([filling + 1.0, filling]).reshape(2, 1, 1, 1, 1, 1)
        mixed_real = weight_low * lower_real + weight_high * upper_real
        mixed_imag = weight_low * lower_imag + weight_high * upper_imag
        factor_real = spec_real[:, phonon, :].reshape(1, 1, -1, points, 1, 1)
        factor_imag = spec_imag[:, phonon, :].reshape(1, 1, -1, points, 1, 1)
        sigma_real = sigma_real + factor_real * mixed_real - factor_imag * mixed_imag
        sigma_imag = sigma_imag + factor_real * mixed_imag + factor_imag * mixed_real
    return (sigma_real, sigma_imag)


def inverse(sigma_real, sigma_imag, basis_low):
    points = sigma_real.shape[3]
    columns = sigma_real.shape[5]
    spectral = jnp.concatenate([sigma_real, sigma_imag], axis=-1).astype(jnp.bfloat16)
    mixture = jnp.einsum(
        "pk,aebkxw->aebpxw", basis_low, spectral, preferred_element_type=jnp.float32
    )
    cosine = mixture[:, :, :, :points]
    sine = mixture[:, :, :, points:]
    real_part = cosine[..., :columns] - sine[..., columns:]
    imag_part = cosine[..., columns:] + sine[..., :columns]
    return (jnp.concatenate([real_part, imag_part], axis=-1) * (1.0 / points)).astype(jnp.bfloat16)


def by_groups(lesser, greater, coupling, occupation, shift, region_map):
    stacked = jnp.stack([lesser, greater])
    widened = with_halo(stacked, (("grp", 1),), SMAX)
    regrouped = lax.all_to_all(widened, "mom", split_axis=4, concat_axis=3, tiled=True)
    points = regrouped.shape[3]
    basis = dft_basis(points)
    basis_low = basis.astype(jnp.bfloat16)
    spec_real, spec_imag = coupling_spectrum(coupling, region_map, basis)
    hat_real, hat_imag = forward(regrouped, basis_low)
    sigma_real, sigma_imag = combine(
        hat_real, hat_imag, spec_real, spec_imag, occupation, shift, lesser.shape[0]
    )
    result = inverse(sigma_real, sigma_imag, basis_low)
    returned = lax.all_to_all(result, "mom", split_axis=3, concat_axis=4, tiled=True)
    return (returned[0], returned[1])


def on_device(groups, shares, lesser, greater, coupling, occupation, shift, region_map):
    energies, blocks, momenta, height, columns = lesser.shape
    devices = groups * shares
    states = energies * momenta
    whole_tiles = (
        blocks == 1
        and devices % 2 == 0
        and height % (TILE * (devices // 2)) == 0
        and TILE % states == 0
        and columns % 128 == 0
    )
    if whole_tiles:
        return by_rows(
            lesser, greater, coupling, occupation, shift, region_map, groups, shares
        )
    return by_groups(lesser, greater, coupling, occupation, shift, region_map)


def solution(mesh):
    return jax.shard_map(
        functools.partial(on_device, mesh.shape["grp"], mesh.shape["mom"]),
        mesh=mesh,
        in_specs=(
            P("grp", None, "mom", None, None),
            P("grp", None, "mom", None, None),
            P(),
            P(),
            P(),
            P(),
        ),
        out_specs=(P("grp", None, "mom", None, None), P("grp", None, "mom", None, None)),
        check_vma=False,
    )
```

```python
import functools
import math

import jax
import jax.numpy as jnp
import numpy as np
from jax import lax
from jax.experimental import pallas as pl
from jax.experimental.pallas import tpu as pltpu
from jax.sharding import PartitionSpec as P

SMAX = 2
TILE = 16
VMEM_BYTES = 60 * 1024 * 1024
APART = 1 << 16


def permutation(energies, momenta, rows):
    inner = energies * momenta
    size = inner * rows
    matrix = np.zeros((size, size), np.float32)
    for state in range(inner):
        for row in range(rows):
            matrix[row * inner + state, state * rows + row] = 1.0
    return matrix


def pack_kernel(perm_ref, lesser_ref, greater_ref, out_ref):
    for side, ref in enumerate((lesser_ref, greater_ref)):
        for piece in range(out_ref.shape[1]):
            rows = out_ref.shape[2] // (ref.shape[0] * ref.shape[2])
            block = ref[:, :, :, piece * rows : (piece + 1) * rows, :]
            block = block.reshape(out_ref.shape[2], out_ref.shape[3])
            moved = jnp.dot(perm_ref[...], block, preferred_element_type=jnp.float32)
            out_ref[side, piece] = moved.astype(out_ref.dtype)


def unpack_kernel(perm_ref, in_ref, *refs):
    for side, ref in enumerate(refs[-2:]):
        for piece in range(in_ref.shape[1]):
            rows = in_ref.shape[2] // (ref.shape[0] * ref.shape[2])
            moved = jnp.dot(
                perm_ref[...], in_ref[side, piece], preferred_element_type=jnp.float32
            )
            moved = moved.astype(ref.dtype).reshape(
                ref.shape[0], 1, ref.shape[2], rows, ref.shape[4]
            )
            ref[:, :, :, piece * rows : (piece + 1) * rows, :] = moved


def mix_kernel(matrix_ref, in_ref, out_ref):
    devices, rows, columns = in_ref.shape
    for start in range(0, rows, TILE):
        block = in_ref[:, start : start + TILE, :].reshape(devices * TILE, columns)
        mixed = jnp.dot(matrix_ref[...], block, preferred_element_type=jnp.float32)
        out_ref[:, start : start + TILE, :] = mixed.astype(out_ref.dtype).reshape(
            devices, TILE, columns
        )


def build_kernel(
    region_ref, side_ref, shift_ref, occupation_ref, coupling_ref, pick_ref, down_ref, across_ref, out_ref
):
    points = pick_ref.shape[1]
    modes = coupling_ref.shape[1]
    chosen = coupling_ref[region_ref[0]]
    greater = side_ref[0].astype(jnp.float32)
    apart = down_ref[...] - across_ref[...]
    total = jnp.zeros(out_ref.shape, jnp.float32)
    for step in range(-SMAX, SMAX + 1):
        if step == 0:
            continue
        row = jnp.zeros((1, 2 * points), jnp.float32)
        for mode in range(modes):
            filling = occupation_ref[mode] + (greater if step > 0 else 1.0 - greater)
            weight = jnp.where(shift_ref[mode] == abs(step), filling, 0.0)
            row = row + weight * chosen[mode : mode + 1, :]
        wide = jnp.broadcast_to(row, (points, 2 * points))
        turned = pltpu.roll(wide, 0, 1, stride=1, stride_axis=0)[:, :points]
        half = jnp.dot(
            pick_ref[...], turned.astype(jnp.bfloat16), preferred_element_type=jnp.float32
        ).astype(jnp.bfloat16)
        full = lax.dot_general(
            pick_ref[...], half, (((1,), (1,)), ((), ())), preferred_element_type=jnp.float32
        )
        total = jnp.where(apart == step, full, total)
    out_ref[...] = total.astype(out_ref.dtype)


def params():
    return pltpu.CompilerParams(vmem_limit_bytes=VMEM_BYTES)


def build(coupling, occupation, shift, region_map, side, groups, shares, energies, momenta, fold):
    devices = groups * shares
    points = shares * momenta
    group, share, row, energy, momentum = np.unravel_index(
        np.arange(devices * fold * energies * momenta), (groups, shares, fold, energies, momenta)
    )
    code = (row * APART + group * energies + energy).astype(np.int32)
    pick = (share * momenta + momentum)[:, None] == np.arange(points)[None, :]
    size = code.size
    scalars = pl.BlockSpec(memory_space=pltpu.SMEM)
    vectors = pl.BlockSpec(memory_space=pltpu.VMEM)
    return pl.pallas_call(
        build_kernel,
        out_shape=jax.ShapeDtypeStruct((size, size), jnp.bfloat16),
        in_specs=[scalars] * 4 + [vectors] * 4,
        out_specs=vectors,
        compiler_params=params(),
        name="build",
    )(
        region_map,
        side.reshape(1),
        shift,
        occupation,
        jnp.concatenate([coupling, coupling], axis=2),
        jnp.asarray(pick, jnp.bfloat16),
        jnp.asarray(code[:, None]),
        jnp.asarray(code[None, :]),
    )


def slab_spec(shape, rows, width, chunk):
    energies, _, momenta, _, _ = shape
    return pl.BlockSpec((energies, 1, momenta, rows, width), lambda i: (0, 0, 0, i, chunk))


def pack(lesser, greater, pieces, rows, batch, width, chunk):
    energies, _, momenta, _, _ = lesser.shape
    size = energies * momenta * rows
    perm = jnp.asarray(permutation(energies, momenta, rows), jnp.bfloat16)
    slab = slab_spec(lesser.shape, batch * rows, width, chunk)
    return pl.pallas_call(
        pack_kernel,
        grid=(pieces // batch,),
        out_shape=jax.ShapeDtypeStruct((2, pieces, size, width), lesser.dtype),
        in_specs=[pl.BlockSpec((size, size), lambda i: (0, 0)), slab, slab],
        out_specs=pl.BlockSpec((2, batch, size, width), lambda i: (0, i, 0, 0)),
        compiler_params=params(),
        name="pack",
    )(perm, lesser, greater)


def unpack(packed, filled, shape, pieces, rows, batch, width, chunk):
    energies, _, momenta, _, _ = shape
    size = energies * momenta * rows
    perm = jnp.asarray(permutation(energies, momenta, rows).T, jnp.bfloat16)
    slab = slab_spec(shape, batch * rows, width, chunk)
    out = jax.ShapeDtypeStruct(shape, packed.dtype)
    return pl.pallas_call(
        unpack_kernel,
        grid=(pieces // batch,),
        out_shape=(out, out),
        in_specs=[
            pl.BlockSpec((size, size), lambda i: (0, 0)),
            pl.BlockSpec((2, batch, size, width), lambda i: (0, i, 0, 0)),
        ]
        + [pl.BlockSpec(memory_space=pl.ANY)] * len(filled),
        out_specs=(slab, slab),
        input_output_aliases={2 + side: side for side in range(len(filled))},
        compiler_params=params(),
        name="unpack",
    )(perm, packed, *filled)


def mix(matrix, received, tall):
    devices, size, width = received.shape
    block = pl.BlockSpec((devices, tall, width), lambda i: (0, i, 0))
    return pl.pallas_call(
        mix_kernel,
        grid=(size // tall,),
        out_shape=jax.ShapeDtypeStruct(received.shape, received.dtype),
        in_specs=[pl.BlockSpec(matrix.shape, lambda i: (0, 0)), block],
        out_specs=block,
        compiler_params=params(),
        name="mix",
    )(matrix, received)


def exchange(array):
    return lax.all_to_all(array, ("grp", "mom"), split_axis=0, concat_axis=0, tiled=True)


def by_rows(lesser, greater, coupling, occupation, shift, region_map, groups, shares):
    energies, _, momenta, height, columns = lesser.shape
    devices = groups * shares
    pieces = devices // 2
    rows = height // pieces
    batch = math.gcd(4, pieces)
    chunks = 2 if columns % 256 == 0 else 1
    width = columns // chunks
    place = lax.axis_index("grp") * shares + lax.axis_index("mom")
    side = lax.div(place, jnp.int32(pieces))
    fold = TILE // (energies * momenta)
    matrix = build(
        coupling, occupation, shift, region_map, side, groups, shares, energies, momenta, fold
    )
    received = []
    for chunk in range(chunks):
        sent = pack(lesser, greater, pieces, rows, batch, width, chunk)
        received.append(exchange(sent.reshape((devices,) + sent.shape[2:])))
    returned = [exchange(mix(matrix, part, 2 * TILE)) for part in received]
    filled = ()
    for chunk, part in enumerate(returned):
        part = part.reshape((2, pieces) + part.shape[1:])
        filled = unpack(part, filled, lesser.shape, pieces, rows, batch, width, chunk)
    return filled


def with_halo(shard, sides, width):
    for axis, dim in sides:
        size, length = (lax.axis_size(axis), shard.shape[dim])
        up = [(i, (i + 1) % size) for i in range(size - 1)]
        down = [(j, i) for i, j in up]
        last = lax.slice_in_dim(shard, length - width, length, axis=dim)
        first = lax.slice_in_dim(shard, 0, width, axis=dim)
        before = lax.ppermute(last, axis, up)
        after = lax.ppermute(first, axis, down)
        shard = jnp.concatenate([before, shard, after], axis=dim)
    return shard


def dft_basis(points):
    row_index = lax.broadcasted_iota(jnp.int32, (points, points), 0)
    col_index = lax.broadcasted_iota(jnp.int32, (points, points), 1)
    angles = (row_index * col_index % points).astype(jnp.float32) * (2.0 * math.pi / points)
    return jnp.concatenate([jnp.cos(angles), jnp.sin(angles)], axis=0)


def coupling_spectrum(coupling, region_map, basis):
    regions = coupling.shape[0]
    points = coupling.shape[2]
    onehot = (region_map[:, None] == jnp.arange(regions, dtype=jnp.int32)[None, :]).astype(
        jnp.float32
    )
    chosen = jnp.einsum("br,rmq->bmq", onehot, coupling, precision=lax.Precision.HIGHEST)
    spectrum = jnp.einsum("pq,bmq->bmp", basis, chosen, precision=lax.Precision.HIGHEST)
    return (spectrum[:, :, :points], -spectrum[:, :, points:])


def forward(stacked, basis_low):
    points = stacked.shape[3]
    columns = stacked.shape[5] // 2
    mixture = jnp.einsum(
        "pk,aebkxw->aebpxw", basis_low, stacked, preferred_element_type=jnp.float32
    )
    cosine = mixture[:, :, :, :points]
    sine = mixture[:, :, :, points:]
    return (
        cosine[..., :columns] + sine[..., columns:],
        cosine[..., columns:] - sine[..., :columns],
    )


def combine(hat_real, hat_imag, spec_real, spec_imag, occupation, shift, energies):
    out_shape = (2, energies) + hat_real.shape[2:]
    sigma_real = jnp.zeros(out_shape, jnp.float32)
    sigma_imag = jnp.zeros(out_shape, jnp.float32)
    points = spec_real.shape[2]
    for phonon in range(occupation.shape[0]):
        offset = shift[phonon]
        filling = occupation[phonon]
        lower_real = lax.dynamic_slice_in_dim(hat_real, SMAX - offset, energies, 1)
        lower_imag = lax.dynamic_slice_in_dim(hat_imag, SMAX - offset, energies, 1)
        upper_real = lax.dynamic_slice_in_dim(hat_real, SMAX + offset, energies, 1)
        upper_imag = lax.dynamic_slice_in_dim(hat_imag, SMAX + offset, energies, 1)
        weight_low = jnp.stack([filling, filling + 1.0]).reshape(2, 1, 1, 1, 1, 1)
        weight_high = jnp.stack([filling + 1.0, filling]).reshape(2, 1, 1, 1, 1, 1)
        mixed_real = weight_low * lower_real + weight_high * upper_real
        mixed_imag = weight_low * lower_imag + weight_high * upper_imag
        factor_real = spec_real[:, phonon, :].reshape(1, 1, -1, points, 1, 1)
        factor_imag = spec_imag[:, phonon, :].reshape(1, 1, -1, points, 1, 1)
        sigma_real = sigma_real + factor_real * mixed_real - factor_imag * mixed_imag
        sigma_imag = sigma_imag + factor_real * mixed_imag + factor_imag * mixed_real
    return (sigma_real, sigma_imag)


def inverse(sigma_real, sigma_imag, basis_low):
    points = sigma_real.shape[3]
    columns = sigma_real.shape[5]
    spectral = jnp.concatenate([sigma_real, sigma_imag], axis=-1).astype(jnp.bfloat16)
    mixture = jnp.einsum(
        "pk,aebkxw->aebpxw", basis_low, spectral, preferred_element_type=jnp.float32
    )
    cosine = mixture[:, :, :, :points]
    sine = mixture[:, :, :, points:]
    real_part = cosine[..., :columns] - sine[..., columns:]
    imag_part = cosine[..., columns:] + sine[..., :columns]
    return (jnp.concatenate([real_part, imag_part], axis=-1) * (1.0 / points)).astype(jnp.bfloat16)


def by_groups(lesser, greater, coupling, occupation, shift, region_map):
    stacked = jnp.stack([lesser, greater])
    widened = with_halo(stacked, (("grp", 1),), SMAX)
    regrouped = lax.all_to_all(widened, "mom", split_axis=4, concat_axis=3, tiled=True)
    points = regrouped.shape[3]
    basis = dft_basis(points)
    basis_low = basis.astype(jnp.bfloat16)
    spec_real, spec_imag = coupling_spectrum(coupling, region_map, basis)
    hat_real, hat_imag = forward(regrouped, basis_low)
    sigma_real, sigma_imag = combine(
        hat_real, hat_imag, spec_real, spec_imag, occupation, shift, lesser.shape[0]
    )
    result = inverse(sigma_real, sigma_imag, basis_low)
    returned = lax.all_to_all(result, "mom", split_axis=3, concat_axis=4, tiled=True)
    return (returned[0], returned[1])


def on_device(groups, shares, lesser, greater, coupling, occupation, shift, region_map):
    energies, blocks, momenta, height, columns = lesser.shape
    devices = groups * shares
    states = energies * momenta
    whole_tiles = (
        blocks == 1
        and devices % 2 == 0
        and height % (TILE * (devices // 2)) == 0
        and TILE % states == 0
        and columns % 128 == 0
    )
    if whole_tiles:
        return by_rows(
            lesser, greater, coupling, occupation, shift, region_map, groups, shares
        )
    return by_groups(lesser, greater, coupling, occupation, shift, region_map)


def solution(mesh):
    return jax.shard_map(
        functools.partial(on_device, mesh.shape["grp"], mesh.shape["mom"]),
        mesh=mesh,
        in_specs=(
            P("grp", None, "mom", None, None),
            P("grp", None, "mom", None, None),
            P(),
            P(),
            P(),
            P(),
        ),
        out_specs=(P("grp", None, "mom", None, None), P("grp", None, "mom", None, None)),
        check_vma=False,
    )
```

```python
import functools
import math

import jax
import jax.numpy as jnp
import numpy as np
from jax import lax
from jax.experimental import pallas as pl
from jax.experimental.pallas import tpu as pltpu
from jax.sharding import PartitionSpec as P

SMAX = 2
TILE = 16
VMEM_BYTES = 48 * 1024 * 1024
APART = 1 << 16
AXES = ("grp", "mom")


def permutation(energies, momenta, rows):
    inner = energies * momenta
    size = inner * rows
    matrix = np.zeros((size, size), np.float32)
    for state in range(inner):
        for row in range(rows):
            matrix[row * inner + state, state * rows + row] = 1.0
    return matrix


def place_of(place_ref, pieces, far):
    place = place_ref[0]
    half = pieces // 2
    block = lax.rem(place, jnp.int32(pieces))
    low = lax.rem(block, jnp.int32(half))
    high = lax.div(block, jnp.int32(half))
    return lax.div(place, jnp.int32(pieces)), low, (1 - high if far else high) * half


def pack_kernel(pieces, far, place_ref, perm_ref, lesser_ref, greater_ref, *refs):
    half = pieces // 2
    outs, held, arrived = refs[: 2 * half], refs[-2], refs[-1]
    rows = held.shape[4]
    size, width = outs[0].shape
    side, low, base = place_of(place_ref, pieces, far)
    copies = []
    for step in range(half):
        start = pl.multiple_of((base + (low ^ step)) * rows, rows)
        for which, ref in enumerate((lesser_ref, greater_ref)):
            copy = pltpu.make_async_copy(
                ref.at[:, 0, :, pl.ds(start, rows), :],
                held.at[step, which],
                arrived.at[step, which],
            )
            copy.start()
            copies.append(copy)
    for step in range(half):
        moved = []
        for which in range(2):
            copies[2 * step + which].wait()
            block = held[step, which].reshape(size, width)
            moved.append(jnp.dot(perm_ref[...], block, preferred_element_type=jnp.float32))
        outs[step][...] = jnp.where(side == 0, moved[0], moved[1]).astype(outs[0].dtype)
        outs[half + step][...] = jnp.where(side == 0, moved[1], moved[0]).astype(outs[0].dtype)


def unpack_kernel(pieces, far, place_ref, perm_ref, *refs):
    half = pieces // 2
    ins, held, sent = refs[: 2 * half], refs[-2], refs[-1]
    outs = refs[-4:-2]
    rows = held.shape[4]
    side, low, base = place_of(place_ref, pieces, far)
    copies = []
    for step in range(half):
        own = jnp.dot(perm_ref[...], ins[step][...], preferred_element_type=jnp.float32)
        other = jnp.dot(perm_ref[...], ins[half + step][...], preferred_element_type=jnp.float32)
        start = pl.multiple_of((base + (low ^ step)) * rows, rows)
        for which, ref in enumerate(outs):
            moved = jnp.where(side == which, own, other).astype(held.dtype)
            held[step, which] = moved.reshape(held.shape[2:])
            copy = pltpu.make_async_copy(
                held.at[step, which],
                ref.at[:, 0, :, pl.ds(start, rows), :],
                sent.at[step, which],
            )
            copy.start()
            copies.append(copy)
    for copy in copies:
        copy.wait()


def mix_kernel(count, matrix_ref, *refs):
    ins, outs = refs[:count], refs[count:]
    size, width = ins[0].shape
    for start in range(0, size, TILE):
        block = jnp.concatenate([ref[start : start + TILE, :] for ref in ins], axis=0)
        mixed = jnp.dot(matrix_ref[...], block, preferred_element_type=jnp.float32)
        mixed = mixed.astype(outs[0].dtype)
        for slot, ref in enumerate(outs):
            ref[start : start + TILE, :] = mixed[slot * TILE : (slot + 1) * TILE, :]


def build_kernel(
    shares, momenta, energies, pieces,
    place_ref, region_ref, shift_ref, occupation_ref, coupling_ref, down_ref, across_ref, *out_refs
):
    points = shares * momenta
    modes = coupling_ref.shape[1]
    place = place_ref[0]
    greater = lax.div(place, jnp.int32(pieces)).astype(jnp.float32)
    chosen = coupling_ref[region_ref[0]]
    bits = shares.bit_length() - 1

    def code_of(slot, own):
        return own + ((slot ^ place) >> bits) * energies

    size = down_ref.shape[0]
    momentum = ((down_ref[:, 0:1] ^ place) & (shares - 1)) * momenta + down_ref[:, 2:3]
    pick = momentum == lax.broadcasted_iota(jnp.int32, (size, points), 1)
    pick = jnp.where(pick, 1.0, 0.0).astype(jnp.bfloat16)
    down = code_of(down_ref[:, 0:1], down_ref[:, 1:2])
    across = code_of(across_ref[0:1, :], across_ref[1:2, :])
    apart = down - across
    total = jnp.zeros((size, size), jnp.float32)
    for step in range(-SMAX, SMAX + 1):
        if step == 0:
            continue
        row = jnp.zeros((1, 2 * points), jnp.float32)
        for mode in range(modes):
            filling = occupation_ref[mode] + (greater if step > 0 else 1.0 - greater)
            weight = jnp.where(shift_ref[mode] == abs(step), filling, 0.0)
            row = row + weight * chosen[mode : mode + 1, :]
        wide = jnp.broadcast_to(row, (points, 2 * points))
        turned = pltpu.roll(wide, 0, 1, stride=1, stride_axis=0)[:, :points]
        half = jnp.dot(
            pick, turned.astype(jnp.bfloat16), preferred_element_type=jnp.float32
        ).astype(jnp.bfloat16)
        full = lax.dot_general(
            pick, half, (((1,), (1,)), ((), ())), preferred_element_type=jnp.float32
        )
        total = jnp.where(apart == step, full, total)
    first = out_refs[0].shape[0]
    out_refs[0][...] = total[:first].astype(out_refs[0].dtype)
    out_refs[1][...] = total[first:].astype(out_refs[1].dtype)


def params():
    return pltpu.CompilerParams(vmem_limit_bytes=VMEM_BYTES)


SCALARS = pl.BlockSpec(memory_space=pltpu.SMEM)
VECTORS = pl.BlockSpec(memory_space=pltpu.VMEM)
WHERE_IT_LIES = pl.BlockSpec(memory_space=pl.ANY)


def build(place, coupling, occupation, shift, region_map, slots, shares, energies, momenta, pieces):
    fold = TILE // (energies * momenta)
    slot, row, energy, momentum = np.meshgrid(
        np.asarray(slots), np.arange(fold), np.arange(energies), np.arange(momenta), indexing="ij"
    )
    static = [slot.ravel(), (row * APART + energy).ravel(), momentum.ravel()]
    down = np.stack(static, axis=1).astype(np.int32)
    size = down.shape[0]
    part = jax.ShapeDtypeStruct((size // 2, size), jnp.bfloat16)
    return pl.pallas_call(
        functools.partial(build_kernel, shares, momenta, energies, pieces),
        out_shape=(part, part),
        in_specs=[SCALARS] * 4 + [VECTORS] * 3,
        out_specs=(VECTORS, VECTORS),
        compiler_params=params(),
        name="build",
    )(
        place,
        region_map,
        shift,
        occupation,
        jnp.concatenate([coupling, coupling], axis=2),
        jnp.asarray(down),
        jnp.asarray(down.T),
    )


def pack(place, lesser, greater, pieces, rows, far):
    energies, _, momenta, _, columns = lesser.shape
    size = energies * momenta * rows
    half = pieces // 2
    perm = jnp.asarray(permutation(energies, momenta, rows), jnp.bfloat16)
    piece = jax.ShapeDtypeStruct((size, columns), lesser.dtype)
    return pl.pallas_call(
        functools.partial(pack_kernel, pieces, far),
        out_shape=(piece,) * (2 * half),
        in_specs=[SCALARS, VECTORS, WHERE_IT_LIES, WHERE_IT_LIES],
        out_specs=(VECTORS,) * (2 * half),
        scratch_shapes=[
            pltpu.VMEM((half, 2, energies, momenta, rows, columns), lesser.dtype),
            pltpu.SemaphoreType.DMA((half, 2)),
        ],
        compiler_params=params(),
        name="pack",
    )(place, perm, lesser, greater)


def unpack(place, parts, filled, shape, pieces, rows, far):
    energies, _, momenta, _, columns = shape
    half = pieces // 2
    perm = jnp.asarray(permutation(energies, momenta, rows).T, jnp.bfloat16)
    out = jax.ShapeDtypeStruct(shape, parts[0].dtype)
    return pl.pallas_call(
        functools.partial(unpack_kernel, pieces, far),
        out_shape=(out, out),
        in_specs=[SCALARS, VECTORS] + [VECTORS] * len(parts) + [WHERE_IT_LIES] * len(filled),
        out_specs=(WHERE_IT_LIES, WHERE_IT_LIES),
        scratch_shapes=[
            pltpu.VMEM((half, 2, energies, momenta, rows, columns), parts[0].dtype),
            pltpu.SemaphoreType.DMA((half, 2)),
        ],
        input_output_aliases={2 + len(parts) + side: side for side in range(len(filled))},
        compiler_params=params(),
        name="unpack",
    )(place, perm, *parts, *filled)


def mix(matrix, parts):
    piece = jax.ShapeDtypeStruct(parts[0].shape, parts[0].dtype)
    count = matrix.shape[0] // TILE
    return pl.pallas_call(
        functools.partial(mix_kernel, len(parts)),
        out_shape=(piece,) * count,
        in_specs=[VECTORS] * (1 + len(parts)),
        out_specs=(VECTORS,) * count,
        compiler_params=params(),
        name="mix",
    )(matrix, *parts)


def exchange(parts, slots, devices):
    return [
        part
        if slot == 0
        else lax.ppermute(part, AXES, [(device, device ^ slot) for device in range(devices)])
        for part, slot in zip(parts, slots)
    ]


def by_rows(lesser, greater, coupling, occupation, shift, region_map, groups, shares):
    energies, _, momenta, height, _ = lesser.shape
    devices = groups * shares
    pieces = devices // 2
    half = pieces // 2
    rows = height // pieces
    far = [side * pieces + half + step for side in range(2) for step in range(half)]
    near = [side * pieces + step for side in range(2) for step in range(half)]
    place = (lax.axis_index("grp") * shares + lax.axis_index("mom")).astype(jnp.int32).reshape(1)
    far_in = exchange(pack(place, lesser, greater, pieces, rows, True), far, devices)
    near_in = exchange(pack(place, lesser, greater, pieces, rows, False), near, devices)
    far_matrix, near_matrix = build(
        place, coupling, occupation, shift, region_map, far + near, shares, energies, momenta, pieces
    )
    received = far_in + near_in
    far_out = exchange(mix(far_matrix, received), far, devices)
    near_out = exchange(mix(near_matrix, received), near, devices)
    filled = unpack(place, far_out, (), lesser.shape, pieces, rows, True)
    return unpack(place, near_out, filled, lesser.shape, pieces, rows, False)


def with_halo(shard, sides, width):
    for axis, dim in sides:
        size, length = (lax.axis_size(axis), shard.shape[dim])
        up = [(i, (i + 1) % size) for i in range(size - 1)]
        down = [(j, i) for i, j in up]
        last = lax.slice_in_dim(shard, length - width, length, axis=dim)
        first = lax.slice_in_dim(shard, 0, width, axis=dim)
        before = lax.ppermute(last, axis, up)
        after = lax.ppermute(first, axis, down)
        shard = jnp.concatenate([before, shard, after], axis=dim)
    return shard


def dft_basis(points):
    row_index = lax.broadcasted_iota(jnp.int32, (points, points), 0)
    col_index = lax.broadcasted_iota(jnp.int32, (points, points), 1)
    angles = (row_index * col_index % points).astype(jnp.float32) * (2.0 * math.pi / points)
    return jnp.concatenate([jnp.cos(angles), jnp.sin(angles)], axis=0)


def coupling_spectrum(coupling, region_map, basis):
    regions = coupling.shape[0]
    points = coupling.shape[2]
    onehot = (region_map[:, None] == jnp.arange(regions, dtype=jnp.int32)[None, :]).astype(
        jnp.float32
    )
    chosen = jnp.einsum("br,rmq->bmq", onehot, coupling, precision=lax.Precision.HIGHEST)
    spectrum = jnp.einsum("pq,bmq->bmp", basis, chosen, precision=lax.Precision.HIGHEST)
    return (spectrum[:, :, :points], -spectrum[:, :, points:])


def forward(stacked, basis_low):
    points = stacked.shape[3]
    columns = stacked.shape[5] // 2
    mixture = jnp.einsum(
        "pk,aebkxw->aebpxw", basis_low, stacked, preferred_element_type=jnp.float32
    )
    cosine = mixture[:, :, :, :points]
    sine = mixture[:, :, :, points:]
    return (
        cosine[..., :columns] + sine[..., columns:],
        cosine[..., columns:] - sine[..., :columns],
    )


def combine(hat_real, hat_imag, spec_real, spec_imag, occupation, shift, energies):
    out_shape = (2, energies) + hat_real.shape[2:]
    sigma_real = jnp.zeros(out_shape, jnp.float32)
    sigma_imag = jnp.zeros(out_shape, jnp.float32)
    points = spec_real.shape[2]
    for phonon in range(occupation.shape[0]):
        offset = shift[phonon]
        filling = occupation[phonon]
        lower_real = lax.dynamic_slice_in_dim(hat_real, SMAX - offset, energies, 1)
        lower_imag = lax.dynamic_slice_in_dim(hat_imag, SMAX - offset, energies, 1)
        upper_real = lax.dynamic_slice_in_dim(hat_real, SMAX + offset, energies, 1)
        upper_imag = lax.dynamic_slice_in_dim(hat_imag, SMAX + offset, energies, 1)
        weight_low = jnp.stack([filling, filling + 1.0]).reshape(2, 1, 1, 1, 1, 1)
        weight_high = jnp.stack([filling + 1.0, filling]).reshape(2, 1, 1, 1, 1, 1)
        mixed_real = weight_low * lower_real + weight_high * upper_real
        mixed_imag = weight_low * lower_imag + weight_high * upper_imag
        factor_real = spec_real[:, phonon, :].reshape(1, 1, -1, points, 1, 1)
        factor_imag = spec_imag[:, phonon, :].reshape(1, 1, -1, points, 1, 1)
        sigma_real = sigma_real + factor_real * mixed_real - factor_imag * mixed_imag
        sigma_imag = sigma_imag + factor_real * mixed_imag + factor_imag * mixed_real
    return (sigma_real, sigma_imag)


def inverse(sigma_real, sigma_imag, basis_low):
    points = sigma_real.shape[3]
    columns = sigma_real.shape[5]
    spectral = jnp.concatenate([sigma_real, sigma_imag], axis=-1).astype(jnp.bfloat16)
    mixture = jnp.einsum(
        "pk,aebkxw->aebpxw", basis_low, spectral, preferred_element_type=jnp.float32
    )
    cosine = mixture[:, :, :, :points]
    sine = mixture[:, :, :, points:]
    real_part = cosine[..., :columns] - sine[..., columns:]
    imag_part = cosine[..., columns:] + sine[..., :columns]
    return (jnp.concatenate([real_part, imag_part], axis=-1) * (1.0 / points)).astype(jnp.bfloat16)


def by_groups(lesser, greater, coupling, occupation, shift, region_map):
    stacked = jnp.stack([lesser, greater])
    widened = with_halo(stacked, (("grp", 1),), SMAX)
    regrouped = lax.all_to_all(widened, "mom", split_axis=4, concat_axis=3, tiled=True)
    points = regrouped.shape[3]
    basis = dft_basis(points)
    basis_low = basis.astype(jnp.bfloat16)
    spec_real, spec_imag = coupling_spectrum(coupling, region_map, basis)
    hat_real, hat_imag = forward(regrouped, basis_low)
    sigma_real, sigma_imag = combine(
        hat_real, hat_imag, spec_real, spec_imag, occupation, shift, lesser.shape[0]
    )
    result = inverse(sigma_real, sigma_imag, basis_low)
    returned = lax.all_to_all(result, "mom", split_axis=3, concat_axis=4, tiled=True)
    return (returned[0], returned[1])


def on_device(groups, shares, lesser, greater, coupling, occupation, shift, region_map):
    energies, blocks, momenta, height, columns = lesser.shape
    devices = groups * shares
    states = energies * momenta
    whole_tiles = (
        blocks == 1
        and devices >= 4
        and devices & (devices - 1) == 0
        and height % (TILE * (devices // 2)) == 0
        and TILE % states == 0
        and columns % 128 == 0
    )
    if whole_tiles:
        return by_rows(
            lesser, greater, coupling, occupation, shift, region_map, groups, shares
        )
    return by_groups(lesser, greater, coupling, occupation, shift, region_map)


def solution(mesh):
    return jax.shard_map(
        functools.partial(on_device, mesh.shape["grp"], mesh.shape["mom"]),
        mesh=mesh,
        in_specs=(
            P("grp", None, "mom", None, None),
            P("grp", None, "mom", None, None),
            P(),
            P(),
            P(),
            P(),
        ),
        out_specs=(P("grp", None, "mom", None, None), P("grp", None, "mom", None, None)),
        check_vma=False,
    )
```

```python
import functools
import math

import jax
import jax.numpy as jnp
import numpy as np
from jax import lax
from jax.experimental import pallas as pl
from jax.experimental.pallas import tpu as pltpu
from jax.sharding import PartitionSpec as P

SMAX = 2
TILE = 16
VMEM_BYTES = 40 * 1024 * 1024
VMEM_WHOLE = 60 * 1024 * 1024
APART = 1 << 16
AXES = ("grp", "mom")


def permutation(energies, momenta, rows):
    inner = energies * momenta
    size = inner * rows
    matrix = np.zeros((size, size), np.float32)
    for state in range(inner):
        for row in range(rows):
            matrix[row * inner + state, state * rows + row] = 1.0
    return matrix


def mix_kernel(matrix_ref, in_ref, out_ref):
    devices, size, width = in_ref.shape
    for start in range(0, size, TILE):
        block = in_ref[:, start : start + TILE, :].reshape(devices * TILE, width)
        mixed = jnp.dot(matrix_ref[...], block, preferred_element_type=jnp.float32)
        out_ref[:, start : start + TILE, :] = mixed.astype(out_ref.dtype).reshape(
            devices, TILE, width
        )


def unpack_kernel(perm_ref, in_ref, lesser_ref, greater_ref, held, sent):
    pieces, rows = held.shape[1], held.shape[4]
    copies = []
    for side, ref in enumerate((lesser_ref, greater_ref)):
        for piece in range(pieces):
            moved = jnp.dot(
                perm_ref[...], in_ref[side * pieces + piece], preferred_element_type=jnp.float32
            )
            held[side, piece] = moved.astype(held.dtype).reshape(held.shape[2:])
            copy = pltpu.make_async_copy(
                held.at[side, piece],
                ref.at[:, 0, :, piece * rows : (piece + 1) * rows, :],
                sent.at[side, piece],
            )
            copy.start()
            copies.append(copy)
    for copy in copies:
        copy.wait()


def pack_kernel(
    shares, momenta, energies,
    place_ref, region_ref, shift_ref, occupation_ref, coupling_ref, down_ref, across_ref,
    perm_ref, lesser_ref, greater_ref, matrix_ref, out_ref, held, arrived, packed, sent,
):
    pieces, rows = held.shape[1], held.shape[4]
    size, width = out_ref.shape[1:]
    copies = []
    for side, ref in enumerate((lesser_ref, greater_ref)):
        for piece in range(pieces):
            copy = pltpu.make_async_copy(
                ref.at[:, 0, :, piece * rows : (piece + 1) * rows, :],
                held.at[side, piece],
                arrived.at[side, piece],
            )
            copy.start()
            copies.append(copy)
    build_kernel(
        shares, momenta, energies, pieces,
        place_ref, region_ref, shift_ref, occupation_ref, coupling_ref, down_ref, across_ref,
        matrix_ref,
    )
    for side in range(2):
        for piece in range(pieces):
            copies[side * pieces + piece].wait()
            block = held[side, piece].reshape(size, width)
            moved = jnp.dot(perm_ref[...], block, preferred_element_type=jnp.float32)
            place = side * pieces + piece
            packed[place] = moved.astype(packed.dtype)
            copies.append(pltpu.make_async_copy(packed.at[place], out_ref.at[place], sent.at[place]))
            copies[-1].start()
    for copy in copies[2 * pieces :]:
        copy.wait()


def build_kernel(
    shares, momenta, energies, pieces,
    place_ref, region_ref, shift_ref, occupation_ref, coupling_ref, down_ref, across_ref, out_ref
):
    points = shares * momenta
    modes = coupling_ref.shape[1]
    greater = lax.div(place_ref[0], jnp.int32(pieces)).astype(jnp.float32)
    chosen = coupling_ref[region_ref[0]]
    size = down_ref.shape[0]
    pick = down_ref[:, 1:2] == lax.broadcasted_iota(jnp.int32, (size, points), 1)
    pick = jnp.where(pick, 1.0, 0.0).astype(jnp.bfloat16)
    apart = down_ref[:, 0:1] - across_ref[0:1, :]
    total = jnp.zeros((size, size), jnp.float32)
    for step in range(-SMAX, SMAX + 1):
        if step == 0:
            continue
        row = jnp.zeros((1, points), jnp.float32)
        for mode in range(modes):
            filling = occupation_ref[mode] + (greater if step > 0 else 1.0 - greater)
            weight = jnp.where(shift_ref[mode] == abs(step), filling, 0.0)
            row = row + weight * chosen[mode : mode + 1, :]
        wide = jnp.broadcast_to(jnp.concatenate([row, row], axis=1), (points, 2 * points))
        turned = pltpu.roll(wide, 0, 1, stride=1, stride_axis=0)[:, :points]
        half = jnp.dot(
            pick, turned.astype(jnp.bfloat16), preferred_element_type=jnp.float32
        ).astype(jnp.bfloat16)
        full = lax.dot_general(
            pick, half, (((1,), (1,)), ((), ())), preferred_element_type=jnp.float32
        )
        total = jnp.where(apart == step, full, total)
    out_ref[...] = total.astype(out_ref.dtype)


def params():
    return pltpu.CompilerParams(vmem_limit_bytes=VMEM_BYTES)


SCALARS = pl.BlockSpec(memory_space=pltpu.SMEM)
VECTORS = pl.BlockSpec(memory_space=pltpu.VMEM)
SLABS = pl.BlockSpec(memory_space=pl.ANY)


def pack(place, lesser, greater, coupling, occupation, shift, region_map, shares, pieces, rows):
    energies, _, momenta, _, columns = lesser.shape
    devices = 2 * pieces
    size = energies * momenta * rows
    fold = TILE // (energies * momenta)
    group, share, row, energy, momentum = np.unravel_index(
        np.arange(devices * TILE), (devices // shares, shares, fold, energies, momenta)
    )
    code = np.stack([row * APART + group * energies + energy, share * momenta + momentum], axis=1)
    code = code.astype(np.int32)
    perm = jnp.asarray(permutation(energies, momenta, rows), jnp.bfloat16)
    return pl.pallas_call(
        functools.partial(pack_kernel, shares, momenta, energies),
        out_shape=(
            jax.ShapeDtypeStruct((devices * TILE, devices * TILE), jnp.bfloat16),
            jax.ShapeDtypeStruct((devices, size, columns), lesser.dtype),
        ),
        in_specs=[SCALARS] * 4 + [VECTORS] * 4 + [SLABS] * 2,
        out_specs=(VECTORS, SLABS),
        scratch_shapes=[
            pltpu.VMEM((2, pieces, energies, momenta, rows, columns), lesser.dtype),
            pltpu.SemaphoreType.DMA((2, pieces)),
            pltpu.VMEM((devices, size, columns), lesser.dtype),
            pltpu.SemaphoreType.DMA((devices,)),
        ],
        compiler_params=pltpu.CompilerParams(vmem_limit_bytes=VMEM_WHOLE),
        name="pack",
    )(
        place,
        region_map,
        shift,
        occupation,
        coupling,
        jnp.asarray(code),
        jnp.asarray(code.T),
        perm,
        lesser,
        greater,
    )


def unpack(packed, shape, pieces, rows):
    energies, _, momenta, _, columns = shape
    perm = jnp.asarray(permutation(energies, momenta, rows).T, jnp.bfloat16)
    out = jax.ShapeDtypeStruct(shape, packed.dtype)
    return pl.pallas_call(
        unpack_kernel,
        out_shape=(out, out),
        in_specs=[VECTORS, VECTORS],
        out_specs=(SLABS, SLABS),
        scratch_shapes=[
            pltpu.VMEM((2, pieces, energies, momenta, rows, columns), packed.dtype),
            pltpu.SemaphoreType.DMA((2, pieces)),
        ],
        compiler_params=params(),
        name="unpack",
    )(perm, packed)


def mix(matrix, received):
    return pl.pallas_call(
        mix_kernel,
        out_shape=jax.ShapeDtypeStruct(received.shape, received.dtype),
        in_specs=[VECTORS, VECTORS],
        out_specs=VECTORS,
        compiler_params=params(),
        name="mix",
    )(matrix, received)


def exchange(array):
    return lax.all_to_all(array, AXES, split_axis=0, concat_axis=0, tiled=True)


def by_rows(lesser, greater, coupling, occupation, shift, region_map, groups, shares):
    pieces = groups * shares // 2
    rows = lesser.shape[3] // pieces
    place = (lax.axis_index("grp") * shares + lax.axis_index("mom")).astype(jnp.int32).reshape(1)
    matrix, sent = pack(
        place, lesser, greater, coupling, occupation, shift, region_map, shares, pieces, rows
    )
    returned = exchange(mix(matrix, exchange(sent)))
    return unpack(returned, lesser.shape, pieces, rows)


def with_halo(shard, sides, width):
    for axis, dim in sides:
        size, length = (lax.axis_size(axis), shard.shape[dim])
        up = [(i, (i + 1) % size) for i in range(size - 1)]
        down = [(j, i) for i, j in up]
        last = lax.slice_in_dim(shard, length - width, length, axis=dim)
        first = lax.slice_in_dim(shard, 0, width, axis=dim)
        before = lax.ppermute(last, axis, up)
        after = lax.ppermute(first, axis, down)
        shard = jnp.concatenate([before, shard, after], axis=dim)
    return shard


def dft_basis(points):
    row_index = lax.broadcasted_iota(jnp.int32, (points, points), 0)
    col_index = lax.broadcasted_iota(jnp.int32, (points, points), 1)
    angles = (row_index * col_index % points).astype(jnp.float32) * (2.0 * math.pi / points)
    return jnp.concatenate([jnp.cos(angles), jnp.sin(angles)], axis=0)


def coupling_spectrum(coupling, region_map, basis):
    regions = coupling.shape[0]
    points = coupling.shape[2]
    onehot = (region_map[:, None] == jnp.arange(regions, dtype=jnp.int32)[None, :]).astype(
        jnp.float32
    )
    chosen = jnp.einsum("br,rmq->bmq", onehot, coupling, precision=lax.Precision.HIGHEST)
    spectrum = jnp.einsum("pq,bmq->bmp", basis, chosen, precision=lax.Precision.HIGHEST)
    return (spectrum[:, :, :points], -spectrum[:, :, points:])


def forward(stacked, basis_low):
    points = stacked.shape[3]
    columns = stacked.shape[5] // 2
    mixture = jnp.einsum(
        "pk,aebkxw->aebpxw", basis_low, stacked, preferred_element_type=jnp.float32
    )
    cosine = mixture[:, :, :, :points]
    sine = mixture[:, :, :, points:]
    return (
        cosine[..., :columns] + sine[..., columns:],
        cosine[..., columns:] - sine[..., :columns],
    )


def combine(hat_real, hat_imag, spec_real, spec_imag, occupation, shift, energies):
    out_shape = (2, energies) + hat_real.shape[2:]
    sigma_real = jnp.zeros(out_shape, jnp.float32)
    sigma_imag = jnp.zeros(out_shape, jnp.float32)
    points = spec_real.shape[2]
    for phonon in range(occupation.shape[0]):
        offset = shift[phonon]
        filling = occupation[phonon]
        lower_real = lax.dynamic_slice_in_dim(hat_real, SMAX - offset, energies, 1)
        lower_imag = lax.dynamic_slice_in_dim(hat_imag, SMAX - offset, energies, 1)
        upper_real = lax.dynamic_slice_in_dim(hat_real, SMAX + offset, energies, 1)
        upper_imag = lax.dynamic_slice_in_dim(hat_imag, SMAX + offset, energies, 1)
        weight_low = jnp.stack([filling, filling + 1.0]).reshape(2, 1, 1, 1, 1, 1)
        weight_high = jnp.stack([filling + 1.0, filling]).reshape(2, 1, 1, 1, 1, 1)
        mixed_real = weight_low * lower_real + weight_high * upper_real
        mixed_imag = weight_low * lower_imag + weight_high * upper_imag
        factor_real = spec_real[:, phonon, :].reshape(1, 1, -1, points, 1, 1)
        factor_imag = spec_imag[:, phonon, :].reshape(1, 1, -1, points, 1, 1)
        sigma_real = sigma_real + factor_real * mixed_real - factor_imag * mixed_imag
        sigma_imag = sigma_imag + factor_real * mixed_imag + factor_imag * mixed_real
    return (sigma_real, sigma_imag)


def inverse(sigma_real, sigma_imag, basis_low):
    points = sigma_real.shape[3]
    columns = sigma_real.shape[5]
    spectral = jnp.concatenate([sigma_real, sigma_imag], axis=-1).astype(jnp.bfloat16)
    mixture = jnp.einsum(
        "pk,aebkxw->aebpxw", basis_low, spectral, preferred_element_type=jnp.float32
    )
    cosine = mixture[:, :, :, :points]
    sine = mixture[:, :, :, points:]
    real_part = cosine[..., :columns] - sine[..., columns:]
    imag_part = cosine[..., columns:] + sine[..., :columns]
    return (jnp.concatenate([real_part, imag_part], axis=-1) * (1.0 / points)).astype(jnp.bfloat16)


def by_groups(lesser, greater, coupling, occupation, shift, region_map):
    stacked = jnp.stack([lesser, greater])
    widened = with_halo(stacked, (("grp", 1),), SMAX)
    regrouped = lax.all_to_all(widened, "mom", split_axis=4, concat_axis=3, tiled=True)
    points = regrouped.shape[3]
    basis = dft_basis(points)
    basis_low = basis.astype(jnp.bfloat16)
    spec_real, spec_imag = coupling_spectrum(coupling, region_map, basis)
    hat_real, hat_imag = forward(regrouped, basis_low)
    sigma_real, sigma_imag = combine(
        hat_real, hat_imag, spec_real, spec_imag, occupation, shift, lesser.shape[0]
    )
    result = inverse(sigma_real, sigma_imag, basis_low)
    returned = lax.all_to_all(result, "mom", split_axis=3, concat_axis=4, tiled=True)
    return (returned[0], returned[1])


def on_device(groups, shares, lesser, greater, coupling, occupation, shift, region_map):
    energies, blocks, momenta, height, columns = lesser.shape
    devices = groups * shares
    states = energies * momenta
    whole_tiles = (
        blocks == 1
        and devices >= 4
        and devices & (devices - 1) == 0
        and height % (TILE * (devices // 2)) == 0
        and TILE % states == 0
        and columns % 128 == 0
    )
    if whole_tiles:
        return by_rows(
            lesser, greater, coupling, occupation, shift, region_map, groups, shares
        )
    return by_groups(lesser, greater, coupling, occupation, shift, region_map)


def solution(mesh):
    return jax.shard_map(
        functools.partial(on_device, mesh.shape["grp"], mesh.shape["mom"]),
        mesh=mesh,
        in_specs=(
            P("grp", None, "mom", None, None),
            P("grp", None, "mom", None, None),
            P(),
            P(),
            P(),
            P(),
        ),
        out_specs=(P("grp", None, "mom", None, None), P("grp", None, "mom", None, None)),
        check_vma=False,
    )
```

```python
import functools
import math

import jax
import jax.numpy as jnp
import numpy as np
from jax import lax
from jax.experimental import pallas as pl
from jax.experimental.pallas import tpu as pltpu
from jax.sharding import PartitionSpec as P

SMAX = 2
TILE = 16
VMEM_BYTES = 60 * 1024 * 1024
APART = 1 << 16


def permutation(energies, momenta, rows):
    inner = energies * momenta
    size = inner * rows
    matrix = np.zeros((size, size), np.float32)
    for state in range(inner):
        for row in range(rows):
            matrix[row * inner + state, state * rows + row] = 1.0
    return matrix


def quarter(place_ref, turn, rows):
    return pl.ds(pl.multiple_of((place_ref[0] ^ turn) * rows, rows), rows)


def cut_kernel(chunk, place_ref, lesser_ref, greater_ref, *refs):
    outs, sent = refs[-4:-1], refs[-1]
    rows, width = outs[0].shape[3:]
    copies = []
    for turn, out in enumerate(outs, 1):
        for side, ref in enumerate((lesser_ref, greater_ref)):
            copies.append(
                pltpu.make_async_copy(
                    ref.at[:, 0, :, quarter(place_ref, turn, rows), pl.ds(chunk * width, width)],
                    out.at[side],
                    sent.at[turn, side],
                )
            )
            copies[-1].start()
    for copy in copies:
        copy.wait()


def join_kernel(chunk, place_ref, *refs):
    turns = len(refs[0:4])
    ins, sent = refs[:turns], refs[-1]
    outs = refs[-3:-1]
    rows, width = ins[0].shape[3:]
    copies = []
    for turn, part in enumerate(ins):
        for side, ref in enumerate(outs):
            copies.append(
                pltpu.make_async_copy(
                    part.at[side],
                    ref.at[:, 0, :, quarter(place_ref, turn, rows), pl.ds(chunk * width, width)],
                    sent.at[turn, side],
                )
            )
            copies[-1].start()
    for copy in copies:
        copy.wait()


def pack_kernel(chunk, place_ref, perm_ref, lesser_ref, greater_ref, *refs):
    others, (out_ref, held, packed, arrived, sent) = refs[:3], refs[3:]
    height, width = held.shape[4:]
    size = packed.shape[2]
    rows = TILE
    own = [
        pltpu.make_async_copy(
            ref.at[:, 0, :, quarter(place_ref, 0, height), pl.ds(chunk * width, width)],
            held.at[0, side],
            arrived.at[0, side],
        )
        for side, ref in enumerate((lesser_ref, greater_ref))
    ]
    come = [own] + [
        [pltpu.make_async_copy(part, held.at[turn], arrived.at[turn, 0])]
        for turn, part in enumerate(others, 1)
    ]
    for copies in come:
        for copy in copies:
            copy.start()
    gone = []
    for turn, copies in enumerate(come):
        for copy in copies:
            copy.wait()
        for side in range(2):
            for piece in range(height // rows):
                block = held[turn, side, :, :, piece * rows : (piece + 1) * rows, :]
                moved = jnp.dot(
                    perm_ref[...], block.reshape(size, width), preferred_element_type=jnp.float32
                )
                packed[side * (height // rows) + piece, turn] = moved.astype(packed.dtype)
        gone.append(pltpu.make_async_copy(packed.at[:, turn], out_ref.at[:, turn], sent.at[turn]))
        gone[-1].start()
    for copy in gone:
        copy.wait()


def unpack_kernel(perm_ref, in_ref, *refs):
    outs, (held, packed, arrived, sent) = refs[:4], refs[4:]
    height, width = held.shape[4:]
    rows = TILE
    order = list(range(1, len(outs))) + [0]
    come = {
        turn: pltpu.make_async_copy(in_ref.at[:, turn], packed.at[:, turn], arrived.at[turn])
        for turn in order
    }
    for turn in order:
        come[turn].start()
    gone = []
    for turn in order:
        come[turn].wait()
        for side in range(2):
            for piece in range(height // rows):
                moved = jnp.dot(
                    perm_ref[...],
                    packed[side * (height // rows) + piece, turn],
                    preferred_element_type=jnp.float32,
                )
                held[turn, side, :, :, piece * rows : (piece + 1) * rows, :] = moved.astype(
                    held.dtype
                ).reshape(held.shape[2], held.shape[3], rows, width)
        gone.append(pltpu.make_async_copy(held.at[turn], outs[turn], sent.at[turn]))
        gone[-1].start()
    for copy in gone:
        copy.wait()


def mix_kernel(matrix_ref, in_ref, out_ref):
    planes, turns, size, width = in_ref.shape
    for start in range(0, size, 4 * TILE):
        blocks = [
            in_ref[:, :, start + step : start + step + TILE, :].reshape(planes * turns * TILE, width)
            for step in range(0, 4 * TILE, TILE)
        ]
        mixed = jnp.dot(
            matrix_ref[...], jnp.concatenate(blocks, axis=1), preferred_element_type=jnp.float32
        ).astype(out_ref.dtype)
        for step in range(4):
            out_ref[:, :, start + step * TILE : start + (step + 1) * TILE, :] = mixed[
                :, step * width : (step + 1) * width
            ].reshape(planes, turns, TILE, width)


def build_kernel(
    points, place_ref, region_ref, shift_ref, occupation_ref, coupling_ref, down_ref, across_ref, out_ref
):
    modes = coupling_ref.shape[1]
    greater = place_ref[1].astype(jnp.float32)
    chosen = coupling_ref[region_ref[0]]
    size = down_ref.shape[0]
    momentum = (down_ref[:, 1:2] ^ place_ref[0]) * down_ref[:, 3:4] + down_ref[:, 2:3]
    pick = momentum == lax.broadcasted_iota(jnp.int32, (size, points), 1)
    pick = jnp.where(pick, 1.0, 0.0).astype(jnp.bfloat16)
    apart = down_ref[:, 0:1] - across_ref[0:1, :]
    total = jnp.zeros((size, size), jnp.float32)
    for step in range(-SMAX, SMAX + 1):
        if step == 0:
            continue
        row = jnp.zeros((1, points), jnp.float32)
        for mode in range(modes):
            filling = occupation_ref[mode] + (greater if step > 0 else 1.0 - greater)
            weight = jnp.where(shift_ref[mode] == abs(step), filling, 0.0)
            row = row + weight * chosen[mode : mode + 1, :]
        wide = jnp.broadcast_to(jnp.concatenate([row, row], axis=1), (points, 2 * points))
        turned = pltpu.roll(wide, 0, 1, stride=1, stride_axis=0)[:, :points]
        half = jnp.dot(
            pick, turned.astype(jnp.bfloat16), preferred_element_type=jnp.float32
        ).astype(jnp.bfloat16)
        full = lax.dot_general(
            pick, half, (((1,), (1,)), ((), ())), preferred_element_type=jnp.float32
        )
        total = jnp.where(apart == step, full, total)
    out_ref[...] = total.astype(out_ref.dtype)


def params():
    return pltpu.CompilerParams(vmem_limit_bytes=VMEM_BYTES)


SCALARS = pl.BlockSpec(memory_space=pltpu.SMEM)
VECTORS = pl.BlockSpec(memory_space=pltpu.VMEM)
ANYWHERE = pl.BlockSpec(memory_space=pl.ANY)


def build(place, coupling, occupation, shift, region_map, groups, inner, outer, energies, momenta):
    points = inner * outer * momenta
    group, share, turn, row, energy, momentum = np.unravel_index(
        np.arange(groups * inner * outer * TILE),
        (groups, inner, outer, TILE // (energies * momenta), energies, momenta),
    )
    code = np.stack(
        [
            row * APART + group * energies + energy,
            turn,
            share * momenta + momentum,
            np.full_like(turn, inner * momenta),
        ],
        axis=1,
    ).astype(np.int32)
    size = code.shape[0]
    return pl.pallas_call(
        functools.partial(build_kernel, points),
        out_shape=jax.ShapeDtypeStruct((size, size), jnp.bfloat16),
        in_specs=[SCALARS] * 4 + [VECTORS] * 3,
        out_specs=VECTORS,
        compiler_params=params(),
        name="build",
    )(
        place, region_map, shift, occupation, coupling, jnp.asarray(code), jnp.asarray(code[:, :1].T)
    )


def cut(place, lesser, greater, before, chunk, width, height):
    energies, _, momenta, _, _ = lesser.shape
    part = jax.ShapeDtypeStruct((2, energies, momenta, height, width), lesser.dtype)
    return pl.pallas_call(
        functools.partial(cut_kernel, chunk),
        out_shape=(part,) * 3,
        in_specs=[SCALARS, ANYWHERE, ANYWHERE] + [ANYWHERE] * len(before),
        out_specs=(ANYWHERE,) * 3,
        scratch_shapes=[pltpu.SemaphoreType.DMA((4, 2))],
        compiler_params=params(),
        name="cut",
    )(place, lesser, greater, *before)


def join(place, parts, filled, shape, chunk):
    out = jax.ShapeDtypeStruct(shape, parts[0].dtype)
    return pl.pallas_call(
        functools.partial(join_kernel, chunk),
        out_shape=(out, out),
        in_specs=[SCALARS] + [ANYWHERE] * (len(parts) + len(filled)),
        out_specs=(ANYWHERE, ANYWHERE),
        scratch_shapes=[pltpu.SemaphoreType.DMA((4, 2))],
        input_output_aliases={1 + len(parts) + side: side for side in range(len(filled))},
        compiler_params=params(),
        name="join",
    )(place, *parts, *filled)


def staging(energies, momenta, height, width, inner, dtype):
    size = energies * momenta * TILE
    return [
        pltpu.VMEM((4, 2, energies, momenta, height, width), dtype),
        pltpu.VMEM((2 * inner, 4, size, width), dtype),
    ]


def pack(place, lesser, greater, others, chunk, inner):
    _, energies, momenta, height, width = others[0].shape
    size = energies * momenta * TILE
    perm = jnp.asarray(permutation(energies, momenta, TILE), jnp.bfloat16)
    return pl.pallas_call(
        functools.partial(pack_kernel, chunk),
        out_shape=jax.ShapeDtypeStruct((2 * inner, 4, size, width), lesser.dtype),
        in_specs=[SCALARS, VECTORS] + [ANYWHERE] * 5,
        out_specs=ANYWHERE,
        scratch_shapes=staging(energies, momenta, height, width, inner, lesser.dtype)
        + [pltpu.SemaphoreType.DMA((4, 2)), pltpu.SemaphoreType.DMA((4,))],
        compiler_params=params(),
        name="pack",
    )(place, perm, lesser, greater, *others)


def unpack(packed, energies, momenta, height, inner):
    width = packed.shape[3]
    perm = jnp.asarray(permutation(energies, momenta, TILE).T, jnp.bfloat16)
    part = jax.ShapeDtypeStruct((2, energies, momenta, height, width), packed.dtype)
    return pl.pallas_call(
        unpack_kernel,
        out_shape=(part,) * 4,
        in_specs=[VECTORS, ANYWHERE],
        out_specs=(ANYWHERE,) * 4,
        scratch_shapes=staging(energies, momenta, height, width, inner, packed.dtype)
        + [pltpu.SemaphoreType.DMA((4,)), pltpu.SemaphoreType.DMA((4,))],
        compiler_params=params(),
        name="unpack",
    )(perm, packed)


def mix(matrix, received):
    return pl.pallas_call(
        mix_kernel,
        out_shape=jax.ShapeDtypeStruct(received.shape, received.dtype),
        in_specs=[VECTORS, VECTORS],
        out_specs=VECTORS,
        compiler_params=params(),
        name="mix",
    )(matrix, received)


def in_plane(array):
    return lax.all_to_all(array, ("grp", "inner"), split_axis=0, concat_axis=0, tiled=True)


def across(parts, outer):
    return [
        lax.ppermute(part, "outer", [(at, at ^ turn) for at in range(outer)])
        for turn, part in enumerate(parts, 1)
    ]


def by_rows(lesser, greater, coupling, occupation, shift, region_map, groups, outer, inner):
    energies, _, momenta, rows, columns = lesser.shape
    height = rows // outer
    width = 128
    chunks = columns // width
    place = jnp.stack([lax.axis_index("outer"), lax.axis_index("grp")]).astype(jnp.int32)
    matrix = build(
        place, coupling, occupation, shift, region_map, groups, inner, outer, energies, momenta
    )
    cuts, come = [], []
    for chunk in range(chunks):
        before = cuts[-1][:1] if chunk else []
        if chunk > 1:
            before = list(before) + come[chunk - 2][:1]
        cuts.append(cut(place, lesser, greater, before, chunk, width, height))
        come.append(across(cuts[-1], outer))
    filled = ()
    for chunk in range(chunks):
        received = in_plane(pack(place, lesser, greater, come[chunk], chunk, inner))
        returned = in_plane(mix(matrix, received))
        parts = unpack(returned, energies, momenta, height, inner)
        parts = [parts[0]] + across(parts[1:], outer)
        filled = join(place, parts, filled, lesser.shape, chunk)
    return filled


def with_halo(shard, sides, width):
    for axis, dim in sides:
        size, length = (lax.axis_size(axis), shard.shape[dim])
        up = [(i, (i + 1) % size) for i in range(size - 1)]
        down = [(j, i) for i, j in up]
        last = lax.slice_in_dim(shard, length - width, length, axis=dim)
        first = lax.slice_in_dim(shard, 0, width, axis=dim)
        before = lax.ppermute(last, axis, up)
        after = lax.ppermute(first, axis, down)
        shard = jnp.concatenate([before, shard, after], axis=dim)
    return shard


def dft_basis(points):
    row_index = lax.broadcasted_iota(jnp.int32, (points, points), 0)
    col_index = lax.broadcasted_iota(jnp.int32, (points, points), 1)
    angles = (row_index * col_index % points).astype(jnp.float32) * (2.0 * math.pi / points)
    return jnp.concatenate([jnp.cos(angles), jnp.sin(angles)], axis=0)


def coupling_spectrum(coupling, region_map, basis):
    regions = coupling.shape[0]
    points = coupling.shape[2]
    onehot = (region_map[:, None] == jnp.arange(regions, dtype=jnp.int32)[None, :]).astype(
        jnp.float32
    )
    chosen = jnp.einsum("br,rmq->bmq", onehot, coupling, precision=lax.Precision.HIGHEST)
    spectrum = jnp.einsum("pq,bmq->bmp", basis, chosen, precision=lax.Precision.HIGHEST)
    return (spectrum[:, :, :points], -spectrum[:, :, points:])


def forward(stacked, basis_low):
    points = stacked.shape[3]
    columns = stacked.shape[5] // 2
    mixture = jnp.einsum(
        "pk,aebkxw->aebpxw", basis_low, stacked, preferred_element_type=jnp.float32
    )
    cosine = mixture[:, :, :, :points]
    sine = mixture[:, :, :, points:]
    return (
        cosine[..., :columns] + sine[..., columns:],
        cosine[..., columns:] - sine[..., :columns],
    )


def combine(hat_real, hat_imag, spec_real, spec_imag, occupation, shift, energies):
    out_shape = (2, energies) + hat_real.shape[2:]
    sigma_real = jnp.zeros(out_shape, jnp.float32)
    sigma_imag = jnp.zeros(out_shape, jnp.float32)
    points = spec_real.shape[2]
    for phonon in range(occupation.shape[0]):
        offset = shift[phonon]
        filling = occupation[phonon]
        lower_real = lax.dynamic_slice_in_dim(hat_real, SMAX - offset, energies, 1)
        lower_imag = lax.dynamic_slice_in_dim(hat_imag, SMAX - offset, energies, 1)
        upper_real = lax.dynamic_slice_in_dim(hat_real, SMAX + offset, energies, 1)
        upper_imag = lax.dynamic_slice_in_dim(hat_imag, SMAX + offset, energies, 1)
        weight_low = jnp.stack([filling, filling + 1.0]).reshape(2, 1, 1, 1, 1, 1)
        weight_high = jnp.stack([filling + 1.0, filling]).reshape(2, 1, 1, 1, 1, 1)
        mixed_real = weight_low * lower_real + weight_high * upper_real
        mixed_imag = weight_low * lower_imag + weight_high * upper_imag
        factor_real = spec_real[:, phonon, :].reshape(1, 1, -1, points, 1, 1)
        factor_imag = spec_imag[:, phonon, :].reshape(1, 1, -1, points, 1, 1)
        sigma_real = sigma_real + factor_real * mixed_real - factor_imag * mixed_imag
        sigma_imag = sigma_imag + factor_real * mixed_imag + factor_imag * mixed_real
    return (sigma_real, sigma_imag)


def inverse(sigma_real, sigma_imag, basis_low):
    points = sigma_real.shape[3]
    columns = sigma_real.shape[5]
    spectral = jnp.concatenate([sigma_real, sigma_imag], axis=-1).astype(jnp.bfloat16)
    mixture = jnp.einsum(
        "pk,aebkxw->aebpxw", basis_low, spectral, preferred_element_type=jnp.float32
    )
    cosine = mixture[:, :, :, :points]
    sine = mixture[:, :, :, points:]
    real_part = cosine[..., :columns] - sine[..., columns:]
    imag_part = cosine[..., columns:] + sine[..., :columns]
    return (jnp.concatenate([real_part, imag_part], axis=-1) * (1.0 / points)).astype(jnp.bfloat16)


def by_groups(lesser, greater, coupling, occupation, shift, region_map, momentum):
    stacked = jnp.stack([lesser, greater])
    widened = with_halo(stacked, (("grp", 1),), SMAX)
    regrouped = lax.all_to_all(widened, momentum, split_axis=4, concat_axis=3, tiled=True)
    points = regrouped.shape[3]
    basis = dft_basis(points)
    basis_low = basis.astype(jnp.bfloat16)
    spec_real, spec_imag = coupling_spectrum(coupling, region_map, basis)
    hat_real, hat_imag = forward(regrouped, basis_low)
    sigma_real, sigma_imag = combine(
        hat_real, hat_imag, spec_real, spec_imag, occupation, shift, lesser.shape[0]
    )
    result = inverse(sigma_real, sigma_imag, basis_low)
    returned = lax.all_to_all(result, momentum, split_axis=3, concat_axis=4, tiled=True)
    return (returned[0], returned[1])


def whole_tiles(shape, groups, outer, inner):
    energies, blocks, momenta, rows, columns = shape
    return (
        groups == 2
        and outer == 4
        and blocks == 1
        and rows == TILE * outer * inner
        and TILE % (energies * momenta) == 0
        and columns % 128 == 0
    )


def solution(mesh):
    groups, shares = mesh.shape["grp"], mesh.shape["mom"]
    outer, inner = 4, shares // 4
    split = jax.sharding.Mesh(
        mesh.devices.reshape(groups, outer, inner), ("grp", "outer", "inner")
    )
    momentum = ("outer", "inner")

    def on_device(lesser, *rest):
        if whole_tiles(lesser.shape, groups, outer, inner):
            return by_rows(lesser, *rest, groups, outer, inner)
        return by_groups(lesser, *rest, momentum)

    slab = P("grp", None, momentum, None, None)
    return jax.shard_map(
        on_device,
        mesh=split,
        in_specs=(slab, slab, P(), P(), P(), P()),
        out_specs=(slab, slab),
        check_vma=False,
    )
```

```python
import functools
import math

import jax
import jax.numpy as jnp
import numpy as np
from jax import lax
from jax.experimental import pallas as pl
from jax.experimental.pallas import tpu as pltpu
from jax.sharding import PartitionSpec as P

SMAX = 2
TILE = 16
VMEM_BYTES = 40 * 1024 * 1024
VMEM_WHOLE = 60 * 1024 * 1024
APART = 1 << 16
AXES = ("grp", "mom")


def permutation(energies, momenta, rows):
    inner = energies * momenta
    size = inner * rows
    matrix = np.zeros((size, size), np.float32)
    for state in range(inner):
        for row in range(rows):
            matrix[row * inner + state, state * rows + row] = 1.0
    return matrix


def pack_kernel(pieces, order, place_ref, perm_ref, lesser_ref, greater_ref, *refs):
    outs, (held, packed, arrived, sent) = refs[:-4], refs[-4:]
    rows = held.shape[4]
    size, width = outs[0].shape
    side, block = lax.div(place_ref[0], jnp.int32(pieces)), lax.rem(place_ref[0], jnp.int32(pieces))
    come = {}
    for step in order:
        start = pl.multiple_of((block ^ step) * rows, rows)
        for which, ref in enumerate((lesser_ref, greater_ref)):
            come[step, which] = pltpu.make_async_copy(
                ref.at[:, 0, :, pl.ds(start, rows), :],
                held.at[step, which],
                arrived.at[step, which],
            )
            come[step, which].start()
    gone = []
    for step in order:
        moved = []
        for which in range(2):
            come[step, which].wait()
            moved.append(
                jnp.dot(
                    perm_ref[...],
                    held[step, which].reshape(size, width),
                    preferred_element_type=jnp.float32,
                )
            )
        packed[step, 0] = jnp.where(side == 0, moved[0], moved[1]).astype(packed.dtype)
        packed[step, 1] = jnp.where(side == 0, moved[1], moved[0]).astype(packed.dtype)
        for turn in range(2):
            gone.append(
                pltpu.make_async_copy(
                    packed.at[step, turn], outs[turn * pieces + step], sent.at[step, turn]
                )
            )
            gone[-1].start()
    for copy in gone:
        copy.wait()


def unpack_kernel(pieces, order, place_ref, perm_ref, *refs):
    ins, (lesser_ref, greater_ref, held, sent) = refs[:-4], refs[-4:]
    rows = held.shape[4]
    side, block = lax.div(place_ref[0], jnp.int32(pieces)), lax.rem(place_ref[0], jnp.int32(pieces))
    gone = []
    for at, step in enumerate(order):
        own = jnp.dot(perm_ref[...], ins[2 * at][...], preferred_element_type=jnp.float32)
        other = jnp.dot(perm_ref[...], ins[2 * at + 1][...], preferred_element_type=jnp.float32)
        start = pl.multiple_of((block ^ step) * rows, rows)
        for which, ref in enumerate((lesser_ref, greater_ref)):
            moved = jnp.where(side == which, own, other).astype(held.dtype)
            held[step, which] = moved.reshape(held.shape[2:])
            gone.append(
                pltpu.make_async_copy(
                    held.at[step, which],
                    ref.at[:, 0, :, pl.ds(start, rows), :],
                    sent.at[step, which],
                )
            )
            gone[-1].start()
    for copy in gone:
        copy.wait()


def mix_kernel(count, matrix_ref, *refs):
    ins, outs = refs[:count], refs[count:]
    size, width = ins[0].shape
    for start in range(0, size, TILE):
        block = jnp.concatenate([ref[start : start + TILE, :] for ref in ins], axis=0)
        mixed = jnp.dot(matrix_ref[...], block, preferred_element_type=jnp.float32)
        mixed = mixed.astype(outs[0].dtype)
        for slot, ref in enumerate(outs):
            ref[start : start + TILE, :] = mixed[slot * TILE : (slot + 1) * TILE, :]


def build_kernel(
    shares, momenta, energies, pieces,
    place_ref, region_ref, shift_ref, occupation_ref, coupling_ref, down_ref, across_ref, out_ref
):
    points = shares * momenta
    modes = coupling_ref.shape[1]
    place = place_ref[0]
    greater = lax.div(place, jnp.int32(pieces)).astype(jnp.float32)
    chosen = coupling_ref[region_ref[0]]
    bits = shares.bit_length() - 1

    def code_of(slot, own):
        return own + ((slot ^ place) >> bits) * energies

    size = down_ref.shape[0]
    momentum = ((down_ref[:, 0:1] ^ place) & (shares - 1)) * momenta + down_ref[:, 2:3]
    pick = momentum == lax.broadcasted_iota(jnp.int32, (size, points), 1)
    pick = jnp.where(pick, 1.0, 0.0).astype(jnp.bfloat16)
    down = code_of(down_ref[:, 0:1], down_ref[:, 1:2])
    across = code_of(across_ref[0:1, :], across_ref[1:2, :])
    apart = down - across
    total = jnp.zeros((size, size), jnp.float32)
    for step in range(-SMAX, SMAX + 1):
        if step == 0:
            continue
        row = jnp.zeros((1, points), jnp.float32)
        for mode in range(modes):
            filling = occupation_ref[mode] + (greater if step > 0 else 1.0 - greater)
            weight = jnp.where(shift_ref[mode] == abs(step), filling, 0.0)
            row = row + weight * chosen[mode : mode + 1, :]
        wide = jnp.broadcast_to(jnp.concatenate([row, row], axis=1), (points, 2 * points))
        turned = pltpu.roll(wide, 0, 1, stride=1, stride_axis=0)[:, :points]
        half = jnp.dot(
            pick, turned.astype(jnp.bfloat16), preferred_element_type=jnp.float32
        ).astype(jnp.bfloat16)
        full = lax.dot_general(
            pick, half, (((1,), (1,)), ((), ())), preferred_element_type=jnp.float32
        )
        total = jnp.where(apart == step, full, total)
    out_ref[...] = total.astype(out_ref.dtype)


def params(size=VMEM_BYTES):
    return pltpu.CompilerParams(vmem_limit_bytes=size)


SCALARS = pl.BlockSpec(memory_space=pltpu.SMEM)
VECTORS = pl.BlockSpec(memory_space=pltpu.VMEM)
ANYWHERE = pl.BlockSpec(memory_space=pl.ANY)


def build(place, coupling, occupation, shift, region_map, slots, shares, energies, momenta, pieces):
    fold = TILE // (energies * momenta)
    slot, row, energy, momentum = np.meshgrid(
        np.asarray(slots), np.arange(fold), np.arange(energies), np.arange(momenta), indexing="ij"
    )
    static = [slot.ravel(), (row * APART + energy).ravel(), momentum.ravel()]
    down = np.stack(static, axis=1).astype(np.int32)
    size = down.shape[0]
    return pl.pallas_call(
        functools.partial(build_kernel, shares, momenta, energies, pieces),
        out_shape=jax.ShapeDtypeStruct((size, size), jnp.bfloat16),
        in_specs=[SCALARS] * 4 + [VECTORS] * 3,
        out_specs=VECTORS,
        compiler_params=params(),
        name="build",
    )(
        place,
        region_map,
        shift,
        occupation,
        coupling,
        jnp.asarray(down),
        jnp.asarray(down.T),
    )


def pack(place, lesser, greater, pieces, rows, order):
    energies, _, momenta, _, columns = lesser.shape
    size = energies * momenta * rows
    perm = jnp.asarray(permutation(energies, momenta, rows), jnp.bfloat16)
    piece = jax.ShapeDtypeStruct((size, columns), lesser.dtype)
    return pl.pallas_call(
        functools.partial(pack_kernel, pieces, order),
        out_shape=(piece,) * (2 * pieces),
        in_specs=[SCALARS, VECTORS, ANYWHERE, ANYWHERE],
        out_specs=(ANYWHERE,) * (2 * pieces),
        scratch_shapes=[
            pltpu.VMEM((pieces, 2, energies, momenta, rows, columns), lesser.dtype),
            pltpu.VMEM((pieces, 2, size, columns), lesser.dtype),
            pltpu.SemaphoreType.DMA((pieces, 2)),
            pltpu.SemaphoreType.DMA((pieces, 2)),
        ],
        compiler_params=params(VMEM_WHOLE),
        name="pack",
    )(place, perm, lesser, greater)


def unpack(place, parts, shape, pieces, rows, order):
    energies, _, momenta, _, columns = shape
    perm = jnp.asarray(permutation(energies, momenta, rows).T, jnp.bfloat16)
    out = jax.ShapeDtypeStruct(shape, parts[0].dtype)
    return pl.pallas_call(
        functools.partial(unpack_kernel, pieces, order),
        out_shape=(out, out),
        in_specs=[SCALARS, VECTORS] + [VECTORS] * len(parts),
        out_specs=(ANYWHERE, ANYWHERE),
        scratch_shapes=[
            pltpu.VMEM((pieces, 2, energies, momenta, rows, columns), parts[0].dtype),
            pltpu.SemaphoreType.DMA((pieces, 2)),
        ],
        compiler_params=params(),
        name="unpack",
    )(place, perm, *parts)


def mix(matrix, parts):
    piece = jax.ShapeDtypeStruct(parts[0].shape, parts[0].dtype)
    return pl.pallas_call(
        functools.partial(mix_kernel, len(parts)),
        out_shape=(piece,) * len(parts),
        in_specs=[VECTORS] * (1 + len(parts)),
        out_specs=(VECTORS,) * len(parts),
        compiler_params=params(),
        name="mix",
    )(matrix, *parts)


def exchange(parts, slots, devices):
    return [
        part
        if slot == 0
        else lax.ppermute(part, AXES, [(device, device ^ slot) for device in range(devices)])
        for part, slot in zip(parts, slots)
    ]


def by_rows(lesser, greater, coupling, occupation, shift, region_map, groups, shares):
    energies, _, momenta, height, _ = lesser.shape
    devices = groups * shares
    pieces = devices // 2
    half = pieces // 2
    rows = height // pieces
    order = [step + far for step in range(half) for far in (half, 0)]
    slots = [step + side for step in order for side in (0, pieces)]
    place = (lax.axis_index("grp") * shares + lax.axis_index("mom")).astype(jnp.int32).reshape(1)
    sent = pack(place, lesser, greater, pieces, rows, order)
    received = exchange([sent[slot] for slot in slots], slots, devices)
    matrix = build(
        place, coupling, occupation, shift, region_map, slots, shares, energies, momenta, pieces
    )
    returned = exchange(mix(matrix, received), slots, devices)
    return unpack(place, returned, lesser.shape, pieces, rows, order)


def with_halo(shard, sides, width):
    for axis, dim in sides:
        size, length = (lax.axis_size(axis), shard.shape[dim])
        up = [(i, (i + 1) % size) for i in range(size - 1)]
        down = [(j, i) for i, j in up]
        last = lax.slice_in_dim(shard, length - width, length, axis=dim)
        first = lax.slice_in_dim(shard, 0, width, axis=dim)
        before = lax.ppermute(last, axis, up)
        after = lax.ppermute(first, axis, down)
        shard = jnp.concatenate([before, shard, after], axis=dim)
    return shard


def dft_basis(points):
    row_index = lax.broadcasted_iota(jnp.int32, (points, points), 0)
    col_index = lax.broadcasted_iota(jnp.int32, (points, points), 1)
    angles = (row_index * col_index % points).astype(jnp.float32) * (2.0 * math.pi / points)
    return jnp.concatenate([jnp.cos(angles), jnp.sin(angles)], axis=0)


def coupling_spectrum(coupling, region_map, basis):
    regions = coupling.shape[0]
    points = coupling.shape[2]
    onehot = (region_map[:, None] == jnp.arange(regions, dtype=jnp.int32)[None, :]).astype(
        jnp.float32
    )
    chosen = jnp.einsum("br,rmq->bmq", onehot, coupling, precision=lax.Precision.HIGHEST)
    spectrum = jnp.einsum("pq,bmq->bmp", basis, chosen, precision=lax.Precision.HIGHEST)
    return (spectrum[:, :, :points], -spectrum[:, :, points:])


def forward(stacked, basis_low):
    points = stacked.shape[3]
    columns = stacked.shape[5] // 2
    mixture = jnp.einsum(
        "pk,aebkxw->aebpxw", basis_low, stacked, preferred_element_type=jnp.float32
    )
    cosine = mixture[:, :, :, :points]
    sine = mixture[:, :, :, points:]
    return (
        cosine[..., :columns] + sine[..., columns:],
        cosine[..., columns:] - sine[..., :columns],
    )


def combine(hat_real, hat_imag, spec_real, spec_imag, occupation, shift, energies):
    out_shape = (2, energies) + hat_real.shape[2:]
    sigma_real = jnp.zeros(out_shape, jnp.float32)
    sigma_imag = jnp.zeros(out_shape, jnp.float32)
    points = spec_real.shape[2]
    for phonon in range(occupation.shape[0]):
        offset = shift[phonon]
        filling = occupation[phonon]
        lower_real = lax.dynamic_slice_in_dim(hat_real, SMAX - offset, energies, 1)
        lower_imag = lax.dynamic_slice_in_dim(hat_imag, SMAX - offset, energies, 1)
        upper_real = lax.dynamic_slice_in_dim(hat_real, SMAX + offset, energies, 1)
        upper_imag = lax.dynamic_slice_in_dim(hat_imag, SMAX + offset, energies, 1)
        weight_low = jnp.stack([filling, filling + 1.0]).reshape(2, 1, 1, 1, 1, 1)
        weight_high = jnp.stack([filling + 1.0, filling]).reshape(2, 1, 1, 1, 1, 1)
        mixed_real = weight_low * lower_real + weight_high * upper_real
        mixed_imag = weight_low * lower_imag + weight_high * upper_imag
        factor_real = spec_real[:, phonon, :].reshape(1, 1, -1, points, 1, 1)
        factor_imag = spec_imag[:, phonon, :].reshape(1, 1, -1, points, 1, 1)
        sigma_real = sigma_real + factor_real * mixed_real - factor_imag * mixed_imag
        sigma_imag = sigma_imag + factor_real * mixed_imag + factor_imag * mixed_real
    return (sigma_real, sigma_imag)


def inverse(sigma_real, sigma_imag, basis_low):
    points = sigma_real.shape[3]
    columns = sigma_real.shape[5]
    spectral = jnp.concatenate([sigma_real, sigma_imag], axis=-1).astype(jnp.bfloat16)
    mixture = jnp.einsum(
        "pk,aebkxw->aebpxw", basis_low, spectral, preferred_element_type=jnp.float32
    )
    cosine = mixture[:, :, :, :points]
    sine = mixture[:, :, :, points:]
    real_part = cosine[..., :columns] - sine[..., columns:]
    imag_part = cosine[..., columns:] + sine[..., :columns]
    return (jnp.concatenate([real_part, imag_part], axis=-1) * (1.0 / points)).astype(jnp.bfloat16)


def by_groups(lesser, greater, coupling, occupation, shift, region_map):
    stacked = jnp.stack([lesser, greater])
    widened = with_halo(stacked, (("grp", 1),), SMAX)
    regrouped = lax.all_to_all(widened, "mom", split_axis=4, concat_axis=3, tiled=True)
    points = regrouped.shape[3]
    basis = dft_basis(points)
    basis_low = basis.astype(jnp.bfloat16)
    spec_real, spec_imag = coupling_spectrum(coupling, region_map, basis)
    hat_real, hat_imag = forward(regrouped, basis_low)
    sigma_real, sigma_imag = combine(
        hat_real, hat_imag, spec_real, spec_imag, occupation, shift, lesser.shape[0]
    )
    result = inverse(sigma_real, sigma_imag, basis_low)
    returned = lax.all_to_all(result, "mom", split_axis=3, concat_axis=4, tiled=True)
    return (returned[0], returned[1])


def on_device(groups, shares, lesser, greater, coupling, occupation, shift, region_map):
    energies, blocks, momenta, height, columns = lesser.shape
    devices = groups * shares
    states = energies * momenta
    whole_tiles = (
        blocks == 1
        and devices >= 4
        and devices & (devices - 1) == 0
        and height % (TILE * (devices // 2)) == 0
        and TILE % states == 0
        and columns % 128 == 0
    )
    if whole_tiles:
        return by_rows(
            lesser, greater, coupling, occupation, shift, region_map, groups, shares
        )
    return by_groups(lesser, greater, coupling, occupation, shift, region_map)


def solution(mesh):
    return jax.shard_map(
        functools.partial(on_device, mesh.shape["grp"], mesh.shape["mom"]),
        mesh=mesh,
        in_specs=(
            P("grp", None, "mom", None, None),
            P("grp", None, "mom", None, None),
            P(),
            P(),
            P(),
            P(),
        ),
        out_specs=(P("grp", None, "mom", None, None), P("grp", None, "mom", None, None)),
        check_vma=False,
    )
```

```python
import functools
import math

import jax
import jax.numpy as jnp
import numpy as np
from jax import lax
from jax.experimental import pallas as pl
from jax.experimental.pallas import tpu as pltpu
from jax.sharding import PartitionSpec as P

SMAX = 2
TILE = 16
VMEM_BYTES = 40 * 1024 * 1024
VMEM_WHOLE = 60 * 1024 * 1024
APART = 1 << 16
AXES = ("grp", "side", "near")
AHEAD = 4


def permutation(energies, momenta, rows):
    inner = energies * momenta
    size = inner * rows
    matrix = np.zeros((size, size), np.float32)
    for state in range(inner):
        for row in range(rows):
            matrix[row * inner + state, state * rows + row] = 1.0
    return matrix


def place_of(place_ref, pieces, far):
    half = pieces // 2
    block = lax.rem(place_ref[0], jnp.int32(pieces))
    low = lax.rem(block, jnp.int32(half))
    high = lax.div(block, jnp.int32(half))
    return lax.div(place_ref[0], jnp.int32(pieces)), low, (1 - high if far else high) * half


def pack_kernel(pieces, far, place_ref, perm_ref, lesser_ref, greater_ref, *refs):
    half = pieces // 2
    outs, (held, arrived) = refs[:-2], refs[-2:]
    rows = held.shape[4]
    size, width = outs[0].shape[-2:]
    side, low, base = place_of(place_ref, pieces, far)
    come = []
    for step in range(half):
        start = pl.multiple_of((base + ((low ^ step) if far else step)) * rows, rows)
        come.append(
            [
                pltpu.make_async_copy(
                    ref.at[:, 0, :, pl.ds(start, rows), :],
                    held.at[step, which],
                    arrived.at[step, which],
                )
                for which, ref in enumerate((lesser_ref, greater_ref))
            ]
        )
    for copies in come[:AHEAD]:
        for copy in copies:
            copy.start()
    for step in range(half):
        moved = []
        for which in range(2):
            come[step][which].wait()
            if step + AHEAD < half:
                come[step + AHEAD][which].start()
            block = held[step, which].reshape(size, width)
            moved.append(jnp.dot(perm_ref[...], block, preferred_element_type=jnp.float32))
        if far:
            moved = [jnp.where(side == 0, *moved), jnp.where(side == 0, *moved[::-1])]
        for which in range(2):
            piece = moved[which].astype(held.dtype)
            if far:
                outs[2 * step + which][...] = piece
            else:
                outs[0][which * half + step] = piece


def unpack_kernel(pieces, far, place_ref, perm_ref, *refs):
    half = pieces // 2
    ins, (lesser_ref, greater_ref, held, sent) = refs[: 2 * half if far else 1], refs[-4:]
    rows = held.shape[4]
    side, low, base = place_of(place_ref, pieces, far)
    gone = []
    for step in range(half):
        pair = [ins[2 * step + at] if far else ins[0].at[at * half + step] for at in range(2)]
        moved = [
            jnp.dot(perm_ref[...], part[...], preferred_element_type=jnp.float32) for part in pair
        ]
        if far:
            moved = [jnp.where(side == 0, *moved), jnp.where(side == 0, *moved[::-1])]
        start = pl.multiple_of((base + ((low ^ step) if far else step)) * rows, rows)
        for which, ref in enumerate((lesser_ref, greater_ref)):
            held[step, which] = moved[which].astype(held.dtype).reshape(held.shape[2:])
            gone.append(
                pltpu.make_async_copy(
                    held.at[step, which],
                    ref.at[:, 0, :, pl.ds(start, rows), :],
                    sent.at[step, which],
                )
            )
            gone[-1].start()
    for copy in gone:
        copy.wait()


def mix_kernel(count, matrix_ref, near_ref, *refs):
    fars, near_out_ref, far_outs = refs[:count], refs[count], refs[count + 1 :]
    size, width = fars[0].shape
    near = near_ref.shape[0]
    for start in range(0, size, TILE):
        rows = slice(start, start + TILE)
        block = jnp.concatenate(
            [near_ref[:, rows, :].reshape(near * TILE, width)] + [ref[rows, :] for ref in fars], axis=0
        )
        mixed = jnp.dot(matrix_ref[...], block, preferred_element_type=jnp.float32)
        mixed = mixed.astype(near_out_ref.dtype)
        near_out_ref[:, rows, :] = mixed[: near * TILE].reshape(near, TILE, width)
        for slot, ref in enumerate(far_outs, near):
            ref[rows, :] = mixed[slot * TILE : (slot + 1) * TILE, :]


def build_kernel(
    shares, momenta, energies, pieces,
    place_ref, region_ref, shift_ref, occupation_ref, coupling_ref, down_ref, across_ref, out_ref
):
    points = shares * momenta
    modes = coupling_ref.shape[1]
    place = place_ref[0]
    greater = lax.div(place, jnp.int32(pieces)).astype(jnp.float32)
    chosen = coupling_ref[region_ref[0]]
    bits = shares.bit_length() - 1

    def device_of(slot, seen):
        return slot ^ (place & seen)

    size = down_ref.shape[0]
    device = device_of(down_ref[:, 0:1], down_ref[:, 3:4])
    momentum = (device & (shares - 1)) * momenta + down_ref[:, 2:3]
    pick = momentum == lax.broadcasted_iota(jnp.int32, (size, points), 1)
    pick = jnp.where(pick, 1.0, 0.0).astype(jnp.bfloat16)
    down = (device >> bits) * energies + down_ref[:, 1:2]
    device = device_of(across_ref[0:1, :], across_ref[3:4, :])
    apart = down - ((device >> bits) * energies + across_ref[1:2, :])
    total = jnp.zeros((size, size), jnp.float32)
    for step in range(-SMAX, SMAX + 1):
        if step == 0:
            continue
        row = jnp.zeros((1, points), jnp.float32)
        for mode in range(modes):
            filling = occupation_ref[mode] + (greater if step > 0 else 1.0 - greater)
            weight = jnp.where(shift_ref[mode] == abs(step), filling, 0.0)
            row = row + weight * chosen[mode : mode + 1, :]
        wide = jnp.broadcast_to(jnp.concatenate([row, row], axis=1), (points, 2 * points))
        turned = pltpu.roll(wide, 0, 1, stride=1, stride_axis=0)[:, :points]
        half = jnp.dot(
            pick, turned.astype(jnp.bfloat16), preferred_element_type=jnp.float32
        ).astype(jnp.bfloat16)
        full = lax.dot_general(
            pick, half, (((1,), (1,)), ((), ())), preferred_element_type=jnp.float32
        )
        total = jnp.where(apart == step, full, total)
    out_ref[...] = total.astype(out_ref.dtype)


def params(size=VMEM_BYTES):
    return pltpu.CompilerParams(vmem_limit_bytes=size)


SCALARS = pl.BlockSpec(memory_space=pltpu.SMEM)
VECTORS = pl.BlockSpec(memory_space=pltpu.VMEM)
ANYWHERE = pl.BlockSpec(memory_space=pl.ANY)


def build(place, coupling, occupation, shift, region_map, slots, shares, energies, momenta, pieces):
    fold = TILE // (energies * momenta)
    at, row, energy, momentum = np.meshgrid(
        np.arange(len(slots)), np.arange(fold), np.arange(energies), np.arange(momenta), indexing="ij"
    )
    slot, seen = np.asarray(slots).T
    static = [slot[at.ravel()], (row * APART + energy).ravel(), momentum.ravel(), seen[at.ravel()]]
    down = np.stack(static, axis=1).astype(np.int32)
    size = down.shape[0]
    return pl.pallas_call(
        functools.partial(build_kernel, shares, momenta, energies, pieces),
        out_shape=jax.ShapeDtypeStruct((size, size), jnp.bfloat16),
        in_specs=[SCALARS] * 4 + [VECTORS] * 3,
        out_specs=VECTORS,
        compiler_params=params(),
        name="build",
    )(
        place,
        region_map,
        shift,
        occupation,
        coupling,
        jnp.asarray(down),
        jnp.asarray(down.T),
    )


def pack(place, lesser, greater, pieces, rows, far):
    energies, _, momenta, _, columns = lesser.shape
    size = energies * momenta * rows
    perm = jnp.asarray(permutation(energies, momenta, rows), jnp.bfloat16)
    if far:
        out = (jax.ShapeDtypeStruct((size, columns), lesser.dtype),) * pieces
    else:
        out = (jax.ShapeDtypeStruct((pieces, size, columns), lesser.dtype),)
    return pl.pallas_call(
        functools.partial(pack_kernel, pieces, far),
        out_shape=out,
        in_specs=[SCALARS, VECTORS, ANYWHERE, ANYWHERE],
        out_specs=(VECTORS,) * len(out),
        scratch_shapes=[
            pltpu.VMEM((pieces // 2, 2, energies, momenta, rows, columns), lesser.dtype),
            pltpu.SemaphoreType.DMA((pieces // 2, 2)),
        ],
        compiler_params=params(VMEM_WHOLE),
        name="pack_far" if far else "pack_near",
    )(place, perm, lesser, greater)


def unpack(place, parts, filled, shape, pieces, rows, far):
    energies, _, momenta, _, columns = shape
    perm = jnp.asarray(permutation(energies, momenta, rows).T, jnp.bfloat16)
    out = jax.ShapeDtypeStruct(shape, parts[0].dtype)
    return pl.pallas_call(
        functools.partial(unpack_kernel, pieces, far),
        out_shape=(out, out),
        in_specs=[SCALARS, VECTORS] + [VECTORS] * len(parts) + [ANYWHERE] * len(filled),
        out_specs=(ANYWHERE, ANYWHERE),
        scratch_shapes=[
            pltpu.VMEM((pieces // 2, 2, energies, momenta, rows, columns), parts[0].dtype),
            pltpu.SemaphoreType.DMA((pieces // 2, 2)),
        ],
        input_output_aliases={2 + len(parts) + side: side for side in range(len(filled))},
        compiler_params=params(),
        name="unpack_far" if far else "unpack_near",
    )(place, perm, *parts, *filled)


def mix(matrix, near, fars):
    piece = jax.ShapeDtypeStruct(fars[0].shape, near.dtype)
    out = (jax.ShapeDtypeStruct(near.shape, near.dtype),) + (piece,) * len(fars)
    return pl.pallas_call(
        functools.partial(mix_kernel, len(fars)),
        out_shape=out,
        in_specs=[VECTORS] * (2 + len(fars)),
        out_specs=(VECTORS,) * len(out),
        compiler_params=params(),
        name="mix",
    )(matrix, near, *fars)


def by_rows(lesser, greater, coupling, occupation, shift, region_map, groups, shares):
    energies, _, momenta, height, _ = lesser.shape
    devices = groups * shares
    pieces = devices // 2
    half = pieces // 2
    rows = height // pieces
    far_slots = [half + step + side for step in range(half) for side in (0, pieces)]
    near_slots = [step + side for side in (0, pieces) for step in range(half)]
    slots = [(slot, half) for slot in near_slots] + [(slot, devices - 1) for slot in far_slots]

    def far_exchange(parts):
        return [
            lax.ppermute(part, AXES, [(device, device ^ slot) for device in range(devices)])
            for part, slot in zip(parts, far_slots)
        ]

    def near_exchange(part):
        return lax.all_to_all(part, ("grp", "near"), split_axis=0, concat_axis=0, tiled=True)

    place = (lax.axis_index(AXES)).astype(jnp.int32).reshape(1)
    far = far_exchange(pack(place, lesser, greater, pieces, rows, True))
    near = near_exchange(pack(place, lesser, greater, pieces, rows, False)[0])
    matrix = build(
        place, coupling, occupation, shift, region_map, slots, shares, energies, momenta, pieces
    )
    near, *far = mix(matrix, near, far)
    near, far = near_exchange(near), far_exchange(far)
    filled = unpack(place, [near], (), lesser.shape, pieces, rows, False)
    return unpack(place, far, filled, lesser.shape, pieces, rows, True)


def with_halo(shard, sides, width):
    for axis, dim in sides:
        size, length = (lax.axis_size(axis), shard.shape[dim])
        up = [(i, (i + 1) % size) for i in range(size - 1)]
        down = [(j, i) for i, j in up]
        last = lax.slice_in_dim(shard, length - width, length, axis=dim)
        first = lax.slice_in_dim(shard, 0, width, axis=dim)
        before = lax.ppermute(last, axis, up)
        after = lax.ppermute(first, axis, down)
        shard = jnp.concatenate([before, shard, after], axis=dim)
    return shard


def dft_basis(points):
    row_index = lax.broadcasted_iota(jnp.int32, (points, points), 0)
    col_index = lax.broadcasted_iota(jnp.int32, (points, points), 1)
    angles = (row_index * col_index % points).astype(jnp.float32) * (2.0 * math.pi / points)
    return jnp.concatenate([jnp.cos(angles), jnp.sin(angles)], axis=0)


def coupling_spectrum(coupling, region_map, basis):
    regions = coupling.shape[0]
    points = coupling.shape[2]
    onehot = (region_map[:, None] == jnp.arange(regions, dtype=jnp.int32)[None, :]).astype(
        jnp.float32
    )
    chosen = jnp.einsum("br,rmq->bmq", onehot, coupling, precision=lax.Precision.HIGHEST)
    spectrum = jnp.einsum("pq,bmq->bmp", basis, chosen, precision=lax.Precision.HIGHEST)
    return (spectrum[:, :, :points], -spectrum[:, :, points:])


def forward(stacked, basis_low):
    points = stacked.shape[3]
    columns = stacked.shape[5] // 2
    mixture = jnp.einsum(
        "pk,aebkxw->aebpxw", basis_low, stacked, preferred_element_type=jnp.float32
    )
    cosine = mixture[:, :, :, :points]
    sine = mixture[:, :, :, points:]
    return (
        cosine[..., :columns] + sine[..., columns:],
        cosine[..., columns:] - sine[..., :columns],
    )


def combine(hat_real, hat_imag, spec_real, spec_imag, occupation, shift, energies):
    out_shape = (2, energies) + hat_real.shape[2:]
    sigma_real = jnp.zeros(out_shape, jnp.float32)
    sigma_imag = jnp.zeros(out_shape, jnp.float32)
    points = spec_real.shape[2]
    for phonon in range(occupation.shape[0]):
        offset = shift[phonon]
        filling = occupation[phonon]
        lower_real = lax.dynamic_slice_in_dim(hat_real, SMAX - offset, energies, 1)
        lower_imag = lax.dynamic_slice_in_dim(hat_imag, SMAX - offset, energies, 1)
        upper_real = lax.dynamic_slice_in_dim(hat_real, SMAX + offset, energies, 1)
        upper_imag = lax.dynamic_slice_in_dim(hat_imag, SMAX + offset, energies, 1)
        weight_low = jnp.stack([filling, filling + 1.0]).reshape(2, 1, 1, 1, 1, 1)
        weight_high = jnp.stack([filling + 1.0, filling]).reshape(2, 1, 1, 1, 1, 1)
        mixed_real = weight_low * lower_real + weight_high * upper_real
        mixed_imag = weight_low * lower_imag + weight_high * upper_imag
        factor_real = spec_real[:, phonon, :].reshape(1, 1, -1, points, 1, 1)
        factor_imag = spec_imag[:, phonon, :].reshape(1, 1, -1, points, 1, 1)
        sigma_real = sigma_real + factor_real * mixed_real - factor_imag * mixed_imag
        sigma_imag = sigma_imag + factor_real * mixed_imag + factor_imag * mixed_real
    return (sigma_real, sigma_imag)


def inverse(sigma_real, sigma_imag, basis_low):
    points = sigma_real.shape[3]
    columns = sigma_real.shape[5]
    spectral = jnp.concatenate([sigma_real, sigma_imag], axis=-1).astype(jnp.bfloat16)
    mixture = jnp.einsum(
        "pk,aebkxw->aebpxw", basis_low, spectral, preferred_element_type=jnp.float32
    )
    cosine = mixture[:, :, :, :points]
    sine = mixture[:, :, :, points:]
    real_part = cosine[..., :columns] - sine[..., columns:]
    imag_part = cosine[..., columns:] + sine[..., :columns]
    return (jnp.concatenate([real_part, imag_part], axis=-1) * (1.0 / points)).astype(jnp.bfloat16)


def by_groups(lesser, greater, coupling, occupation, shift, region_map, momentum):
    stacked = jnp.stack([lesser, greater])
    widened = with_halo(stacked, (("grp", 1),), SMAX)
    regrouped = lax.all_to_all(widened, momentum, split_axis=4, concat_axis=3, tiled=True)
    points = regrouped.shape[3]
    basis = dft_basis(points)
    basis_low = basis.astype(jnp.bfloat16)
    spec_real, spec_imag = coupling_spectrum(coupling, region_map, basis)
    hat_real, hat_imag = forward(regrouped, basis_low)
    sigma_real, sigma_imag = combine(
        hat_real, hat_imag, spec_real, spec_imag, occupation, shift, lesser.shape[0]
    )
    result = inverse(sigma_real, sigma_imag, basis_low)
    returned = lax.all_to_all(result, momentum, split_axis=3, concat_axis=4, tiled=True)
    return (returned[0], returned[1])


def whole_tiles(shape, groups, shares):
    energies, blocks, momenta, height, columns = shape
    return (
        groups == 2
        and shares >= 4
        and shares & (shares - 1) == 0
        and blocks == 1
        and height == TILE * shares
        and TILE % (energies * momenta) == 0
        and columns % 128 == 0
    )


def solution(mesh):
    groups, shares = mesh.shape["grp"], mesh.shape["mom"]
    split = jax.sharding.Mesh(mesh.devices.reshape(groups, 2, shares // 2), AXES)

    def on_device(lesser, *rest):
        if whole_tiles(lesser.shape, groups, shares):
            return by_rows(lesser, *rest, groups, shares)
        return by_groups(lesser, *rest, AXES[1:])

    slab = P("grp", None, AXES[1:], None, None)
    return jax.shard_map(
        on_device,
        mesh=split,
        in_specs=(slab, slab, P(), P(), P(), P()),
        out_specs=(slab, slab),
        check_vma=False,
    )
```

```python
import functools
import math

import jax
import jax.numpy as jnp
from jax import lax
from jax.experimental import pallas as pl
from jax.experimental.pallas import tpu as pltpu
from jax.sharding import PartitionSpec as P

SMAX = 2
TILE = 16
VMEM_BYTES = 32 * 1024 * 1024
APART = 1 << 16
AXES = ("grp", "mom")


def turned(states, rows, back):
    size = states * rows
    down = lax.broadcasted_iota(jnp.int32, (size, size), 0)
    across = lax.broadcasted_iota(jnp.int32, (size, size), 1)
    if back:
        down, across = across, down
    bits = states.bit_length() - 1
    there = (down & (states - 1)) * rows + (down >> bits) == across
    return jnp.where(there, 1.0, 0.0).astype(jnp.bfloat16)


def mix_kernel(matrix_ref, in_ref, out_ref):
    devices, size, width = in_ref.shape
    for start in range(0, size, TILE):
        block = in_ref[:, start : start + TILE, :].reshape(devices * TILE, width)
        mixed = jnp.dot(matrix_ref[...], block, preferred_element_type=jnp.float32)
        out_ref[:, start : start + TILE, :] = mixed.astype(out_ref.dtype).reshape(
            devices, TILE, width
        )


def unpack_kernel(in_ref, lesser_ref, greater_ref, held, sent):
    pieces, rows = held.shape[1], held.shape[4]
    perm = turned(in_ref.shape[1] // rows, rows, True)
    copies = []
    for side, ref in enumerate((lesser_ref, greater_ref)):
        for piece in range(pieces):
            moved = jnp.dot(perm, in_ref[side * pieces + piece], preferred_element_type=jnp.float32)
            held[side, piece] = moved.astype(held.dtype).reshape(held.shape[2:])
            copy = pltpu.make_async_copy(
                held.at[side, piece],
                ref.at[:, 0, :, piece * rows : (piece + 1) * rows, :],
                sent.at[side, piece],
            )
            copy.start()
            copies.append(copy)
    for copy in copies:
        copy.wait()


def pack_kernel(matrix_ref, lesser_ref, greater_ref, out_ref):
    pieces, (size, width) = out_ref.shape[0] // 2, out_ref.shape[1:]
    rows = lesser_ref.shape[3] // pieces
    perm = turned(size // rows, rows, False)
    for side, ref in enumerate((lesser_ref, greater_ref)):
        for piece in range(pieces):
            block = ref[:, :, :, piece * rows : (piece + 1) * rows, :].reshape(size, width)
            moved = jnp.dot(perm, block, preferred_element_type=jnp.float32)
            out_ref[side * pieces + piece] = moved.astype(out_ref.dtype)


def build_kernel(
    groups, shares, momenta, energies, region_ref, shift_ref, occupation_ref, coupling_ref, out_ref
):
    points = shares * momenta
    states = energies * momenta
    regions, modes = coupling_ref.shape[:2]
    size = out_ref.shape[0]
    place = lax.axis_index("grp") * shares + lax.axis_index("mom")
    greater = lax.div(place, jnp.int32(groups * shares // 2)).astype(jnp.float32)
    chosen = jnp.zeros(coupling_ref.shape[1:], jnp.float32)
    for region in range(regions):
        chosen = jnp.where(region_ref[...] == region, coupling_ref[region], chosen)

    def energy_code(at):
        device, row = at >> (TILE.bit_length() - 1), (at & (TILE - 1)) >> (states.bit_length() - 1)
        energy = (at & (states - 1)) >> (momenta.bit_length() - 1)
        return row * APART + (device >> (shares.bit_length() - 1)) * energies + energy

    down = lax.broadcasted_iota(jnp.int32, (size, points), 0)
    momentum = ((down >> (TILE.bit_length() - 1)) & (shares - 1)) * momenta + (down & (momenta - 1))
    pick = momentum == lax.broadcasted_iota(jnp.int32, (size, points), 1)
    pick = jnp.where(pick, 1.0, 0.0).astype(jnp.bfloat16)
    apart = energy_code(lax.broadcasted_iota(jnp.int32, (size, 1), 0)) - energy_code(
        lax.broadcasted_iota(jnp.int32, (1, size), 1)
    )
    total = jnp.zeros((size, size), jnp.float32)
    for step in range(-SMAX, SMAX + 1):
        if step == 0:
            continue
        row = jnp.zeros((1, points), jnp.float32)
        for mode in range(modes):
            filling = occupation_ref[mode] + (greater if step > 0 else 1.0 - greater)
            weight = jnp.where(shift_ref[mode] == abs(step), filling, 0.0)
            row = row + weight * chosen[mode : mode + 1, :]
        wide = jnp.broadcast_to(jnp.concatenate([row, row], axis=1), (points, 2 * points))
        circle = pltpu.roll(wide, 0, 1, stride=1, stride_axis=0)[:, :points]
        half = jnp.dot(
            pick, circle.astype(jnp.bfloat16), preferred_element_type=jnp.float32
        ).astype(jnp.bfloat16)
        full = lax.dot_general(
            pick, half, (((1,), (1,)), ((), ())), preferred_element_type=jnp.float32
        )
        total = jnp.where(apart == step, full, total)
    out_ref[...] = total.astype(out_ref.dtype)


def params():
    return pltpu.CompilerParams(vmem_limit_bytes=VMEM_BYTES)


SCALARS = pl.BlockSpec(memory_space=pltpu.SMEM)
VECTORS = pl.BlockSpec(memory_space=pltpu.VMEM)
SLABS = pl.BlockSpec(memory_space=pl.ANY)


def build(coupling, occupation, shift, region_map, groups, shares, momenta, energies):
    size, points = groups * shares * TILE, shares * momenta
    return pl.pallas_call(
        functools.partial(build_kernel, groups, shares, momenta, energies),
        out_shape=jax.ShapeDtypeStruct((size, size), jnp.bfloat16),
        in_specs=[VECTORS, SCALARS, SCALARS, VECTORS],
        out_specs=VECTORS,
        compiler_params=params(),
        cost_estimate=pl.CostEstimate(
            flops=400 * size * size * points, bytes_accessed=80 * size * size, transcendentals=0
        ),
        name="build",
    )(region_map.reshape(1, 1), shift, occupation, coupling)


def pack(matrix, lesser, greater, pieces, rows):
    energies, _, momenta, _, columns = lesser.shape
    size = energies * momenta * rows
    return pl.pallas_call(
        pack_kernel,
        out_shape=jax.ShapeDtypeStruct((2 * pieces, size, columns), lesser.dtype),
        in_specs=[SLABS, VECTORS, VECTORS],
        out_specs=VECTORS,
        compiler_params=params(),
        name="pack",
    )(matrix, lesser, greater)


def unpack(packed, shape, pieces, rows):
    energies, _, momenta, _, columns = shape
    out = jax.ShapeDtypeStruct(shape, packed.dtype)
    return pl.pallas_call(
        unpack_kernel,
        out_shape=(out, out),
        in_specs=[VECTORS],
        out_specs=(SLABS, SLABS),
        scratch_shapes=[
            pltpu.VMEM((2, pieces, energies, momenta, rows, columns), packed.dtype),
            pltpu.SemaphoreType.DMA((2, pieces)),
        ],
        compiler_params=params(),
        name="unpack",
    )(packed)


def mix(matrix, received):
    return pl.pallas_call(
        mix_kernel,
        out_shape=jax.ShapeDtypeStruct(received.shape, received.dtype),
        in_specs=[VECTORS, VECTORS],
        out_specs=VECTORS,
        compiler_params=params(),
        name="mix",
    )(matrix, received)


def exchange(array):
    return lax.all_to_all(array, AXES, split_axis=0, concat_axis=0, tiled=True)


def by_rows(lesser, greater, coupling, occupation, shift, region_map, groups, shares):
    pieces = groups * shares // 2
    rows = lesser.shape[3] // pieces
    matrix = build(
        coupling, occupation, shift, region_map, groups, shares, lesser.shape[2], lesser.shape[0]
    )
    sent = pack(matrix, lesser, greater, pieces, rows)
    returned = exchange(mix(matrix, exchange(sent)))
    return unpack(returned, lesser.shape, pieces, rows)


def with_halo(shard, sides, width):
    for axis, dim in sides:
        size, length = (lax.axis_size(axis), shard.shape[dim])
        up = [(i, (i + 1) % size) for i in range(size - 1)]
        down = [(j, i) for i, j in up]
        last = lax.slice_in_dim(shard, length - width, length, axis=dim)
        first = lax.slice_in_dim(shard, 0, width, axis=dim)
        before = lax.ppermute(last, axis, up)
        after = lax.ppermute(first, axis, down)
        shard = jnp.concatenate([before, shard, after], axis=dim)
    return shard


def dft_basis(points):
    row_index = lax.broadcasted_iota(jnp.int32, (points, points), 0)
    col_index = lax.broadcasted_iota(jnp.int32, (points, points), 1)
    angles = (row_index * col_index % points).astype(jnp.float32) * (2.0 * math.pi / points)
    return jnp.concatenate([jnp.cos(angles), jnp.sin(angles)], axis=0)


def coupling_spectrum(coupling, region_map, basis):
    regions = coupling.shape[0]
    points = coupling.shape[2]
    onehot = (region_map[:, None] == jnp.arange(regions, dtype=jnp.int32)[None, :]).astype(
        jnp.float32
    )
    chosen = jnp.einsum("br,rmq->bmq", onehot, coupling, precision=lax.Precision.HIGHEST)
    spectrum = jnp.einsum("pq,bmq->bmp", basis, chosen, precision=lax.Precision.HIGHEST)
    return (spectrum[:, :, :points], -spectrum[:, :, points:])


def forward(stacked, basis_low):
    points = stacked.shape[3]
    columns = stacked.shape[5] // 2
    mixture = jnp.einsum(
        "pk,aebkxw->aebpxw", basis_low, stacked, preferred_element_type=jnp.float32
    )
    cosine = mixture[:, :, :, :points]
    sine = mixture[:, :, :, points:]
    return (
        cosine[..., :columns] + sine[..., columns:],
        cosine[..., columns:] - sine[..., :columns],
    )


def combine(hat_real, hat_imag, spec_real, spec_imag, occupation, shift, energies):
    out_shape = (2, energies) + hat_real.shape[2:]
    sigma_real = jnp.zeros(out_shape, jnp.float32)
    sigma_imag = jnp.zeros(out_shape, jnp.float32)
    points = spec_real.shape[2]
    for phonon in range(occupation.shape[0]):
        offset = shift[phonon]
        filling = occupation[phonon]
        lower_real = lax.dynamic_slice_in_dim(hat_real, SMAX - offset, energies, 1)
        lower_imag = lax.dynamic_slice_in_dim(hat_imag, SMAX - offset, energies, 1)
        upper_real = lax.dynamic_slice_in_dim(hat_real, SMAX + offset, energies, 1)
        upper_imag = lax.dynamic_slice_in_dim(hat_imag, SMAX + offset, energies, 1)
        weight_low = jnp.stack([filling, filling + 1.0]).reshape(2, 1, 1, 1, 1, 1)
        weight_high = jnp.stack([filling + 1.0, filling]).reshape(2, 1, 1, 1, 1, 1)
        mixed_real = weight_low * lower_real + weight_high * upper_real
        mixed_imag = weight_low * lower_imag + weight_high * upper_imag
        factor_real = spec_real[:, phonon, :].reshape(1, 1, -1, points, 1, 1)
        factor_imag = spec_imag[:, phonon, :].reshape(1, 1, -1, points, 1, 1)
        sigma_real = sigma_real + factor_real * mixed_real - factor_imag * mixed_imag
        sigma_imag = sigma_imag + factor_real * mixed_imag + factor_imag * mixed_real
    return (sigma_real, sigma_imag)


def inverse(sigma_real, sigma_imag, basis_low):
    points = sigma_real.shape[3]
    columns = sigma_real.shape[5]
    spectral = jnp.concatenate([sigma_real, sigma_imag], axis=-1).astype(jnp.bfloat16)
    mixture = jnp.einsum(
        "pk,aebkxw->aebpxw", basis_low, spectral, preferred_element_type=jnp.float32
    )
    cosine = mixture[:, :, :, :points]
    sine = mixture[:, :, :, points:]
    real_part = cosine[..., :columns] - sine[..., columns:]
    imag_part = cosine[..., columns:] + sine[..., :columns]
    return (jnp.concatenate([real_part, imag_part], axis=-1) * (1.0 / points)).astype(jnp.bfloat16)


def by_groups(lesser, greater, coupling, occupation, shift, region_map):
    stacked = jnp.stack([lesser, greater])
    widened = with_halo(stacked, (("grp", 1),), SMAX)
    regrouped = lax.all_to_all(widened, "mom", split_axis=4, concat_axis=3, tiled=True)
    points = regrouped.shape[3]
    basis = dft_basis(points)
    basis_low = basis.astype(jnp.bfloat16)
    spec_real, spec_imag = coupling_spectrum(coupling, region_map, basis)
    hat_real, hat_imag = forward(regrouped, basis_low)
    sigma_real, sigma_imag = combine(
        hat_real, hat_imag, spec_real, spec_imag, occupation, shift, lesser.shape[0]
    )
    result = inverse(sigma_real, sigma_imag, basis_low)
    returned = lax.all_to_all(result, "mom", split_axis=3, concat_axis=4, tiled=True)
    return (returned[0], returned[1])


def on_device(groups, shares, lesser, greater, coupling, occupation, shift, region_map):
    energies, blocks, momenta, height, columns = lesser.shape
    devices = groups * shares
    states = energies * momenta
    whole_tiles = (
        blocks == 1
        and devices >= 4
        and devices & (devices - 1) == 0
        and height % (TILE * (devices // 2)) == 0
        and TILE % states == 0
        and columns % 128 == 0
    )
    if whole_tiles:
        return by_rows(
            lesser, greater, coupling, occupation, shift, region_map, groups, shares
        )
    return by_groups(lesser, greater, coupling, occupation, shift, region_map)


def solution(mesh):
    return jax.shard_map(
        functools.partial(on_device, mesh.shape["grp"], mesh.shape["mom"]),
        mesh=mesh,
        in_specs=(
            P("grp", None, "mom", None, None),
            P("grp", None, "mom", None, None),
            P(),
            P(),
            P(),
            P(),
        ),
        out_specs=(P("grp", None, "mom", None, None), P("grp", None, "mom", None, None)),
        check_vma=False,
    )
```

```python
import functools
import math

import jax
import jax.numpy as jnp
from jax import lax
from jax.experimental import pallas as pl
from jax.experimental.pallas import tpu as pltpu
from jax.sharding import PartitionSpec as P

SMAX = 2
TILE = 16
VMEM_BYTES = 32 * 1024 * 1024
APART = 1 << 16
AXES = ("grp", "near", "half")


def turned(states, rows, back):
    size = states * rows
    down = lax.broadcasted_iota(jnp.int32, (size, size), 0)
    across = lax.broadcasted_iota(jnp.int32, (size, size), 1)
    if back:
        down, across = across, down
    bits = states.bit_length() - 1
    there = (down & (states - 1)) * rows + (down >> bits) == across
    return jnp.where(there, 1.0, 0.0).astype(jnp.bfloat16)


def mix_kernel(matrix_ref, in_ref, out_ref):
    devices, size, width = in_ref.shape
    for start in range(0, size, TILE):
        block = in_ref[:, start : start + TILE, :].reshape(devices * TILE, width)
        mixed = jnp.dot(matrix_ref[...], block, preferred_element_type=jnp.float32)
        out_ref[:, start : start + TILE, :] = mixed.astype(out_ref.dtype).reshape(
            devices, TILE, width
        )


def unpack_kernel(in_ref, lesser_ref, greater_ref, held, sent):
    pieces, rows = held.shape[1], held.shape[4]
    perm = turned(in_ref.shape[1] // rows, rows, True)
    copies = []
    for side, ref in enumerate((lesser_ref, greater_ref)):
        for piece in range(pieces):
            moved = jnp.dot(perm, in_ref[side * pieces + piece], preferred_element_type=jnp.float32)
            held[side, piece] = moved.astype(held.dtype).reshape(held.shape[2:])
            copy = pltpu.make_async_copy(
                held.at[side, piece],
                ref.at[:, 0, :, piece * rows : (piece + 1) * rows, :],
                sent.at[side, piece],
            )
            copy.start()
            copies.append(copy)
    for copy in copies:
        copy.wait()


def pack_kernel(matrix_ref, lesser_ref, greater_ref, out_ref):
    pieces, (size, width) = out_ref.shape[0] // 2, out_ref.shape[1:]
    rows = lesser_ref.shape[3] // pieces
    perm = turned(size // rows, rows, False)
    for side, ref in enumerate((lesser_ref, greater_ref)):
        for piece in range(pieces):
            block = ref[:, :, :, piece * rows : (piece + 1) * rows, :].reshape(size, width)
            moved = jnp.dot(perm, block, preferred_element_type=jnp.float32)
            out_ref[side * pieces + piece] = moved.astype(out_ref.dtype)


def build_kernel(
    groups, shares, momenta, energies, region_ref, shift_ref, occupation_ref, coupling_ref, out_ref
):
    points = shares * momenta
    states = energies * momenta
    regions, modes = coupling_ref.shape[:2]
    size = out_ref.shape[0]
    greater = lax.axis_index("grp").astype(jnp.float32)
    chosen = jnp.zeros(coupling_ref.shape[1:], jnp.float32)
    for region in range(regions):
        chosen = jnp.where(region_ref[...] == region, coupling_ref[region], chosen)

    def energy_code(at):
        device, row = at >> (TILE.bit_length() - 1), (at & (TILE - 1)) >> (states.bit_length() - 1)
        energy = (at & (states - 1)) >> (momenta.bit_length() - 1)
        return row * APART + (device >> (shares.bit_length() - 1)) * energies + energy

    down = lax.broadcasted_iota(jnp.int32, (size, points), 0)
    share = (down >> (TILE.bit_length() - 1)) & (shares - 1)
    share = (share & 1) * (shares // 2) + (share >> 1)
    momentum = share * momenta + (down & (momenta - 1))
    pick = momentum == lax.broadcasted_iota(jnp.int32, (size, points), 1)
    pick = jnp.where(pick, 1.0, 0.0).astype(jnp.bfloat16)
    apart = energy_code(lax.broadcasted_iota(jnp.int32, (size, 1), 0)) - energy_code(
        lax.broadcasted_iota(jnp.int32, (1, size), 1)
    )
    total = jnp.zeros((size, size), jnp.float32)
    for step in range(-SMAX, SMAX + 1):
        if step == 0:
            continue
        row = jnp.zeros((1, points), jnp.float32)
        for mode in range(modes):
            filling = occupation_ref[mode] + (greater if step > 0 else 1.0 - greater)
            weight = jnp.where(shift_ref[mode] == abs(step), filling, 0.0)
            row = row + weight * chosen[mode : mode + 1, :]
        wide = jnp.broadcast_to(jnp.concatenate([row, row], axis=1), (points, 2 * points))
        circle = pltpu.roll(wide, 0, 1, stride=1, stride_axis=0)[:, :points]
        half = jnp.dot(
            pick, circle.astype(jnp.bfloat16), preferred_element_type=jnp.float32
        ).astype(jnp.bfloat16)
        full = lax.dot_general(
            pick, half, (((1,), (1,)), ((), ())), preferred_element_type=jnp.float32
        )
        total = jnp.where(apart == step, full, total)
    out_ref[...] = total.astype(out_ref.dtype)


def params():
    return pltpu.CompilerParams(vmem_limit_bytes=VMEM_BYTES)


SCALARS = pl.BlockSpec(memory_space=pltpu.SMEM)
VECTORS = pl.BlockSpec(memory_space=pltpu.VMEM)
SLABS = pl.BlockSpec(memory_space=pl.ANY)


def build(coupling, occupation, shift, region_map, groups, shares, momenta, energies):
    size, points = groups * shares * TILE, shares * momenta
    return pl.pallas_call(
        functools.partial(build_kernel, groups, shares, momenta, energies),
        out_shape=jax.ShapeDtypeStruct((size, size), jnp.bfloat16),
        in_specs=[VECTORS, SCALARS, SCALARS, VECTORS],
        out_specs=VECTORS,
        compiler_params=params(),
        cost_estimate=pl.CostEstimate(
            flops=400 * size * size * points, bytes_accessed=80 * size * size, transcendentals=0
        ),
        name="build",
    )(region_map.reshape(1, 1), shift, occupation, coupling)


def pack(matrix, lesser, greater, pieces, rows):
    energies, _, momenta, _, columns = lesser.shape
    size = energies * momenta * rows
    return pl.pallas_call(
        pack_kernel,
        out_shape=jax.ShapeDtypeStruct((2 * pieces, size, columns), lesser.dtype),
        in_specs=[SLABS, VECTORS, VECTORS],
        out_specs=VECTORS,
        compiler_params=params(),
        name="pack",
    )(matrix, lesser, greater)


def unpack(packed, shape, pieces, rows):
    energies, _, momenta, _, columns = shape
    out = jax.ShapeDtypeStruct(shape, packed.dtype)
    return pl.pallas_call(
        unpack_kernel,
        out_shape=(out, out),
        in_specs=[VECTORS],
        out_specs=(SLABS, SLABS),
        scratch_shapes=[
            pltpu.VMEM((2, pieces, energies, momenta, rows, columns), packed.dtype),
            pltpu.SemaphoreType.DMA((2, pieces)),
        ],
        compiler_params=params(),
        name="unpack",
    )(packed)


def mix(matrix, received):
    return pl.pallas_call(
        mix_kernel,
        out_shape=jax.ShapeDtypeStruct(received.shape, received.dtype),
        in_specs=[VECTORS, VECTORS],
        out_specs=VECTORS,
        compiler_params=params(),
        name="mix",
    )(matrix, received)


def exchange(array):
    return lax.all_to_all(array, AXES, split_axis=0, concat_axis=0, tiled=True)


def by_rows(lesser, greater, coupling, occupation, shift, region_map, groups, shares):
    pieces = groups * shares // 2
    rows = lesser.shape[3] // pieces
    matrix = build(
        coupling, occupation, shift, region_map, groups, shares, lesser.shape[2], lesser.shape[0]
    )
    sent = pack(matrix, lesser, greater, pieces, rows)
    returned = exchange(mix(matrix, exchange(sent)))
    return unpack(returned, lesser.shape, pieces, rows)


def with_halo(shard, sides, width):
    for axis, dim in sides:
        size, length = (lax.axis_size(axis), shard.shape[dim])
        up = [(i, (i + 1) % size) for i in range(size - 1)]
        down = [(j, i) for i, j in up]
        last = lax.slice_in_dim(shard, length - width, length, axis=dim)
        first = lax.slice_in_dim(shard, 0, width, axis=dim)
        before = lax.ppermute(last, axis, up)
        after = lax.ppermute(first, axis, down)
        shard = jnp.concatenate([before, shard, after], axis=dim)
    return shard


def dft_basis(points):
    row_index = lax.broadcasted_iota(jnp.int32, (points, points), 0)
    col_index = lax.broadcasted_iota(jnp.int32, (points, points), 1)
    angles = (row_index * col_index % points).astype(jnp.float32) * (2.0 * math.pi / points)
    return jnp.concatenate([jnp.cos(angles), jnp.sin(angles)], axis=0)


def coupling_spectrum(coupling, region_map, basis):
    regions = coupling.shape[0]
    points = coupling.shape[2]
    onehot = (region_map[:, None] == jnp.arange(regions, dtype=jnp.int32)[None, :]).astype(
        jnp.float32
    )
    chosen = jnp.einsum("br,rmq->bmq", onehot, coupling, precision=lax.Precision.HIGHEST)
    spectrum = jnp.einsum("pq,bmq->bmp", basis, chosen, precision=lax.Precision.HIGHEST)
    return (spectrum[:, :, :points], -spectrum[:, :, points:])


def forward(stacked, basis_low):
    points = stacked.shape[3]
    columns = stacked.shape[5] // 2
    mixture = jnp.einsum(
        "pk,aebkxw->aebpxw", basis_low, stacked, preferred_element_type=jnp.float32
    )
    cosine = mixture[:, :, :, :points]
    sine = mixture[:, :, :, points:]
    return (
        cosine[..., :columns] + sine[..., columns:],
        cosine[..., columns:] - sine[..., :columns],
    )


def combine(hat_real, hat_imag, spec_real, spec_imag, occupation, shift, energies):
    out_shape = (2, energies) + hat_real.shape[2:]
    sigma_real = jnp.zeros(out_shape, jnp.float32)
    sigma_imag = jnp.zeros(out_shape, jnp.float32)
    points = spec_real.shape[2]
    for phonon in range(occupation.shape[0]):
        offset = shift[phonon]
        filling = occupation[phonon]
        lower_real = lax.dynamic_slice_in_dim(hat_real, SMAX - offset, energies, 1)
        lower_imag = lax.dynamic_slice_in_dim(hat_imag, SMAX - offset, energies, 1)
        upper_real = lax.dynamic_slice_in_dim(hat_real, SMAX + offset, energies, 1)
        upper_imag = lax.dynamic_slice_in_dim(hat_imag, SMAX + offset, energies, 1)
        weight_low = jnp.stack([filling, filling + 1.0]).reshape(2, 1, 1, 1, 1, 1)
        weight_high = jnp.stack([filling + 1.0, filling]).reshape(2, 1, 1, 1, 1, 1)
        mixed_real = weight_low * lower_real + weight_high * upper_real
        mixed_imag = weight_low * lower_imag + weight_high * upper_imag
        factor_real = spec_real[:, phonon, :].reshape(1, 1, -1, points, 1, 1)
        factor_imag = spec_imag[:, phonon, :].reshape(1, 1, -1, points, 1, 1)
        sigma_real = sigma_real + factor_real * mixed_real - factor_imag * mixed_imag
        sigma_imag = sigma_imag + factor_real * mixed_imag + factor_imag * mixed_real
    return (sigma_real, sigma_imag)


def inverse(sigma_real, sigma_imag, basis_low):
    points = sigma_real.shape[3]
    columns = sigma_real.shape[5]
    spectral = jnp.concatenate([sigma_real, sigma_imag], axis=-1).astype(jnp.bfloat16)
    mixture = jnp.einsum(
        "pk,aebkxw->aebpxw", basis_low, spectral, preferred_element_type=jnp.float32
    )
    cosine = mixture[:, :, :, :points]
    sine = mixture[:, :, :, points:]
    real_part = cosine[..., :columns] - sine[..., columns:]
    imag_part = cosine[..., columns:] + sine[..., :columns]
    return (jnp.concatenate([real_part, imag_part], axis=-1) * (1.0 / points)).astype(jnp.bfloat16)


def by_groups(lesser, greater, coupling, occupation, shift, region_map, momentum):
    stacked = jnp.stack([lesser, greater])
    widened = with_halo(stacked, (("grp", 1),), SMAX)
    regrouped = lax.all_to_all(widened, momentum, split_axis=4, concat_axis=3, tiled=True)
    points = regrouped.shape[3]
    basis = dft_basis(points)
    basis_low = basis.astype(jnp.bfloat16)
    spec_real, spec_imag = coupling_spectrum(coupling, region_map, basis)
    hat_real, hat_imag = forward(regrouped, basis_low)
    sigma_real, sigma_imag = combine(
        hat_real, hat_imag, spec_real, spec_imag, occupation, shift, lesser.shape[0]
    )
    result = inverse(sigma_real, sigma_imag, basis_low)
    returned = lax.all_to_all(result, momentum, split_axis=3, concat_axis=4, tiled=True)
    return (returned[0], returned[1])


def whole_tiles(shape, groups, shares):
    energies, blocks, momenta, height, columns = shape
    return (
        groups == 2
        and shares & (shares - 1) == 0
        and blocks == 1
        and height == TILE * shares
        and TILE % (energies * momenta) == 0
        and columns % 128 == 0
    )


def solution(mesh):
    groups, shares = mesh.shape["grp"], mesh.shape["mom"]
    momentum = ("half", "near")
    split = jax.sharding.Mesh(mesh.devices.reshape(groups, 2, shares // 2), ("grp",) + momentum)

    def on_device(lesser, *rest):
        if whole_tiles(lesser.shape, groups, shares):
            return by_rows(lesser, *rest, groups, shares)
        return by_groups(lesser, *rest, momentum)

    slab = P("grp", None, momentum, None, None)
    return jax.shard_map(
        on_device,
        mesh=split,
        in_specs=(slab, slab, P(), P(), P(), P()),
        out_specs=(slab, slab),
        check_vma=False,
    )
```

```python
import functools
import math

import jax
import jax.numpy as jnp
from jax import lax
from jax.experimental import pallas as pl
from jax.experimental.pallas import tpu as pltpu
from jax.sharding import PartitionSpec as P

SMAX = 2
TILE = 16
VMEM_BYTES = 32 * 1024 * 1024
AXES = ("grp", "mom")


def turned(states, rows, back):
    size = states * rows
    down = lax.broadcasted_iota(jnp.int32, (size, size), 0)
    across = lax.broadcasted_iota(jnp.int32, (size, size), 1)
    if back:
        down, across = across, down
    bits = states.bit_length() - 1
    there = (down & (states - 1)) * rows + (down >> bits) == across
    return jnp.where(there, 1.0, 0.0).astype(jnp.bfloat16)


def mix_kernel(matrix_ref, in_ref, out_ref):
    devices, size, width = in_ref.shape
    for start in range(0, size, TILE):
        block = in_ref[:, start : start + TILE, :].reshape(devices * TILE, width)
        mixed = jnp.dot(matrix_ref[...], block, preferred_element_type=jnp.float32)
        out_ref[:, start : start + TILE, :] = mixed.astype(out_ref.dtype).reshape(
            devices, TILE, width
        )


def unpack_kernel(in_ref, lesser_ref, greater_ref, held, sent):
    pieces, rows = held.shape[1], held.shape[4]
    perm = turned(in_ref.shape[1] // rows, rows, True)
    copies = []
    for side, ref in enumerate((lesser_ref, greater_ref)):
        for piece in range(pieces):
            moved = jnp.dot(perm, in_ref[side * pieces + piece], preferred_element_type=jnp.float32)
            held[side, piece] = moved.astype(held.dtype).reshape(held.shape[2:])
            copy = pltpu.make_async_copy(
                held.at[side, piece],
                ref.at[:, 0, :, piece * rows : (piece + 1) * rows, :],
                sent.at[side, piece],
            )
            copy.start()
            copies.append(copy)
    for copy in copies:
        copy.wait()


def pack_kernel(matrix_ref, lesser_ref, greater_ref, out_ref):
    pieces, (size, width) = out_ref.shape[0] // 2, out_ref.shape[1:]
    rows = lesser_ref.shape[3] // pieces
    perm = turned(size // rows, rows, False)
    for side, ref in enumerate((lesser_ref, greater_ref)):
        for piece in range(pieces):
            block = ref[:, :, :, piece * rows : (piece + 1) * rows, :].reshape(size, width)
            moved = jnp.dot(perm, block, preferred_element_type=jnp.float32)
            out_ref[side * pieces + piece] = moved.astype(out_ref.dtype)


def build_kernel(groups, shares, momenta, energies, regions, small_ref, out_ref):
    points = shares * momenta
    states = energies * momenta
    size, levels = out_ref.shape[0], groups * energies
    modes = (small_ref.shape[0] - 3) // regions
    occupation, shift, region = (
        small_ref[at : at + 1, :] for at in range(regions * modes, regions * modes + 3)
    )
    place = lax.axis_index("grp") * shares + lax.axis_index("mom")
    greater = lax.div(place, jnp.int32(groups * shares // 2)).astype(jnp.float32)
    chosen = jnp.zeros((modes, points), jnp.float32)
    for at in range(regions):
        here = region[:, 0:1] == float(at)
        chosen = jnp.where(here, small_ref[at * modes : (at + 1) * modes, :], chosen)
    circles = {}
    for step in range(-SMAX, SMAX + 1):
        if step == 0:
            continue
        row = jnp.zeros((1, points), jnp.float32)
        for mode in range(modes):
            filling = occupation[:, mode : mode + 1] + (greater if step > 0 else 1.0 - greater)
            weight = jnp.where(shift[:, mode : mode + 1] == float(abs(step)), filling, 0.0)
            row = row + weight * chosen[mode : mode + 1, :]
        wide = jnp.broadcast_to(jnp.concatenate([row, row], axis=1), (points, 2 * points))
        circles[step] = pltpu.roll(wide, 0, 1, stride=1, stride_axis=0)[:, :points]
    nothing = jnp.zeros((points, points), jnp.float32)
    plain = jnp.concatenate(
        [
            jnp.concatenate([circles.get(out - level, nothing) for out in range(levels)], axis=1)
            for level in range(levels)
        ],
        axis=0,
    ).astype(jnp.bfloat16)

    def parts(at):
        device, row = at >> (TILE.bit_length() - 1), (at & (TILE - 1)) >> (states.bit_length() - 1)
        energy = (at & (states - 1)) >> (momenta.bit_length() - 1)
        energy = (device >> (shares.bit_length() - 1)) * energies + energy
        return row, (energy * shares + (device & (shares - 1))) * momenta + (at & (momenta - 1))

    state = parts(lax.broadcasted_iota(jnp.int32, (size, 1), 0))[1]
    pick = state == lax.broadcasted_iota(jnp.int32, (size, levels * points), 1)
    pick = jnp.where(pick, 1.0, 0.0).astype(jnp.bfloat16)
    half = jnp.dot(pick, plain, preferred_element_type=jnp.float32).astype(jnp.bfloat16)
    full = lax.dot_general(
        pick, half, (((1,), (1,)), ((), ())), preferred_element_type=jnp.float32
    )
    same = parts(lax.broadcasted_iota(jnp.int32, (size, 1), 0))[0] == parts(
        lax.broadcasted_iota(jnp.int32, (1, size), 1)
    )[0]
    out_ref[...] = jnp.where(same, full, 0.0).astype(out_ref.dtype)


def params():
    return pltpu.CompilerParams(vmem_limit_bytes=VMEM_BYTES)


VECTORS = pl.BlockSpec(memory_space=pltpu.VMEM)
SLABS = pl.BlockSpec(memory_space=pl.ANY)


def build(coupling, occupation, shift, region_map, groups, shares, momenta, energies):
    size, points = groups * shares * TILE, shares * momenta
    scalars = [
        jnp.pad(part[None, :], ((0, 0), (0, points - part.shape[0]))).astype(jnp.float32)
        for part in (occupation, shift, region_map)
    ]
    small = jnp.concatenate([coupling.reshape(-1, points)] + scalars, axis=0)
    return pl.pallas_call(
        functools.partial(build_kernel, groups, shares, momenta, energies, coupling.shape[0]),
        out_shape=jax.ShapeDtypeStruct((size, size), jnp.bfloat16),
        in_specs=[VECTORS],
        out_specs=VECTORS,
        compiler_params=params(),
        cost_estimate=pl.CostEstimate(
            flops=400 * size * size * points, bytes_accessed=80 * size * size, transcendentals=0
        ),
        name="build",
    )(small)


def pack(matrix, lesser, greater, pieces, rows):
    energies, _, momenta, _, columns = lesser.shape
    size = energies * momenta * rows
    return pl.pallas_call(
        pack_kernel,
        out_shape=jax.ShapeDtypeStruct((2 * pieces, size, columns), lesser.dtype),
        in_specs=[SLABS, VECTORS, VECTORS],
        out_specs=VECTORS,
        compiler_params=params(),
        name="pack",
    )(matrix, lesser, greater)


def unpack(packed, shape, pieces, rows):
    energies, _, momenta, _, columns = shape
    out = jax.ShapeDtypeStruct(shape, packed.dtype)
    return pl.pallas_call(
        unpack_kernel,
        out_shape=(out, out),
        in_specs=[VECTORS],
        out_specs=(SLABS, SLABS),
        scratch_shapes=[
            pltpu.VMEM((2, pieces, energies, momenta, rows, columns), packed.dtype),
            pltpu.SemaphoreType.DMA((2, pieces)),
        ],
        compiler_params=params(),
        name="unpack",
    )(packed)


def mix(matrix, received):
    return pl.pallas_call(
        mix_kernel,
        out_shape=jax.ShapeDtypeStruct(received.shape, received.dtype),
        in_specs=[VECTORS, VECTORS],
        out_specs=VECTORS,
        compiler_params=params(),
        name="mix",
    )(matrix, received)


def exchange(array):
    return lax.all_to_all(array, AXES, split_axis=0, concat_axis=0, tiled=True)


def by_rows(lesser, greater, coupling, occupation, shift, region_map, groups, shares):
    pieces = groups * shares // 2
    rows = lesser.shape[3] // pieces
    matrix = build(
        coupling, occupation, shift, region_map, groups, shares, lesser.shape[2], lesser.shape[0]
    )
    sent = pack(matrix, lesser, greater, pieces, rows)
    returned = exchange(mix(matrix, exchange(sent)))
    return unpack(returned, lesser.shape, pieces, rows)


def with_halo(shard, sides, width):
    for axis, dim in sides:
        size, length = (lax.axis_size(axis), shard.shape[dim])
        up = [(i, (i + 1) % size) for i in range(size - 1)]
        down = [(j, i) for i, j in up]
        last = lax.slice_in_dim(shard, length - width, length, axis=dim)
        first = lax.slice_in_dim(shard, 0, width, axis=dim)
        before = lax.ppermute(last, axis, up)
        after = lax.ppermute(first, axis, down)
        shard = jnp.concatenate([before, shard, after], axis=dim)
    return shard


def dft_basis(points):
    row_index = lax.broadcasted_iota(jnp.int32, (points, points), 0)
    col_index = lax.broadcasted_iota(jnp.int32, (points, points), 1)
    angles = (row_index * col_index % points).astype(jnp.float32) * (2.0 * math.pi / points)
    return jnp.concatenate([jnp.cos(angles), jnp.sin(angles)], axis=0)


def coupling_spectrum(coupling, region_map, basis):
    regions = coupling.shape[0]
    points = coupling.shape[2]
    onehot = (region_map[:, None] == jnp.arange(regions, dtype=jnp.int32)[None, :]).astype(
        jnp.float32
    )
    chosen = jnp.einsum("br,rmq->bmq", onehot, coupling, precision=lax.Precision.HIGHEST)
    spectrum = jnp.einsum("pq,bmq->bmp", basis, chosen, precision=lax.Precision.HIGHEST)
    return (spectrum[:, :, :points], -spectrum[:, :, points:])


def forward(stacked, basis_low):
    points = stacked.shape[3]
    columns = stacked.shape[5] // 2
    mixture = jnp.einsum(
        "pk,aebkxw->aebpxw", basis_low, stacked, preferred_element_type=jnp.float32
    )
    cosine = mixture[:, :, :, :points]
    sine = mixture[:, :, :, points:]
    return (
        cosine[..., :columns] + sine[..., columns:],
        cosine[..., columns:] - sine[..., :columns],
    )


def combine(hat_real, hat_imag, spec_real, spec_imag, occupation, shift, energies):
    out_shape = (2, energies) + hat_real.shape[2:]
    sigma_real = jnp.zeros(out_shape, jnp.float32)
    sigma_imag = jnp.zeros(out_shape, jnp.float32)
    points = spec_real.shape[2]
    for phonon in range(occupation.shape[0]):
        offset = shift[phonon]
        filling = occupation[phonon]
        lower_real = lax.dynamic_slice_in_dim(hat_real, SMAX - offset, energies, 1)
        lower_imag = lax.dynamic_slice_in_dim(hat_imag, SMAX - offset, energies, 1)
        upper_real = lax.dynamic_slice_in_dim(hat_real, SMAX + offset, energies, 1)
        upper_imag = lax.dynamic_slice_in_dim(hat_imag, SMAX + offset, energies, 1)
        weight_low = jnp.stack([filling, filling + 1.0]).reshape(2, 1, 1, 1, 1, 1)
        weight_high = jnp.stack([filling + 1.0, filling]).reshape(2, 1, 1, 1, 1, 1)
        mixed_real = weight_low * lower_real + weight_high * upper_real
        mixed_imag = weight_low * lower_imag + weight_high * upper_imag
        factor_real = spec_real[:, phonon, :].reshape(1, 1, -1, points, 1, 1)
        factor_imag = spec_imag[:, phonon, :].reshape(1, 1, -1, points, 1, 1)
        sigma_real = sigma_real + factor_real * mixed_real - factor_imag * mixed_imag
        sigma_imag = sigma_imag + factor_real * mixed_imag + factor_imag * mixed_real
    return (sigma_real, sigma_imag)


def inverse(sigma_real, sigma_imag, basis_low):
    points = sigma_real.shape[3]
    columns = sigma_real.shape[5]
    spectral = jnp.concatenate([sigma_real, sigma_imag], axis=-1).astype(jnp.bfloat16)
    mixture = jnp.einsum(
        "pk,aebkxw->aebpxw", basis_low, spectral, preferred_element_type=jnp.float32
    )
    cosine = mixture[:, :, :, :points]
    sine = mixture[:, :, :, points:]
    real_part = cosine[..., :columns] - sine[..., columns:]
    imag_part = cosine[..., columns:] + sine[..., :columns]
    return (jnp.concatenate([real_part, imag_part], axis=-1) * (1.0 / points)).astype(jnp.bfloat16)


def by_groups(lesser, greater, coupling, occupation, shift, region_map):
    stacked = jnp.stack([lesser, greater])
    widened = with_halo(stacked, (("grp", 1),), SMAX)
    regrouped = lax.all_to_all(widened, "mom", split_axis=4, concat_axis=3, tiled=True)
    points = regrouped.shape[3]
    basis = dft_basis(points)
    basis_low = basis.astype(jnp.bfloat16)
    spec_real, spec_imag = coupling_spectrum(coupling, region_map, basis)
    hat_real, hat_imag = forward(regrouped, basis_low)
    sigma_real, sigma_imag = combine(
        hat_real, hat_imag, spec_real, spec_imag, occupation, shift, lesser.shape[0]
    )
    result = inverse(sigma_real, sigma_imag, basis_low)
    returned = lax.all_to_all(result, "mom", split_axis=3, concat_axis=4, tiled=True)
    return (returned[0], returned[1])


def on_device(groups, shares, lesser, greater, coupling, occupation, shift, region_map):
    energies, blocks, momenta, height, columns = lesser.shape
    devices = groups * shares
    states = energies * momenta
    whole_tiles = (
        blocks == 1
        and devices >= 4
        and devices & (devices - 1) == 0
        and height % (TILE * (devices // 2)) == 0
        and TILE % states == 0
        and columns % 128 == 0
    )
    if whole_tiles:
        return by_rows(
            lesser, greater, coupling, occupation, shift, region_map, groups, shares
        )
    return by_groups(lesser, greater, coupling, occupation, shift, region_map)


def solution(mesh):
    return jax.shard_map(
        functools.partial(on_device, mesh.shape["grp"], mesh.shape["mom"]),
        mesh=mesh,
        in_specs=(
            P("grp", None, "mom", None, None),
            P("grp", None, "mom", None, None),
            P(),
            P(),
            P(),
            P(),
        ),
        out_specs=(P("grp", None, "mom", None, None), P("grp", None, "mom", None, None)),
        check_vma=False,
    )
```

```python
import functools
import math

import jax
import jax.numpy as jnp
from jax import lax
from jax.experimental import pallas as pl
from jax.experimental.pallas import tpu as pltpu
from jax.sharding import PartitionSpec as P

SMAX = 2
TILE = 16
VMEM_BYTES = 32 * 1024 * 1024
AXES = ("grp", "mom")


def turned(states, rows, back):
    size = states * rows
    down = lax.broadcasted_iota(jnp.int32, (size, size), 0)
    across = lax.broadcasted_iota(jnp.int32, (size, size), 1)
    if back:
        down, across = across, down
    bits = states.bit_length() - 1
    there = (down & (states - 1)) * rows + (down >> bits) == across
    return jnp.where(there, 1.0, 0.0).astype(jnp.bfloat16)


def mix_kernel(matrix_ref, in_ref, out_ref):
    devices, size, width = in_ref.shape
    for start in range(0, size, TILE):
        block = in_ref[:, start : start + TILE, :].reshape(devices * TILE, width)
        mixed = jnp.dot(matrix_ref[...], block, preferred_element_type=jnp.float32)
        out_ref[:, start : start + TILE, :] = mixed.astype(out_ref.dtype).reshape(
            devices, TILE, width
        )


def unpack_kernel(in_ref, lesser_ref, greater_ref, held, sent):
    pieces, rows = held.shape[1], held.shape[4]
    perm = turned(in_ref.shape[1] // rows, rows, True)
    copies = []
    for side, ref in enumerate((lesser_ref, greater_ref)):
        for piece in range(pieces):
            moved = jnp.dot(perm, in_ref[side * pieces + piece], preferred_element_type=jnp.float32)
            held[side, piece] = moved.astype(held.dtype).reshape(held.shape[2:])
            copy = pltpu.make_async_copy(
                held.at[side, piece],
                ref.at[:, 0, :, piece * rows : (piece + 1) * rows, :],
                sent.at[side, piece],
            )
            copy.start()
            copies.append(copy)
    for copy in copies:
        copy.wait()


def pack_kernel(matrix_ref, lesser_ref, greater_ref, out_ref):
    pieces, (size, width) = out_ref.shape[0] // 2, out_ref.shape[1:]
    rows = lesser_ref.shape[3] // pieces
    perm = turned(size // rows, rows, False)
    for side, ref in enumerate((lesser_ref, greater_ref)):
        for piece in range(pieces):
            block = ref[:, :, :, piece * rows : (piece + 1) * rows, :].reshape(size, width)
            moved = jnp.dot(perm, block, preferred_element_type=jnp.float32)
            out_ref[side * pieces + piece] = moved.astype(out_ref.dtype)


def build_kernel(groups, shares, momenta, energies, regions, small_ref, out_ref):
    points = shares * momenta
    states = energies * momenta
    size, levels = out_ref.shape[0], groups * energies
    modes = (small_ref.shape[0] - 3) // regions
    occupation, shift, region = (
        small_ref[at : at + 1, :] for at in range(regions * modes, regions * modes + 3)
    )
    place = lax.axis_index("grp") * shares + lax.axis_index("mom")
    greater = lax.div(place, jnp.int32(groups * shares // 2)).astype(jnp.float32)
    chosen = jnp.zeros((modes, points), jnp.float32)
    for at in range(regions):
        here = region[:, 0:1] == float(at)
        chosen = jnp.where(here, small_ref[at * modes : (at + 1) * modes, :], chosen)
    circles = {}
    for step in range(-SMAX, SMAX + 1):
        if step == 0:
            continue
        row = jnp.zeros((1, points), jnp.float32)
        for mode in range(modes):
            filling = occupation[:, mode : mode + 1] + (greater if step > 0 else 1.0 - greater)
            weight = jnp.where(shift[:, mode : mode + 1] == float(abs(step)), filling, 0.0)
            row = row + weight * chosen[mode : mode + 1, :]
        wide = jnp.broadcast_to(jnp.concatenate([row, row], axis=1), (points, 2 * points))
        circles[step] = pltpu.roll(wide, 0, 1, stride=1, stride_axis=0)[:, :points]
    nothing = jnp.zeros((points, points), jnp.float32)
    plain = jnp.concatenate(
        [
            jnp.concatenate([circles.get(out - level, nothing) for out in range(levels)], axis=1)
            for level in range(levels)
        ],
        axis=0,
    ).astype(jnp.bfloat16)

    def parts(at):
        device, row = at >> (TILE.bit_length() - 1), (at & (TILE - 1)) >> (states.bit_length() - 1)
        energy = (at & (states - 1)) >> (momenta.bit_length() - 1)
        energy = (device >> (shares.bit_length() - 1)) * energies + energy
        return row, (energy * shares + (device & (shares - 1))) * momenta + (at & (momenta - 1))

    state = parts(lax.broadcasted_iota(jnp.int32, (size, 1), 0))[1]
    pick = state == lax.broadcasted_iota(jnp.int32, (size, levels * points), 1)
    pick = jnp.where(pick, 1.0, 0.0).astype(jnp.bfloat16)
    half = jnp.dot(pick, plain, preferred_element_type=jnp.float32).astype(jnp.bfloat16)
    full = lax.dot_general(
        pick, half, (((1,), (1,)), ((), ())), preferred_element_type=jnp.float32
    )
    same = parts(lax.broadcasted_iota(jnp.int32, (size, 1), 0))[0] == parts(
        lax.broadcasted_iota(jnp.int32, (1, size), 1)
    )[0]
    out_ref[...] = jnp.where(same, full, 0.0).astype(out_ref.dtype)


def params():
    return pltpu.CompilerParams(vmem_limit_bytes=VMEM_BYTES)


VECTORS = pl.BlockSpec(memory_space=pltpu.VMEM)
SLABS = pl.BlockSpec(memory_space=pl.ANY)


def build(coupling, occupation, shift, region_map, groups, shares, momenta, energies):
    size, points = groups * shares * TILE, shares * momenta
    rows = coupling.shape[0] * coupling.shape[1]
    small = jnp.pad(coupling.reshape(rows, points), ((0, 3), (0, 0)))
    for at, part in enumerate((occupation, shift, region_map)):
        part = jnp.pad(part[None, :], ((rows + at, 2 - at), (0, points - part.shape[0])))
        small = small + part.astype(jnp.float32)
    return pl.pallas_call(
        functools.partial(build_kernel, groups, shares, momenta, energies, coupling.shape[0]),
        out_shape=jax.ShapeDtypeStruct((size, size), jnp.bfloat16),
        in_specs=[VECTORS],
        out_specs=VECTORS,
        compiler_params=params(),
        cost_estimate=pl.CostEstimate(
            flops=400 * size * size * points, bytes_accessed=80 * size * size, transcendentals=0
        ),
        name="build",
    )(small)


def pack(matrix, lesser, greater, pieces, rows):
    energies, _, momenta, _, columns = lesser.shape
    size = energies * momenta * rows
    return pl.pallas_call(
        pack_kernel,
        out_shape=jax.ShapeDtypeStruct((2 * pieces, size, columns), lesser.dtype),
        in_specs=[SLABS, VECTORS, VECTORS],
        out_specs=VECTORS,
        compiler_params=params(),
        name="pack",
    )(matrix, lesser, greater)


def unpack(packed, shape, pieces, rows):
    energies, _, momenta, _, columns = shape
    out = jax.ShapeDtypeStruct(shape, packed.dtype)
    return pl.pallas_call(
        unpack_kernel,
        out_shape=(out, out),
        in_specs=[VECTORS],
        out_specs=(SLABS, SLABS),
        scratch_shapes=[
            pltpu.VMEM((2, pieces, energies, momenta, rows, columns), packed.dtype),
            pltpu.SemaphoreType.DMA((2, pieces)),
        ],
        compiler_params=params(),
        name="unpack",
    )(packed)


def mix(matrix, received):
    return pl.pallas_call(
        mix_kernel,
        out_shape=jax.ShapeDtypeStruct(received.shape, received.dtype),
        in_specs=[VECTORS, VECTORS],
        out_specs=VECTORS,
        compiler_params=params(),
        name="mix",
    )(matrix, received)


def exchange(array):
    return lax.all_to_all(array, AXES, split_axis=0, concat_axis=0, tiled=True)


def by_rows(lesser, greater, coupling, occupation, shift, region_map, groups, shares):
    pieces = groups * shares // 2
    rows = lesser.shape[3] // pieces
    matrix = build(
        coupling, occupation, shift, region_map, groups, shares, lesser.shape[2], lesser.shape[0]
    )
    sent = pack(matrix, lesser, greater, pieces, rows)
    returned = exchange(mix(matrix, exchange(sent)))
    return unpack(returned, lesser.shape, pieces, rows)


def with_halo(shard, sides, width):
    for axis, dim in sides:
        size, length = (lax.axis_size(axis), shard.shape[dim])
        up = [(i, (i + 1) % size) for i in range(size - 1)]
        down = [(j, i) for i, j in up]
        last = lax.slice_in_dim(shard, length - width, length, axis=dim)
        first = lax.slice_in_dim(shard, 0, width, axis=dim)
        before = lax.ppermute(last, axis, up)
        after = lax.ppermute(first, axis, down)
        shard = jnp.concatenate([before, shard, after], axis=dim)
    return shard


def dft_basis(points):
    row_index = lax.broadcasted_iota(jnp.int32, (points, points), 0)
    col_index = lax.broadcasted_iota(jnp.int32, (points, points), 1)
    angles = (row_index * col_index % points).astype(jnp.float32) * (2.0 * math.pi / points)
    return jnp.concatenate([jnp.cos(angles), jnp.sin(angles)], axis=0)


def coupling_spectrum(coupling, region_map, basis):
    regions = coupling.shape[0]
    points = coupling.shape[2]
    onehot = (region_map[:, None] == jnp.arange(regions, dtype=jnp.int32)[None, :]).astype(
        jnp.float32
    )
    chosen = jnp.einsum("br,rmq->bmq", onehot, coupling, precision=lax.Precision.HIGHEST)
    spectrum = jnp.einsum("pq,bmq->bmp", basis, chosen, precision=lax.Precision.HIGHEST)
    return (spectrum[:, :, :points], -spectrum[:, :, points:])


def forward(stacked, basis_low):
    points = stacked.shape[3]
    columns = stacked.shape[5] // 2
    mixture = jnp.einsum(
        "pk,aebkxw->aebpxw", basis_low, stacked, preferred_element_type=jnp.float32
    )
    cosine = mixture[:, :, :, :points]
    sine = mixture[:, :, :, points:]
    return (
        cosine[..., :columns] + sine[..., columns:],
        cosine[..., columns:] - sine[..., :columns],
    )


def combine(hat_real, hat_imag, spec_real, spec_imag, occupation, shift, energies):
    out_shape = (2, energies) + hat_real.shape[2:]
    sigma_real = jnp.zeros(out_shape, jnp.float32)
    sigma_imag = jnp.zeros(out_shape, jnp.float32)
    points = spec_real.shape[2]
    for phonon in range(occupation.shape[0]):
        offset = shift[phonon]
        filling = occupation[phonon]
        lower_real = lax.dynamic_slice_in_dim(hat_real, SMAX - offset, energies, 1)
        lower_imag = lax.dynamic_slice_in_dim(hat_imag, SMAX - offset, energies, 1)
        upper_real = lax.dynamic_slice_in_dim(hat_real, SMAX + offset, energies, 1)
        upper_imag = lax.dynamic_slice_in_dim(hat_imag, SMAX + offset, energies, 1)
        weight_low = jnp.stack([filling, filling + 1.0]).reshape(2, 1, 1, 1, 1, 1)
        weight_high = jnp.stack([filling + 1.0, filling]).reshape(2, 1, 1, 1, 1, 1)
        mixed_real = weight_low * lower_real + weight_high * upper_real
        mixed_imag = weight_low * lower_imag + weight_high * upper_imag
        factor_real = spec_real[:, phonon, :].reshape(1, 1, -1, points, 1, 1)
        factor_imag = spec_imag[:, phonon, :].reshape(1, 1, -1, points, 1, 1)
        sigma_real = sigma_real + factor_real * mixed_real - factor_imag * mixed_imag
        sigma_imag = sigma_imag + factor_real * mixed_imag + factor_imag * mixed_real
    return (sigma_real, sigma_imag)


def inverse(sigma_real, sigma_imag, basis_low):
    points = sigma_real.shape[3]
    columns = sigma_real.shape[5]
    spectral = jnp.concatenate([sigma_real, sigma_imag], axis=-1).astype(jnp.bfloat16)
    mixture = jnp.einsum(
        "pk,aebkxw->aebpxw", basis_low, spectral, preferred_element_type=jnp.float32
    )
    cosine = mixture[:, :, :, :points]
    sine = mixture[:, :, :, points:]
    real_part = cosine[..., :columns] - sine[..., columns:]
    imag_part = cosine[..., columns:] + sine[..., :columns]
    return (jnp.concatenate([real_part, imag_part], axis=-1) * (1.0 / points)).astype(jnp.bfloat16)


def by_groups(lesser, greater, coupling, occupation, shift, region_map):
    stacked = jnp.stack([lesser, greater])
    widened = with_halo(stacked, (("grp", 1),), SMAX)
    regrouped = lax.all_to_all(widened, "mom", split_axis=4, concat_axis=3, tiled=True)
    points = regrouped.shape[3]
    basis = dft_basis(points)
    basis_low = basis.astype(jnp.bfloat16)
    spec_real, spec_imag = coupling_spectrum(coupling, region_map, basis)
    hat_real, hat_imag = forward(regrouped, basis_low)
    sigma_real, sigma_imag = combine(
        hat_real, hat_imag, spec_real, spec_imag, occupation, shift, lesser.shape[0]
    )
    result = inverse(sigma_real, sigma_imag, basis_low)
    returned = lax.all_to_all(result, "mom", split_axis=3, concat_axis=4, tiled=True)
    return (returned[0], returned[1])


def on_device(groups, shares, lesser, greater, coupling, occupation, shift, region_map):
    energies, blocks, momenta, height, columns = lesser.shape
    devices = groups * shares
    states = energies * momenta
    whole_tiles = (
        blocks == 1
        and devices >= 4
        and devices & (devices - 1) == 0
        and height % (TILE * (devices // 2)) == 0
        and TILE % states == 0
        and columns % 128 == 0
    )
    if whole_tiles:
        return by_rows(
            lesser, greater, coupling, occupation, shift, region_map, groups, shares
        )
    return by_groups(lesser, greater, coupling, occupation, shift, region_map)


def solution(mesh):
    return jax.shard_map(
        functools.partial(on_device, mesh.shape["grp"], mesh.shape["mom"]),
        mesh=mesh,
        in_specs=(
            P("grp", None, "mom", None, None),
            P("grp", None, "mom", None, None),
            P(),
            P(),
            P(),
            P(),
        ),
        out_specs=(P("grp", None, "mom", None, None), P("grp", None, "mom", None, None)),
        check_vma=False,
    )
```

```python
import functools
import math

import jax
import jax.numpy as jnp
from jax import lax
from jax.experimental import pallas as pl
from jax.experimental.pallas import tpu as pltpu
from jax.sharding import PartitionSpec as P

SMAX = 2
TILE = 16
VMEM_BYTES = 32 * 1024 * 1024
AXES = ("grp", "mom")


def turned(states, rows, back):
    size = states * rows
    down = lax.broadcasted_iota(jnp.int32, (size, size), 0)
    across = lax.broadcasted_iota(jnp.int32, (size, size), 1)
    if back:
        down, across = across, down
    bits = states.bit_length() - 1
    there = (down & (states - 1)) * rows + (down >> bits) == across
    return jnp.where(there, 1.0, 0.0).astype(jnp.bfloat16)


def mix_kernel(matrix_ref, in_ref, out_ref):
    devices, size, width = in_ref.shape
    for start in range(0, size, TILE):
        block = in_ref[:, start : start + TILE, :].reshape(devices * TILE, width)
        mixed = jnp.dot(matrix_ref[...], block, preferred_element_type=jnp.float32)
        out_ref[:, start : start + TILE, :] = mixed.astype(out_ref.dtype).reshape(
            devices, TILE, width
        )


def unpack_kernel(in_ref, lesser_ref, greater_ref, held, sent):
    pieces, rows = held.shape[1], held.shape[4]
    perm = turned(in_ref.shape[1] // rows, rows, True)
    copies = []
    for side, ref in enumerate((lesser_ref, greater_ref)):
        for piece in range(pieces):
            moved = jnp.dot(perm, in_ref[side * pieces + piece], preferred_element_type=jnp.float32)
            held[side, piece] = moved.astype(held.dtype).reshape(held.shape[2:])
            copy = pltpu.make_async_copy(
                held.at[side, piece],
                ref.at[:, 0, :, piece * rows : (piece + 1) * rows, :],
                sent.at[side, piece],
            )
            copy.start()
            copies.append(copy)
    for copy in copies:
        copy.wait()


def pack_kernel(matrix_ref, lesser_ref, greater_ref, out_ref):
    pieces, (size, width) = out_ref.shape[0] // 2, out_ref.shape[1:]
    rows = lesser_ref.shape[3] // pieces
    perm = turned(size // rows, rows, False)
    for side, ref in enumerate((lesser_ref, greater_ref)):
        for piece in range(pieces):
            block = ref[:, :, :, piece * rows : (piece + 1) * rows, :].reshape(size, width)
            moved = jnp.dot(perm, block, preferred_element_type=jnp.float32)
            out_ref[side * pieces + piece] = moved.astype(out_ref.dtype)


def build_kernel(groups, shares, momenta, energies, regions, small_ref, out_ref):
    points = shares * momenta
    states = energies * momenta
    size, levels = out_ref.shape[0], groups * energies
    modes = (small_ref.shape[0] - 3) // regions
    occupation, shift, region = (
        small_ref[at : at + 1, :] for at in range(regions * modes, regions * modes + 3)
    )
    place = lax.axis_index("grp") * shares + lax.axis_index("mom")
    greater = lax.div(place, jnp.int32(groups * shares // 2)).astype(jnp.float32)
    chosen = jnp.zeros((modes, points), jnp.float32)
    for at in range(regions):
        here = region[:, 0:1] == float(at)
        chosen = jnp.where(here, small_ref[at * modes : (at + 1) * modes, :], chosen)
    circles = {}
    for step in range(-SMAX, SMAX + 1):
        if step == 0:
            continue
        row = jnp.zeros((1, points), jnp.float32)
        for mode in range(modes):
            filling = occupation[:, mode : mode + 1] + (greater if step > 0 else 1.0 - greater)
            weight = jnp.where(shift[:, mode : mode + 1] == float(abs(step)), filling, 0.0)
            row = row + weight * chosen[mode : mode + 1, :]
        wide = jnp.broadcast_to(jnp.concatenate([row, row], axis=1), (points, 2 * points))
        circles[step] = pltpu.roll(wide, 0, 1, stride=1, stride_axis=0)[:, :points]
    nothing = jnp.zeros((points, points), jnp.float32)
    plain = jnp.concatenate(
        [
            jnp.concatenate([circles.get(out - level, nothing) for out in range(levels)], axis=1)
            for level in range(levels)
        ],
        axis=0,
    ).astype(jnp.bfloat16)

    def parts(at):
        device, row = at >> (TILE.bit_length() - 1), (at & (TILE - 1)) >> (states.bit_length() - 1)
        energy = (at & (states - 1)) >> (momenta.bit_length() - 1)
        energy = (device >> (shares.bit_length() - 1)) * energies + energy
        return row, (energy * shares + (device & (shares - 1))) * momenta + (at & (momenta - 1))

    state = parts(lax.broadcasted_iota(jnp.int32, (size, 1), 0))[1]
    pick = state == lax.broadcasted_iota(jnp.int32, (size, levels * points), 1)
    pick = jnp.where(pick, 1.0, 0.0).astype(jnp.bfloat16)
    half = jnp.dot(pick, plain, preferred_element_type=jnp.float32).astype(jnp.bfloat16)
    full = lax.dot_general(
        pick, half, (((1,), (1,)), ((), ())), preferred_element_type=jnp.float32
    )
    same = parts(lax.broadcasted_iota(jnp.int32, (size, 1), 0))[0] == parts(
        lax.broadcasted_iota(jnp.int32, (1, size), 1)
    )[0]
    out_ref[...] = jnp.where(same, full, 0.0).astype(out_ref.dtype)


def params():
    return pltpu.CompilerParams(vmem_limit_bytes=VMEM_BYTES)


VECTORS = pl.BlockSpec(memory_space=pltpu.VMEM)
SLABS = pl.BlockSpec(memory_space=pl.ANY)


def build(coupling, occupation, shift, region_map, groups, shares, momenta, energies):
    size, points = groups * shares * TILE, shares * momenta
    rows = coupling.shape[0] * coupling.shape[1]
    small = jnp.pad(coupling.reshape(rows, points), ((0, 3), (0, 0)))
    for at, part in enumerate((occupation, shift, region_map)):
        part = jnp.pad(part[None, :], ((rows + at, 2 - at), (0, points - part.shape[0])))
        small = small + part.astype(jnp.float32)
    return pl.pallas_call(
        functools.partial(build_kernel, groups, shares, momenta, energies, coupling.shape[0]),
        out_shape=jax.ShapeDtypeStruct((size, size), jnp.bfloat16),
        in_specs=[VECTORS],
        out_specs=VECTORS,
        compiler_params=params(),
        cost_estimate=pl.CostEstimate(
            flops=110 * size * size * points, bytes_accessed=22 * size * size, transcendentals=0
        ),
        name="build",
    )(small)


def pack(matrix, lesser, greater, pieces, rows):
    energies, _, momenta, _, columns = lesser.shape
    size = energies * momenta * rows
    return pl.pallas_call(
        pack_kernel,
        out_shape=jax.ShapeDtypeStruct((2 * pieces, size, columns), lesser.dtype),
        in_specs=[SLABS, VECTORS, VECTORS],
        out_specs=VECTORS,
        compiler_params=params(),
        name="pack",
    )(matrix, lesser, greater)


def unpack(packed, shape, pieces, rows):
    energies, _, momenta, _, columns = shape
    out = jax.ShapeDtypeStruct(shape, packed.dtype)
    return pl.pallas_call(
        unpack_kernel,
        out_shape=(out, out),
        in_specs=[VECTORS],
        out_specs=(SLABS, SLABS),
        scratch_shapes=[
            pltpu.VMEM((2, pieces, energies, momenta, rows, columns), packed.dtype),
            pltpu.SemaphoreType.DMA((2, pieces)),
        ],
        compiler_params=params(),
        name="unpack",
    )(packed)


def mix(matrix, received):
    return pl.pallas_call(
        mix_kernel,
        out_shape=jax.ShapeDtypeStruct(received.shape, received.dtype),
        in_specs=[VECTORS, VECTORS],
        out_specs=VECTORS,
        compiler_params=params(),
        name="mix",
    )(matrix, received)


def exchange(array):
    return lax.all_to_all(array, AXES, split_axis=0, concat_axis=0, tiled=True)


def by_rows(lesser, greater, coupling, occupation, shift, region_map, groups, shares):
    pieces = groups * shares // 2
    rows = lesser.shape[3] // pieces
    matrix = build(
        coupling, occupation, shift, region_map, groups, shares, lesser.shape[2], lesser.shape[0]
    )
    sent = pack(matrix, lesser, greater, pieces, rows)
    returned = exchange(mix(matrix, exchange(sent)))
    return unpack(returned, lesser.shape, pieces, rows)


def with_halo(shard, sides, width):
    for axis, dim in sides:
        size, length = (lax.axis_size(axis), shard.shape[dim])
        up = [(i, (i + 1) % size) for i in range(size - 1)]
        down = [(j, i) for i, j in up]
        last = lax.slice_in_dim(shard, length - width, length, axis=dim)
        first = lax.slice_in_dim(shard, 0, width, axis=dim)
        before = lax.ppermute(last, axis, up)
        after = lax.ppermute(first, axis, down)
        shard = jnp.concatenate([before, shard, after], axis=dim)
    return shard


def dft_basis(points):
    row_index = lax.broadcasted_iota(jnp.int32, (points, points), 0)
    col_index = lax.broadcasted_iota(jnp.int32, (points, points), 1)
    angles = (row_index * col_index % points).astype(jnp.float32) * (2.0 * math.pi / points)
    return jnp.concatenate([jnp.cos(angles), jnp.sin(angles)], axis=0)


def coupling_spectrum(coupling, region_map, basis):
    regions = coupling.shape[0]
    points = coupling.shape[2]
    onehot = (region_map[:, None] == jnp.arange(regions, dtype=jnp.int32)[None, :]).astype(
        jnp.float32
    )
    chosen = jnp.einsum("br,rmq->bmq", onehot, coupling, precision=lax.Precision.HIGHEST)
    spectrum = jnp.einsum("pq,bmq->bmp", basis, chosen, precision=lax.Precision.HIGHEST)
    return (spectrum[:, :, :points], -spectrum[:, :, points:])


def forward(stacked, basis_low):
    points = stacked.shape[3]
    columns = stacked.shape[5] // 2
    mixture = jnp.einsum(
        "pk,aebkxw->aebpxw", basis_low, stacked, preferred_element_type=jnp.float32
    )
    cosine = mixture[:, :, :, :points]
    sine = mixture[:, :, :, points:]
    return (
        cosine[..., :columns] + sine[..., columns:],
        cosine[..., columns:] - sine[..., :columns],
    )


def combine(hat_real, hat_imag, spec_real, spec_imag, occupation, shift, energies):
    out_shape = (2, energies) + hat_real.shape[2:]
    sigma_real = jnp.zeros(out_shape, jnp.float32)
    sigma_imag = jnp.zeros(out_shape, jnp.float32)
    points = spec_real.shape[2]
    for phonon in range(occupation.shape[0]):
        offset = shift[phonon]
        filling = occupation[phonon]
        lower_real = lax.dynamic_slice_in_dim(hat_real, SMAX - offset, energies, 1)
        lower_imag = lax.dynamic_slice_in_dim(hat_imag, SMAX - offset, energies, 1)
        upper_real = lax.dynamic_slice_in_dim(hat_real, SMAX + offset, energies, 1)
        upper_imag = lax.dynamic_slice_in_dim(hat_imag, SMAX + offset, energies, 1)
        weight_low = jnp.stack([filling, filling + 1.0]).reshape(2, 1, 1, 1, 1, 1)
        weight_high = jnp.stack([filling + 1.0, filling]).reshape(2, 1, 1, 1, 1, 1)
        mixed_real = weight_low * lower_real + weight_high * upper_real
        mixed_imag = weight_low * lower_imag + weight_high * upper_imag
        factor_real = spec_real[:, phonon, :].reshape(1, 1, -1, points, 1, 1)
        factor_imag = spec_imag[:, phonon, :].reshape(1, 1, -1, points, 1, 1)
        sigma_real = sigma_real + factor_real * mixed_real - factor_imag * mixed_imag
        sigma_imag = sigma_imag + factor_real * mixed_imag + factor_imag * mixed_real
    return (sigma_real, sigma_imag)


def inverse(sigma_real, sigma_imag, basis_low):
    points = sigma_real.shape[3]
    columns = sigma_real.shape[5]
    spectral = jnp.concatenate([sigma_real, sigma_imag], axis=-1).astype(jnp.bfloat16)
    mixture = jnp.einsum(
        "pk,aebkxw->aebpxw", basis_low, spectral, preferred_element_type=jnp.float32
    )
    cosine = mixture[:, :, :, :points]
    sine = mixture[:, :, :, points:]
    real_part = cosine[..., :columns] - sine[..., columns:]
    imag_part = cosine[..., columns:] + sine[..., :columns]
    return (jnp.concatenate([real_part, imag_part], axis=-1) * (1.0 / points)).astype(jnp.bfloat16)


def by_groups(lesser, greater, coupling, occupation, shift, region_map):
    stacked = jnp.stack([lesser, greater])
    widened = with_halo(stacked, (("grp", 1),), SMAX)
    regrouped = lax.all_to_all(widened, "mom", split_axis=4, concat_axis=3, tiled=True)
    points = regrouped.shape[3]
    basis = dft_basis(points)
    basis_low = basis.astype(jnp.bfloat16)
    spec_real, spec_imag = coupling_spectrum(coupling, region_map, basis)
    hat_real, hat_imag = forward(regrouped, basis_low)
    sigma_real, sigma_imag = combine(
        hat_real, hat_imag, spec_real, spec_imag, occupation, shift, lesser.shape[0]
    )
    result = inverse(sigma_real, sigma_imag, basis_low)
    returned = lax.all_to_all(result, "mom", split_axis=3, concat_axis=4, tiled=True)
    return (returned[0], returned[1])


def on_device(groups, shares, lesser, greater, coupling, occupation, shift, region_map):
    energies, blocks, momenta, height, columns = lesser.shape
    devices = groups * shares
    states = energies * momenta
    whole_tiles = (
        blocks == 1
        and devices >= 4
        and devices & (devices - 1) == 0
        and height % (TILE * (devices // 2)) == 0
        and TILE % states == 0
        and columns % 128 == 0
    )
    if whole_tiles:
        return by_rows(
            lesser, greater, coupling, occupation, shift, region_map, groups, shares
        )
    return by_groups(lesser, greater, coupling, occupation, shift, region_map)


def solution(mesh):
    return jax.shard_map(
        functools.partial(on_device, mesh.shape["grp"], mesh.shape["mom"]),
        mesh=mesh,
        in_specs=(
            P("grp", None, "mom", None, None),
            P("grp", None, "mom", None, None),
            P(),
            P(),
            P(),
            P(),
        ),
        out_specs=(P("grp", None, "mom", None, None), P("grp", None, "mom", None, None)),
        check_vma=False,
    )
```

```python
import functools
import math

import jax
import jax.numpy as jnp
from jax import lax
from jax.experimental import pallas as pl
from jax.experimental.pallas import tpu as pltpu
from jax.sharding import PartitionSpec as P

SMAX = 2
TILE = 16
VMEM_BYTES = 32 * 1024 * 1024
AXES = ("grp", "mom")


def turned(states, rows, back):
    size = states * rows
    down = lax.broadcasted_iota(jnp.int32, (size, size), 0)
    across = lax.broadcasted_iota(jnp.int32, (size, size), 1)
    if back:
        down, across = across, down
    bits = states.bit_length() - 1
    there = (down & (states - 1)) * rows + (down >> bits) == across
    return jnp.where(there, 1.0, 0.0).astype(jnp.bfloat16)


def mix_kernel(matrix_ref, in_ref, out_ref):
    devices, size, width = in_ref.shape
    states = matrix_ref.shape[0] // devices
    for start in range(0, size, states):
        block = in_ref[:, start : start + states, :].reshape(devices * states, width)
        mixed = jnp.dot(matrix_ref[...], block, preferred_element_type=jnp.float32)
        out_ref[:, start : start + states, :] = mixed.astype(out_ref.dtype).reshape(
            devices, states, width
        )


def unpack_kernel(in_ref, lesser_ref, greater_ref, held, sent):
    pieces, rows = held.shape[1], held.shape[4]
    perm = turned(in_ref.shape[1] // rows, rows, True)
    copies = []
    for side, ref in enumerate((lesser_ref, greater_ref)):
        for piece in range(pieces):
            moved = jnp.dot(perm, in_ref[side * pieces + piece], preferred_element_type=jnp.float32)
            held[side, piece] = moved.astype(held.dtype).reshape(held.shape[2:])
            copy = pltpu.make_async_copy(
                held.at[side, piece],
                ref.at[:, 0, :, piece * rows : (piece + 1) * rows, :],
                sent.at[side, piece],
            )
            copy.start()
            copies.append(copy)
    for copy in copies:
        copy.wait()


def pack_kernel(matrix_ref, lesser_ref, greater_ref, out_ref):
    pieces, (size, width) = out_ref.shape[0] // 2, out_ref.shape[1:]
    rows = lesser_ref.shape[3] // pieces
    perm = turned(size // rows, rows, False)
    for side, ref in enumerate((lesser_ref, greater_ref)):
        for piece in range(pieces):
            block = ref[:, :, :, piece * rows : (piece + 1) * rows, :].reshape(size, width)
            moved = jnp.dot(perm, block, preferred_element_type=jnp.float32)
            out_ref[side * pieces + piece] = moved.astype(out_ref.dtype)


def build_kernel(groups, shares, momenta, energies, regions, small_ref, out_ref):
    points = shares * momenta
    states = energies * momenta
    size, levels = out_ref.shape[0], groups * energies
    modes = (small_ref.shape[0] - 3) // regions
    occupation, shift, region = (
        small_ref[at : at + 1, :] for at in range(regions * modes, regions * modes + 3)
    )
    place = lax.axis_index("grp") * shares + lax.axis_index("mom")
    greater = lax.div(place, jnp.int32(groups * shares // 2)).astype(jnp.float32)
    chosen = jnp.zeros((modes, points), jnp.float32)
    for at in range(regions):
        here = region[:, 0:1] == float(at)
        chosen = jnp.where(here, small_ref[at * modes : (at + 1) * modes, :], chosen)
    circles = {}
    for step in range(-SMAX, SMAX + 1):
        if step == 0:
            continue
        row = jnp.zeros((1, points), jnp.float32)
        for mode in range(modes):
            filling = occupation[:, mode : mode + 1] + (greater if step > 0 else 1.0 - greater)
            weight = jnp.where(shift[:, mode : mode + 1] == float(abs(step)), filling, 0.0)
            row = row + weight * chosen[mode : mode + 1, :]
        wide = jnp.broadcast_to(jnp.concatenate([row, row], axis=1), (points, 2 * points))
        circles[step] = pltpu.roll(wide, 0, 1, stride=1, stride_axis=0)[:, :points]
    nothing = jnp.zeros((points, points), jnp.float32)
    plain = jnp.concatenate(
        [
            jnp.concatenate([circles.get(out - level, nothing) for out in range(levels)], axis=1)
            for level in range(levels)
        ],
        axis=0,
    ).astype(jnp.bfloat16)

    at = lax.broadcasted_iota(jnp.int32, (size, 1), 0)
    device, energy = at >> (states.bit_length() - 1), (at & (states - 1)) >> (momenta.bit_length() - 1)
    energy = (device >> (shares.bit_length() - 1)) * energies + energy
    state = (energy * shares + (device & (shares - 1))) * momenta + (at & (momenta - 1))
    pick = state == lax.broadcasted_iota(jnp.int32, (size, levels * points), 1)
    pick = jnp.where(pick, 1.0, 0.0).astype(jnp.bfloat16)
    half = jnp.dot(pick, plain, preferred_element_type=jnp.float32).astype(jnp.bfloat16)
    full = lax.dot_general(
        pick, half, (((1,), (1,)), ((), ())), preferred_element_type=jnp.float32
    )
    out_ref[...] = full.astype(out_ref.dtype)


def params():
    return pltpu.CompilerParams(vmem_limit_bytes=VMEM_BYTES)


VECTORS = pl.BlockSpec(memory_space=pltpu.VMEM)
SLABS = pl.BlockSpec(memory_space=pl.ANY)


def build(coupling, occupation, shift, region_map, groups, shares, momenta, energies):
    size, points = groups * shares * energies * momenta, shares * momenta
    rows = coupling.shape[0] * coupling.shape[1]
    small = jnp.pad(coupling.reshape(rows, points), ((0, 3), (0, 0)))
    for at, part in enumerate((occupation, shift, region_map)):
        part = jnp.pad(part[None, :], ((rows + at, 2 - at), (0, points - part.shape[0])))
        small = small + part.astype(jnp.float32)
    return pl.pallas_call(
        functools.partial(build_kernel, groups, shares, momenta, energies, coupling.shape[0]),
        out_shape=jax.ShapeDtypeStruct((size, size), jnp.bfloat16),
        in_specs=[VECTORS],
        out_specs=VECTORS,
        compiler_params=params(),
        cost_estimate=pl.CostEstimate(
            flops=440 * size * size * points, bytes_accessed=88 * size * size, transcendentals=0
        ),
        name="build",
    )(small)


def pack(matrix, lesser, greater, pieces, rows):
    energies, _, momenta, _, columns = lesser.shape
    size = energies * momenta * rows
    return pl.pallas_call(
        pack_kernel,
        out_shape=jax.ShapeDtypeStruct((2 * pieces, size, columns), lesser.dtype),
        in_specs=[SLABS, VECTORS, VECTORS],
        out_specs=VECTORS,
        compiler_params=params(),
        name="pack",
    )(matrix, lesser, greater)


def unpack(packed, shape, pieces, rows):
    energies, _, momenta, _, columns = shape
    out = jax.ShapeDtypeStruct(shape, packed.dtype)
    return pl.pallas_call(
        unpack_kernel,
        out_shape=(out, out),
        in_specs=[VECTORS],
        out_specs=(SLABS, SLABS),
        scratch_shapes=[
            pltpu.VMEM((2, pieces, energies, momenta, rows, columns), packed.dtype),
            pltpu.SemaphoreType.DMA((2, pieces)),
        ],
        compiler_params=params(),
        name="unpack",
    )(packed)


def mix(matrix, received):
    return pl.pallas_call(
        mix_kernel,
        out_shape=jax.ShapeDtypeStruct(received.shape, received.dtype),
        in_specs=[VECTORS, VECTORS],
        out_specs=VECTORS,
        compiler_params=params(),
        name="mix",
    )(matrix, received)


def exchange(array):
    return lax.all_to_all(array, AXES, split_axis=0, concat_axis=0, tiled=True)


def by_rows(lesser, greater, coupling, occupation, shift, region_map, groups, shares):
    pieces = groups * shares // 2
    rows = lesser.shape[3] // pieces
    matrix = build(
        coupling, occupation, shift, region_map, groups, shares, lesser.shape[2], lesser.shape[0]
    )
    sent = pack(matrix, lesser, greater, pieces, rows)
    returned = exchange(mix(matrix, exchange(sent)))
    return unpack(returned, lesser.shape, pieces, rows)


def with_halo(shard, sides, width):
    for axis, dim in sides:
        size, length = (lax.axis_size(axis), shard.shape[dim])
        up = [(i, (i + 1) % size) for i in range(size - 1)]
        down = [(j, i) for i, j in up]
        last = lax.slice_in_dim(shard, length - width, length, axis=dim)
        first = lax.slice_in_dim(shard, 0, width, axis=dim)
        before = lax.ppermute(last, axis, up)
        after = lax.ppermute(first, axis, down)
        shard = jnp.concatenate([before, shard, after], axis=dim)
    return shard


def dft_basis(points):
    row_index = lax.broadcasted_iota(jnp.int32, (points, points), 0)
    col_index = lax.broadcasted_iota(jnp.int32, (points, points), 1)
    angles = (row_index * col_index % points).astype(jnp.float32) * (2.0 * math.pi / points)
    return jnp.concatenate([jnp.cos(angles), jnp.sin(angles)], axis=0)


def coupling_spectrum(coupling, region_map, basis):
    regions = coupling.shape[0]
    points = coupling.shape[2]
    onehot = (region_map[:, None] == jnp.arange(regions, dtype=jnp.int32)[None, :]).astype(
        jnp.float32
    )
    chosen = jnp.einsum("br,rmq->bmq", onehot, coupling, precision=lax.Precision.HIGHEST)
    spectrum = jnp.einsum("pq,bmq->bmp", basis, chosen, precision=lax.Precision.HIGHEST)
    return (spectrum[:, :, :points], -spectrum[:, :, points:])


def forward(stacked, basis_low):
    points = stacked.shape[3]
    columns = stacked.shape[5] // 2
    mixture = jnp.einsum(
        "pk,aebkxw->aebpxw", basis_low, stacked, preferred_element_type=jnp.float32
    )
    cosine = mixture[:, :, :, :points]
    sine = mixture[:, :, :, points:]
    return (
        cosine[..., :columns] + sine[..., columns:],
        cosine[..., columns:] - sine[..., :columns],
    )


def combine(hat_real, hat_imag, spec_real, spec_imag, occupation, shift, energies):
    out_shape = (2, energies) + hat_real.shape[2:]
    sigma_real = jnp.zeros(out_shape, jnp.float32)
    sigma_imag = jnp.zeros(out_shape, jnp.float32)
    points = spec_real.shape[2]
    for phonon in range(occupation.shape[0]):
        offset = shift[phonon]
        filling = occupation[phonon]
        lower_real = lax.dynamic_slice_in_dim(hat_real, SMAX - offset, energies, 1)
        lower_imag = lax.dynamic_slice_in_dim(hat_imag, SMAX - offset, energies, 1)
        upper_real = lax.dynamic_slice_in_dim(hat_real, SMAX + offset, energies, 1)
        upper_imag = lax.dynamic_slice_in_dim(hat_imag, SMAX + offset, energies, 1)
        weight_low = jnp.stack([filling, filling + 1.0]).reshape(2, 1, 1, 1, 1, 1)
        weight_high = jnp.stack([filling + 1.0, filling]).reshape(2, 1, 1, 1, 1, 1)
        mixed_real = weight_low * lower_real + weight_high * upper_real
        mixed_imag = weight_low * lower_imag + weight_high * upper_imag
        factor_real = spec_real[:, phonon, :].reshape(1, 1, -1, points, 1, 1)
        factor_imag = spec_imag[:, phonon, :].reshape(1, 1, -1, points, 1, 1)
        sigma_real = sigma_real + factor_real * mixed_real - factor_imag * mixed_imag
        sigma_imag = sigma_imag + factor_real * mixed_imag + factor_imag * mixed_real
    return (sigma_real, sigma_imag)


def inverse(sigma_real, sigma_imag, basis_low):
    points = sigma_real.shape[3]
    columns = sigma_real.shape[5]
    spectral = jnp.concatenate([sigma_real, sigma_imag], axis=-1).astype(jnp.bfloat16)
    mixture = jnp.einsum(
        "pk,aebkxw->aebpxw", basis_low, spectral, preferred_element_type=jnp.float32
    )
    cosine = mixture[:, :, :, :points]
    sine = mixture[:, :, :, points:]
    real_part = cosine[..., :columns] - sine[..., columns:]
    imag_part = cosine[..., columns:] + sine[..., :columns]
    return (jnp.concatenate([real_part, imag_part], axis=-1) * (1.0 / points)).astype(jnp.bfloat16)


def by_groups(lesser, greater, coupling, occupation, shift, region_map):
    stacked = jnp.stack([lesser, greater])
    widened = with_halo(stacked, (("grp", 1),), SMAX)
    regrouped = lax.all_to_all(widened, "mom", split_axis=4, concat_axis=3, tiled=True)
    points = regrouped.shape[3]
    basis = dft_basis(points)
    basis_low = basis.astype(jnp.bfloat16)
    spec_real, spec_imag = coupling_spectrum(coupling, region_map, basis)
    hat_real, hat_imag = forward(regrouped, basis_low)
    sigma_real, sigma_imag = combine(
        hat_real, hat_imag, spec_real, spec_imag, occupation, shift, lesser.shape[0]
    )
    result = inverse(sigma_real, sigma_imag, basis_low)
    returned = lax.all_to_all(result, "mom", split_axis=3, concat_axis=4, tiled=True)
    return (returned[0], returned[1])


def on_device(groups, shares, lesser, greater, coupling, occupation, shift, region_map):
    energies, blocks, momenta, height, columns = lesser.shape
    devices = groups * shares
    states = energies * momenta
    whole_tiles = (
        blocks == 1
        and devices >= 4
        and devices & (devices - 1) == 0
        and height % (TILE * (devices // 2)) == 0
        and TILE % states == 0
        and columns % 128 == 0
    )
    if whole_tiles:
        return by_rows(
            lesser, greater, coupling, occupation, shift, region_map, groups, shares
        )
    return by_groups(lesser, greater, coupling, occupation, shift, region_map)


def solution(mesh):
    return jax.shard_map(
        functools.partial(on_device, mesh.shape["grp"], mesh.shape["mom"]),
        mesh=mesh,
        in_specs=(
            P("grp", None, "mom", None, None),
            P("grp", None, "mom", None, None),
            P(),
            P(),
            P(),
            P(),
        ),
        out_specs=(P("grp", None, "mom", None, None), P("grp", None, "mom", None, None)),
        check_vma=False,
    )
```

```python
import functools
import math

import jax
import jax.numpy as jnp
from jax import lax
from jax.experimental import pallas as pl
from jax.experimental.pallas import tpu as pltpu
from jax.sharding import PartitionSpec as P

SMAX = 2
TILE = 16
VMEM_BYTES = 32 * 1024 * 1024
AXES = ("grp", "mom")


def turned(states, rows, back):
    size = states * rows
    down = lax.broadcasted_iota(jnp.int32, (size, size), 0)
    across = lax.broadcasted_iota(jnp.int32, (size, size), 1)
    if back:
        down, across = across, down
    bits = states.bit_length() - 1
    there = (down & (states - 1)) * rows + (down >> bits) == across
    return jnp.where(there, 1.0, 0.0).astype(jnp.bfloat16)


def mix_kernel(matrix_ref, in_ref, out_ref):
    devices, size, width = in_ref.shape
    states = matrix_ref.shape[0] // devices
    for start in range(0, size, states):
        block = in_ref[:, start : start + states, :].reshape(devices * states, width)
        mixed = jnp.dot(matrix_ref[...], block, preferred_element_type=jnp.float32)
        out_ref[:, start : start + states, :] = mixed.astype(out_ref.dtype).reshape(
            devices, states, width
        )


def unpack_kernel(in_ref, lesser_ref, greater_ref, held, sent):
    pieces, steps = in_ref.shape[0] // 2, sent.shape[1]
    rows = held.shape[3] // pieces
    batch = pieces // steps
    perm = turned(in_ref.shape[1] // rows, rows, True)
    copies = []
    for step in range(steps):
        span = slice(step * batch * rows, (step + 1) * batch * rows)
        for side, ref in enumerate((lesser_ref, greater_ref)):
            for piece in range(step * batch, (step + 1) * batch):
                moved = jnp.dot(
                    perm, in_ref[side * pieces + piece], preferred_element_type=jnp.float32
                )
                held[side, :, :, piece * rows : (piece + 1) * rows, :] = moved.astype(
                    held.dtype
                ).reshape(held.shape[1:3] + (rows, held.shape[4]))
            copy = pltpu.make_async_copy(
                held.at[side, :, :, span, :], ref.at[:, 0, :, span, :], sent.at[side, step]
            )
            copy.start()
            copies.append(copy)
    for copy in copies:
        copy.wait()


def pack_kernel(matrix_ref, lesser_ref, greater_ref, out_ref):
    pieces, (size, width) = out_ref.shape[0] // 2, out_ref.shape[1:]
    rows = lesser_ref.shape[3] // pieces
    perm = turned(size // rows, rows, False)
    for side, ref in enumerate((lesser_ref, greater_ref)):
        for piece in range(pieces):
            block = ref[:, :, :, piece * rows : (piece + 1) * rows, :].reshape(size, width)
            moved = jnp.dot(perm, block, preferred_element_type=jnp.float32)
            out_ref[side * pieces + piece] = moved.astype(out_ref.dtype)


def build_kernel(groups, shares, momenta, energies, regions, small_ref, out_ref):
    points = shares * momenta
    states = energies * momenta
    size, levels = out_ref.shape[0], groups * energies
    modes = (small_ref.shape[0] - 3) // regions
    occupation, shift, region = (
        small_ref[at : at + 1, :] for at in range(regions * modes, regions * modes + 3)
    )
    place = lax.axis_index("grp") * shares + lax.axis_index("mom")
    greater = lax.div(place, jnp.int32(groups * shares // 2)).astype(jnp.float32)
    chosen = jnp.zeros((modes, points), jnp.float32)
    for at in range(regions):
        here = region[:, 0:1] == float(at)
        chosen = jnp.where(here, small_ref[at * modes : (at + 1) * modes, :], chosen)
    circles = {}
    for step in range(-SMAX, SMAX + 1):
        if step == 0:
            continue
        row = jnp.zeros((1, points), jnp.float32)
        for mode in range(modes):
            filling = occupation[:, mode : mode + 1] + (greater if step > 0 else 1.0 - greater)
            weight = jnp.where(shift[:, mode : mode + 1] == float(abs(step)), filling, 0.0)
            row = row + weight * chosen[mode : mode + 1, :]
        wide = jnp.broadcast_to(jnp.concatenate([row, row], axis=1), (points, 2 * points))
        circles[step] = pltpu.roll(wide, 0, 1, stride=1, stride_axis=0)[:, :points]
    nothing = jnp.zeros((points, points), jnp.float32)
    plain = jnp.concatenate(
        [
            jnp.concatenate([circles.get(out - level, nothing) for out in range(levels)], axis=1)
            for level in range(levels)
        ],
        axis=0,
    ).astype(jnp.bfloat16)

    at = lax.broadcasted_iota(jnp.int32, (size, 1), 0)
    device, energy = at >> (states.bit_length() - 1), (at & (states - 1)) >> (momenta.bit_length() - 1)
    energy = (device >> (shares.bit_length() - 1)) * energies + energy
    state = (energy * shares + (device & (shares - 1))) * momenta + (at & (momenta - 1))
    pick = state == lax.broadcasted_iota(jnp.int32, (size, levels * points), 1)
    pick = jnp.where(pick, 1.0, 0.0).astype(jnp.bfloat16)
    half = jnp.dot(pick, plain, preferred_element_type=jnp.float32).astype(jnp.bfloat16)
    full = lax.dot_general(
        pick, half, (((1,), (1,)), ((), ())), preferred_element_type=jnp.float32
    )
    out_ref[...] = full.astype(out_ref.dtype)


def params():
    return pltpu.CompilerParams(vmem_limit_bytes=VMEM_BYTES)


VECTORS = pl.BlockSpec(memory_space=pltpu.VMEM)
SLABS = pl.BlockSpec(memory_space=pl.ANY)


def build(coupling, occupation, shift, region_map, groups, shares, momenta, energies):
    size, points = groups * shares * energies * momenta, shares * momenta
    rows = coupling.shape[0] * coupling.shape[1]
    small = jnp.pad(coupling.reshape(rows, points), ((0, 3), (0, 0)))
    for at, part in enumerate((occupation, shift, region_map)):
        part = jnp.pad(part[None, :], ((rows + at, 2 - at), (0, points - part.shape[0])))
        small = small + part.astype(jnp.float32)
    return pl.pallas_call(
        functools.partial(build_kernel, groups, shares, momenta, energies, coupling.shape[0]),
        out_shape=jax.ShapeDtypeStruct((size, size), jnp.bfloat16),
        in_specs=[VECTORS],
        out_specs=VECTORS,
        compiler_params=params(),
        cost_estimate=pl.CostEstimate(
            flops=440 * size * size * points, bytes_accessed=88 * size * size, transcendentals=0
        ),
        name="build",
    )(small)


def pack(matrix, lesser, greater, pieces, rows):
    energies, _, momenta, _, columns = lesser.shape
    size = energies * momenta * rows
    return pl.pallas_call(
        pack_kernel,
        out_shape=jax.ShapeDtypeStruct((2 * pieces, size, columns), lesser.dtype),
        in_specs=[SLABS, VECTORS, VECTORS],
        out_specs=VECTORS,
        compiler_params=params(),
        name="pack",
    )(matrix, lesser, greater)


def unpack(packed, shape, pieces, rows):
    energies, _, momenta, _, columns = shape
    out = jax.ShapeDtypeStruct(shape, packed.dtype)
    return pl.pallas_call(
        unpack_kernel,
        out_shape=(out, out),
        in_specs=[VECTORS],
        out_specs=(SLABS, SLABS),
        scratch_shapes=[
            pltpu.VMEM((2, energies, momenta, pieces * rows, columns), packed.dtype),
            pltpu.SemaphoreType.DMA((2, math.gcd(pieces, 4))),
        ],
        compiler_params=params(),
        name="unpack",
    )(packed)


def mix(matrix, received):
    return pl.pallas_call(
        mix_kernel,
        out_shape=jax.ShapeDtypeStruct(received.shape, received.dtype),
        in_specs=[VECTORS, VECTORS],
        out_specs=VECTORS,
        compiler_params=params(),
        name="mix",
    )(matrix, received)


def exchange(array):
    return lax.all_to_all(array, AXES, split_axis=0, concat_axis=0, tiled=True)


def by_rows(lesser, greater, coupling, occupation, shift, region_map, groups, shares):
    pieces = groups * shares // 2
    rows = lesser.shape[3] // pieces
    matrix = build(
        coupling, occupation, shift, region_map, groups, shares, lesser.shape[2], lesser.shape[0]
    )
    sent = pack(matrix, lesser, greater, pieces, rows)
    returned = exchange(mix(matrix, exchange(sent)))
    return unpack(returned, lesser.shape, pieces, rows)


def with_halo(shard, sides, width):
    for axis, dim in sides:
        size, length = (lax.axis_size(axis), shard.shape[dim])
        up = [(i, (i + 1) % size) for i in range(size - 1)]
        down = [(j, i) for i, j in up]
        last = lax.slice_in_dim(shard, length - width, length, axis=dim)
        first = lax.slice_in_dim(shard, 0, width, axis=dim)
        before = lax.ppermute(last, axis, up)
        after = lax.ppermute(first, axis, down)
        shard = jnp.concatenate([before, shard, after], axis=dim)
    return shard


def dft_basis(points):
    row_index = lax.broadcasted_iota(jnp.int32, (points, points), 0)
    col_index = lax.broadcasted_iota(jnp.int32, (points, points), 1)
    angles = (row_index * col_index % points).astype(jnp.float32) * (2.0 * math.pi / points)
    return jnp.concatenate([jnp.cos(angles), jnp.sin(angles)], axis=0)


def coupling_spectrum(coupling, region_map, basis):
    regions = coupling.shape[0]
    points = coupling.shape[2]
    onehot = (region_map[:, None] == jnp.arange(regions, dtype=jnp.int32)[None, :]).astype(
        jnp.float32
    )
    chosen = jnp.einsum("br,rmq->bmq", onehot, coupling, precision=lax.Precision.HIGHEST)
    spectrum = jnp.einsum("pq,bmq->bmp", basis, chosen, precision=lax.Precision.HIGHEST)
    return (spectrum[:, :, :points], -spectrum[:, :, points:])


def forward(stacked, basis_low):
    points = stacked.shape[3]
    columns = stacked.shape[5] // 2
    mixture = jnp.einsum(
        "pk,aebkxw->aebpxw", basis_low, stacked, preferred_element_type=jnp.float32
    )
    cosine = mixture[:, :, :, :points]
    sine = mixture[:, :, :, points:]
    return (
        cosine[..., :columns] + sine[..., columns:],
        cosine[..., columns:] - sine[..., :columns],
    )


def combine(hat_real, hat_imag, spec_real, spec_imag, occupation, shift, energies):
    out_shape = (2, energies) + hat_real.shape[2:]
    sigma_real = jnp.zeros(out_shape, jnp.float32)
    sigma_imag = jnp.zeros(out_shape, jnp.float32)
    points = spec_real.shape[2]
    for phonon in range(occupation.shape[0]):
        offset = shift[phonon]
        filling = occupation[phonon]
        lower_real = lax.dynamic_slice_in_dim(hat_real, SMAX - offset, energies, 1)
        lower_imag = lax.dynamic_slice_in_dim(hat_imag, SMAX - offset, energies, 1)
        upper_real = lax.dynamic_slice_in_dim(hat_real, SMAX + offset, energies, 1)
        upper_imag = lax.dynamic_slice_in_dim(hat_imag, SMAX + offset, energies, 1)
        weight_low = jnp.stack([filling, filling + 1.0]).reshape(2, 1, 1, 1, 1, 1)
        weight_high = jnp.stack([filling + 1.0, filling]).reshape(2, 1, 1, 1, 1, 1)
        mixed_real = weight_low * lower_real + weight_high * upper_real
        mixed_imag = weight_low * lower_imag + weight_high * upper_imag
        factor_real = spec_real[:, phonon, :].reshape(1, 1, -1, points, 1, 1)
        factor_imag = spec_imag[:, phonon, :].reshape(1, 1, -1, points, 1, 1)
        sigma_real = sigma_real + factor_real * mixed_real - factor_imag * mixed_imag
        sigma_imag = sigma_imag + factor_real * mixed_imag + factor_imag * mixed_real
    return (sigma_real, sigma_imag)


def inverse(sigma_real, sigma_imag, basis_low):
    points = sigma_real.shape[3]
    columns = sigma_real.shape[5]
    spectral = jnp.concatenate([sigma_real, sigma_imag], axis=-1).astype(jnp.bfloat16)
    mixture = jnp.einsum(
        "pk,aebkxw->aebpxw", basis_low, spectral, preferred_element_type=jnp.float32
    )
    cosine = mixture[:, :, :, :points]
    sine = mixture[:, :, :, points:]
    real_part = cosine[..., :columns] - sine[..., columns:]
    imag_part = cosine[..., columns:] + sine[..., :columns]
    return (jnp.concatenate([real_part, imag_part], axis=-1) * (1.0 / points)).astype(jnp.bfloat16)


def by_groups(lesser, greater, coupling, occupation, shift, region_map):
    stacked = jnp.stack([lesser, greater])
    widened = with_halo(stacked, (("grp", 1),), SMAX)
    regrouped = lax.all_to_all(widened, "mom", split_axis=4, concat_axis=3, tiled=True)
    points = regrouped.shape[3]
    basis = dft_basis(points)
    basis_low = basis.astype(jnp.bfloat16)
    spec_real, spec_imag = coupling_spectrum(coupling, region_map, basis)
    hat_real, hat_imag = forward(regrouped, basis_low)
    sigma_real, sigma_imag = combine(
        hat_real, hat_imag, spec_real, spec_imag, occupation, shift, lesser.shape[0]
    )
    result = inverse(sigma_real, sigma_imag, basis_low)
    returned = lax.all_to_all(result, "mom", split_axis=3, concat_axis=4, tiled=True)
    return (returned[0], returned[1])


def on_device(groups, shares, lesser, greater, coupling, occupation, shift, region_map):
    energies, blocks, momenta, height, columns = lesser.shape
    devices = groups * shares
    states = energies * momenta
    whole_tiles = (
        blocks == 1
        and devices >= 4
        and devices & (devices - 1) == 0
        and height % (TILE * (devices // 2)) == 0
        and TILE % states == 0
        and columns % 128 == 0
    )
    if whole_tiles:
        return by_rows(
            lesser, greater, coupling, occupation, shift, region_map, groups, shares
        )
    return by_groups(lesser, greater, coupling, occupation, shift, region_map)


def solution(mesh):
    return jax.shard_map(
        functools.partial(on_device, mesh.shape["grp"], mesh.shape["mom"]),
        mesh=mesh,
        in_specs=(
            P("grp", None, "mom", None, None),
            P("grp", None, "mom", None, None),
            P(),
            P(),
            P(),
            P(),
        ),
        out_specs=(P("grp", None, "mom", None, None), P("grp", None, "mom", None, None)),
        check_vma=False,
    )
```

```python
import functools
import math

import jax
import jax.numpy as jnp
from jax import lax
from jax.experimental import pallas as pl
from jax.experimental.pallas import tpu as pltpu
from jax.sharding import PartitionSpec as P

SMAX = 2
TILE = 16
VMEM_BYTES = 32 * 1024 * 1024
AXES = ("grp", "mom")


def turned(states, rows, pairs, back):
    piece = states * rows
    down = lax.broadcasted_iota(jnp.int32, (pairs * piece, pairs * piece), 0)
    across = lax.broadcasted_iota(jnp.int32, (pairs * piece, pairs * piece), 1)
    if back:
        down, across = across, down
    bits = states.bit_length() - 1
    inside = down & (piece - 1)
    there = (inside & (states - 1)) * rows + (inside >> bits) + (down - inside) == across
    return jnp.where(there, 1.0, 0.0).astype(jnp.bfloat16)


def mix_kernel(matrix_ref, in_ref, out_ref):
    devices, size, width = in_ref.shape
    states = matrix_ref.shape[0] // devices
    for start in range(0, size, states):
        block = in_ref[:, start : start + states, :].reshape(devices * states, width)
        mixed = jnp.dot(matrix_ref[...], block, preferred_element_type=jnp.float32)
        out_ref[:, start : start + states, :] = mixed.astype(out_ref.dtype).reshape(
            devices, states, width
        )


def unpack_kernel(in_ref, lesser_ref, greater_ref, held, sent):
    pieces, steps = in_ref.shape[0] // 2, sent.shape[1]
    rows = held.shape[3] // pieces
    batch = pieces // steps
    perm = turned(in_ref.shape[1] // rows, rows, 2, True)
    size, width = in_ref.shape[1:]
    copies = []
    for step in range(steps):
        span = slice(step * batch * rows, (step + 1) * batch * rows)
        for side, ref in enumerate((lesser_ref, greater_ref)):
            for piece in range(step * batch, (step + 1) * batch, 2):
                at = side * pieces + piece
                pair = in_ref[at : at + 2].reshape(2 * size, width)
                moved = jnp.dot(perm, pair, preferred_element_type=jnp.float32).astype(held.dtype)
                for turn in range(2):
                    begin = (piece + turn) * rows
                    held[side, :, :, begin : begin + rows, :] = moved[
                        turn * size : (turn + 1) * size
                    ].reshape(held.shape[1:3] + (rows, width))
            copy = pltpu.make_async_copy(
                held.at[side, :, :, span, :], ref.at[:, 0, :, span, :], sent.at[side, step]
            )
            copy.start()
            copies.append(copy)
    for copy in copies:
        copy.wait()


def pack_kernel(matrix_ref, lesser_ref, greater_ref, out_ref):
    pieces, (size, width) = out_ref.shape[0] // 2, out_ref.shape[1:]
    rows = lesser_ref.shape[3] // pieces
    perm = turned(size // rows, rows, 2, False)
    for side, ref in enumerate((lesser_ref, greater_ref)):
        for piece in range(0, pieces, 2):
            pair = [
                ref[:, :, :, at * rows : (at + 1) * rows, :].reshape(size, width)
                for at in (piece, piece + 1)
            ]
            moved = jnp.dot(
                perm, jnp.concatenate(pair, axis=0), preferred_element_type=jnp.float32
            )
            at = side * pieces + piece
            out_ref[at : at + 2] = moved.astype(out_ref.dtype).reshape(2, size, width)


def build_kernel(groups, shares, momenta, energies, regions, small_ref, out_ref):
    points = shares * momenta
    states = energies * momenta
    size, levels = out_ref.shape[0], groups * energies
    modes = (small_ref.shape[0] - 3) // regions
    occupation, shift, region = (
        small_ref[at : at + 1, :] for at in range(regions * modes, regions * modes + 3)
    )
    place = lax.axis_index("grp") * shares + lax.axis_index("mom")
    greater = lax.div(place, jnp.int32(groups * shares // 2)).astype(jnp.float32)
    chosen = jnp.zeros((modes, points), jnp.float32)
    for at in range(regions):
        here = region[:, 0:1] == float(at)
        chosen = jnp.where(here, small_ref[at * modes : (at + 1) * modes, :], chosen)
    circles = {}
    for step in range(-SMAX, SMAX + 1):
        if step == 0:
            continue
        row = jnp.zeros((1, points), jnp.float32)
        for mode in range(modes):
            filling = occupation[:, mode : mode + 1] + (greater if step > 0 else 1.0 - greater)
            weight = jnp.where(shift[:, mode : mode + 1] == float(abs(step)), filling, 0.0)
            row = row + weight * chosen[mode : mode + 1, :]
        wide = jnp.broadcast_to(jnp.concatenate([row, row], axis=1), (points, 2 * points))
        circles[step] = pltpu.roll(wide, 0, 1, stride=1, stride_axis=0)[:, :points]
    nothing = jnp.zeros((points, points), jnp.float32)
    plain = jnp.concatenate(
        [
            jnp.concatenate([circles.get(out - level, nothing) for out in range(levels)], axis=1)
            for level in range(levels)
        ],
        axis=0,
    ).astype(jnp.bfloat16)

    at = lax.broadcasted_iota(jnp.int32, (size, 1), 0)
    device, energy = at >> (states.bit_length() - 1), (at & (states - 1)) >> (momenta.bit_length() - 1)
    energy = (device >> (shares.bit_length() - 1)) * energies + energy
    state = (energy * shares + (device & (shares - 1))) * momenta + (at & (momenta - 1))
    pick = state == lax.broadcasted_iota(jnp.int32, (size, levels * points), 1)
    pick = jnp.where(pick, 1.0, 0.0).astype(jnp.bfloat16)
    half = jnp.dot(pick, plain, preferred_element_type=jnp.float32).astype(jnp.bfloat16)
    full = lax.dot_general(
        pick, half, (((1,), (1,)), ((), ())), preferred_element_type=jnp.float32
    )
    out_ref[...] = full.astype(out_ref.dtype)


def params():
    return pltpu.CompilerParams(vmem_limit_bytes=VMEM_BYTES)


VECTORS = pl.BlockSpec(memory_space=pltpu.VMEM)
SLABS = pl.BlockSpec(memory_space=pl.ANY)


def build(coupling, occupation, shift, region_map, groups, shares, momenta, energies):
    size, points = groups * shares * energies * momenta, shares * momenta
    rows = coupling.shape[0] * coupling.shape[1]
    small = jnp.pad(coupling.reshape(rows, points), ((0, 3), (0, 0)))
    for at, part in enumerate((occupation, shift, region_map)):
        part = jnp.pad(part[None, :], ((rows + at, 2 - at), (0, points - part.shape[0])))
        small = small + part.astype(jnp.float32)
    return pl.pallas_call(
        functools.partial(build_kernel, groups, shares, momenta, energies, coupling.shape[0]),
        out_shape=jax.ShapeDtypeStruct((size, size), jnp.bfloat16),
        in_specs=[VECTORS],
        out_specs=VECTORS,
        compiler_params=params(),
        cost_estimate=pl.CostEstimate(
            flops=440 * size * size * points, bytes_accessed=88 * size * size, transcendentals=0
        ),
        name="build",
    )(small)


def pack(matrix, lesser, greater, pieces, rows):
    energies, _, momenta, _, columns = lesser.shape
    size = energies * momenta * rows
    return pl.pallas_call(
        pack_kernel,
        out_shape=jax.ShapeDtypeStruct((2 * pieces, size, columns), lesser.dtype),
        in_specs=[SLABS, VECTORS, VECTORS],
        out_specs=VECTORS,
        compiler_params=params(),
        name="pack",
    )(matrix, lesser, greater)


def unpack(packed, shape, pieces, rows):
    energies, _, momenta, _, columns = shape
    out = jax.ShapeDtypeStruct(shape, packed.dtype)
    return pl.pallas_call(
        unpack_kernel,
        out_shape=(out, out),
        in_specs=[VECTORS],
        out_specs=(SLABS, SLABS),
        scratch_shapes=[
            pltpu.VMEM((2, energies, momenta, pieces * rows, columns), packed.dtype),
            pltpu.SemaphoreType.DMA((2, math.gcd(pieces, 4))),
        ],
        compiler_params=params(),
        name="unpack",
    )(packed)


def mix(matrix, received):
    return pl.pallas_call(
        mix_kernel,
        out_shape=jax.ShapeDtypeStruct(received.shape, received.dtype),
        in_specs=[VECTORS, VECTORS],
        out_specs=VECTORS,
        compiler_params=params(),
        name="mix",
    )(matrix, received)


def exchange(array):
    return lax.all_to_all(array, AXES, split_axis=0, concat_axis=0, tiled=True)


def by_rows(lesser, greater, coupling, occupation, shift, region_map, groups, shares):
    pieces = groups * shares // 2
    rows = lesser.shape[3] // pieces
    matrix = build(
        coupling, occupation, shift, region_map, groups, shares, lesser.shape[2], lesser.shape[0]
    )
    sent = pack(matrix, lesser, greater, pieces, rows)
    returned = exchange(mix(matrix, exchange(sent)))
    return unpack(returned, lesser.shape, pieces, rows)


def with_halo(shard, sides, width):
    for axis, dim in sides:
        size, length = (lax.axis_size(axis), shard.shape[dim])
        up = [(i, (i + 1) % size) for i in range(size - 1)]
        down = [(j, i) for i, j in up]
        last = lax.slice_in_dim(shard, length - width, length, axis=dim)
        first = lax.slice_in_dim(shard, 0, width, axis=dim)
        before = lax.ppermute(last, axis, up)
        after = lax.ppermute(first, axis, down)
        shard = jnp.concatenate([before, shard, after], axis=dim)
    return shard


def dft_basis(points):
    row_index = lax.broadcasted_iota(jnp.int32, (points, points), 0)
    col_index = lax.broadcasted_iota(jnp.int32, (points, points), 1)
    angles = (row_index * col_index % points).astype(jnp.float32) * (2.0 * math.pi / points)
    return jnp.concatenate([jnp.cos(angles), jnp.sin(angles)], axis=0)


def coupling_spectrum(coupling, region_map, basis):
    regions = coupling.shape[0]
    points = coupling.shape[2]
    onehot = (region_map[:, None] == jnp.arange(regions, dtype=jnp.int32)[None, :]).astype(
        jnp.float32
    )
    chosen = jnp.einsum("br,rmq->bmq", onehot, coupling, precision=lax.Precision.HIGHEST)
    spectrum = jnp.einsum("pq,bmq->bmp", basis, chosen, precision=lax.Precision.HIGHEST)
    return (spectrum[:, :, :points], -spectrum[:, :, points:])


def forward(stacked, basis_low):
    points = stacked.shape[3]
    columns = stacked.shape[5] // 2
    mixture = jnp.einsum(
        "pk,aebkxw->aebpxw", basis_low, stacked, preferred_element_type=jnp.float32
    )
    cosine = mixture[:, :, :, :points]
    sine = mixture[:, :, :, points:]
    return (
        cosine[..., :columns] + sine[..., columns:],
        cosine[..., columns:] - sine[..., :columns],
    )


def combine(hat_real, hat_imag, spec_real, spec_imag, occupation, shift, energies):
    out_shape = (2, energies) + hat_real.shape[2:]
    sigma_real = jnp.zeros(out_shape, jnp.float32)
    sigma_imag = jnp.zeros(out_shape, jnp.float32)
    points = spec_real.shape[2]
    for phonon in range(occupation.shape[0]):
        offset = shift[phonon]
        filling = occupation[phonon]
        lower_real = lax.dynamic_slice_in_dim(hat_real, SMAX - offset, energies, 1)
        lower_imag = lax.dynamic_slice_in_dim(hat_imag, SMAX - offset, energies, 1)
        upper_real = lax.dynamic_slice_in_dim(hat_real, SMAX + offset, energies, 1)
        upper_imag = lax.dynamic_slice_in_dim(hat_imag, SMAX + offset, energies, 1)
        weight_low = jnp.stack([filling, filling + 1.0]).reshape(2, 1, 1, 1, 1, 1)
        weight_high = jnp.stack([filling + 1.0, filling]).reshape(2, 1, 1, 1, 1, 1)
        mixed_real = weight_low * lower_real + weight_high * upper_real
        mixed_imag = weight_low * lower_imag + weight_high * upper_imag
        factor_real = spec_real[:, phonon, :].reshape(1, 1, -1, points, 1, 1)
        factor_imag = spec_imag[:, phonon, :].reshape(1, 1, -1, points, 1, 1)
        sigma_real = sigma_real + factor_real * mixed_real - factor_imag * mixed_imag
        sigma_imag = sigma_imag + factor_real * mixed_imag + factor_imag * mixed_real
    return (sigma_real, sigma_imag)


def inverse(sigma_real, sigma_imag, basis_low):
    points = sigma_real.shape[3]
    columns = sigma_real.shape[5]
    spectral = jnp.concatenate([sigma_real, sigma_imag], axis=-1).astype(jnp.bfloat16)
    mixture = jnp.einsum(
        "pk,aebkxw->aebpxw", basis_low, spectral, preferred_element_type=jnp.float32
    )
    cosine = mixture[:, :, :, :points]
    sine = mixture[:, :, :, points:]
    real_part = cosine[..., :columns] - sine[..., columns:]
    imag_part = cosine[..., columns:] + sine[..., :columns]
    return (jnp.concatenate([real_part, imag_part], axis=-1) * (1.0 / points)).astype(jnp.bfloat16)


def by_groups(lesser, greater, coupling, occupation, shift, region_map):
    stacked = jnp.stack([lesser, greater])
    widened = with_halo(stacked, (("grp", 1),), SMAX)
    regrouped = lax.all_to_all(widened, "mom", split_axis=4, concat_axis=3, tiled=True)
    points = regrouped.shape[3]
    basis = dft_basis(points)
    basis_low = basis.astype(jnp.bfloat16)
    spec_real, spec_imag = coupling_spectrum(coupling, region_map, basis)
    hat_real, hat_imag = forward(regrouped, basis_low)
    sigma_real, sigma_imag = combine(
        hat_real, hat_imag, spec_real, spec_imag, occupation, shift, lesser.shape[0]
    )
    result = inverse(sigma_real, sigma_imag, basis_low)
    returned = lax.all_to_all(result, "mom", split_axis=3, concat_axis=4, tiled=True)
    return (returned[0], returned[1])


def on_device(groups, shares, lesser, greater, coupling, occupation, shift, region_map):
    energies, blocks, momenta, height, columns = lesser.shape
    devices = groups * shares
    states = energies * momenta
    whole_tiles = (
        blocks == 1
        and devices >= 16
        and devices & (devices - 1) == 0
        and height & (height - 1) == 0
        and height % (TILE * (devices // 2)) == 0
        and TILE % states == 0
        and columns % 128 == 0
    )
    if whole_tiles:
        return by_rows(
            lesser, greater, coupling, occupation, shift, region_map, groups, shares
        )
    return by_groups(lesser, greater, coupling, occupation, shift, region_map)


def solution(mesh):
    return jax.shard_map(
        functools.partial(on_device, mesh.shape["grp"], mesh.shape["mom"]),
        mesh=mesh,
        in_specs=(
            P("grp", None, "mom", None, None),
            P("grp", None, "mom", None, None),
            P(),
            P(),
            P(),
            P(),
        ),
        out_specs=(P("grp", None, "mom", None, None), P("grp", None, "mom", None, None)),
        check_vma=False,
    )
```

```python
import functools
import math

import jax
import jax.numpy as jnp
from jax import lax
from jax.experimental import pallas as pl
from jax.experimental.pallas import tpu as pltpu
from jax.sharding import PartitionSpec as P

SMAX = 2
TILE = 16
VMEM_BYTES = 32 * 1024 * 1024
AXES = ("grp", "mom")


def turned(states, rows, back):
    size = states * rows
    down = lax.broadcasted_iota(jnp.int32, (size, size), 0)
    across = lax.broadcasted_iota(jnp.int32, (size, size), 1)
    if back:
        down, across = across, down
    bits = states.bit_length() - 1
    there = (down & (states - 1)) * rows + (down >> bits) == across
    return jnp.where(there, 1.0, 0.0).astype(jnp.bfloat16)


def mix_kernel(matrix_ref, in_ref, out_ref):
    devices, size, width = in_ref.shape
    states = matrix_ref.shape[0] // devices
    for start in range(0, size, states):
        block = in_ref[:, start : start + states, :].reshape(devices * states, width)
        mixed = jnp.dot(matrix_ref[...], block, preferred_element_type=jnp.float32)
        out_ref[:, start : start + states, :] = mixed.astype(out_ref.dtype).reshape(
            devices, states, width
        )


def unpack_kernel(in_ref, lesser_ref, greater_ref, held, sent):
    pieces, steps = in_ref.shape[0] // 2, sent.shape[1]
    rows = held.shape[3] // pieces
    batch = pieces // steps
    perm = turned(in_ref.shape[1] // rows, rows, True)
    copies = []
    for step in range(steps):
        span = slice(step * batch * rows, (step + 1) * batch * rows)
        for side, ref in enumerate((lesser_ref, greater_ref)):
            for piece in range(step * batch, (step + 1) * batch):
                moved = jnp.dot(
                    perm, in_ref[side * pieces + piece], preferred_element_type=jnp.float32
                )
                held[side, :, :, piece * rows : (piece + 1) * rows, :] = moved.astype(
                    held.dtype
                ).reshape(held.shape[1:3] + (rows, held.shape[4]))
            copy = pltpu.make_async_copy(
                held.at[side, :, :, span, :], ref.at[:, 0, :, span, :], sent.at[side, step]
            )
            copy.start(priority=side)
            copies.append(copy)
    for copy in copies:
        copy.wait()


def pack_kernel(matrix_ref, lesser_ref, greater_ref, out_ref):
    pieces, (size, width) = out_ref.shape[0] // 2, out_ref.shape[1:]
    rows = lesser_ref.shape[3] // pieces
    perm = turned(size // rows, rows, False)
    for side, ref in enumerate((lesser_ref, greater_ref)):
        for piece in range(pieces):
            block = ref[:, :, :, piece * rows : (piece + 1) * rows, :].reshape(size, width)
            moved = jnp.dot(perm, block, preferred_element_type=jnp.float32)
            out_ref[side * pieces + piece] = moved.astype(out_ref.dtype)


def build_kernel(groups, shares, momenta, energies, regions, small_ref, out_ref):
    points = shares * momenta
    states = energies * momenta
    size, levels = out_ref.shape[0], groups * energies
    modes = (small_ref.shape[0] - 3) // regions
    occupation, shift, region = (
        small_ref[at : at + 1, :] for at in range(regions * modes, regions * modes + 3)
    )
    place = lax.axis_index("grp") * shares + lax.axis_index("mom")
    greater = lax.div(place, jnp.int32(groups * shares // 2)).astype(jnp.float32)
    chosen = jnp.zeros((modes, points), jnp.float32)
    for at in range(regions):
        here = region[:, 0:1] == float(at)
        chosen = jnp.where(here, small_ref[at * modes : (at + 1) * modes, :], chosen)
    circles = {}
    for step in range(-SMAX, SMAX + 1):
        if step == 0:
            continue
        row = jnp.zeros((1, points), jnp.float32)
        for mode in range(modes):
            filling = occupation[:, mode : mode + 1] + (greater if step > 0 else 1.0 - greater)
            weight = jnp.where(shift[:, mode : mode + 1] == float(abs(step)), filling, 0.0)
            row = row + weight * chosen[mode : mode + 1, :]
        wide = jnp.broadcast_to(jnp.concatenate([row, row], axis=1), (points, 2 * points))
        circles[step] = pltpu.roll(wide, 0, 1, stride=1, stride_axis=0)[:, :points]
    nothing = jnp.zeros((points, points), jnp.float32)
    plain = jnp.concatenate(
        [
            jnp.concatenate([circles.get(out - level, nothing) for out in range(levels)], axis=1)
            for level in range(levels)
        ],
        axis=0,
    ).astype(jnp.bfloat16)

    at = lax.broadcasted_iota(jnp.int32, (size, 1), 0)
    device, energy = at >> (states.bit_length() - 1), (at & (states - 1)) >> (momenta.bit_length() - 1)
    energy = (device >> (shares.bit_length() - 1)) * energies + energy
    state = (energy * shares + (device & (shares - 1))) * momenta + (at & (momenta - 1))
    pick = state == lax.broadcasted_iota(jnp.int32, (size, levels * points), 1)
    pick = jnp.where(pick, 1.0, 0.0).astype(jnp.bfloat16)
    half = jnp.dot(pick, plain, preferred_element_type=jnp.float32).astype(jnp.bfloat16)
    full = lax.dot_general(
        pick, half, (((1,), (1,)), ((), ())), preferred_element_type=jnp.float32
    )
    out_ref[...] = full.astype(out_ref.dtype)


def params():
    return pltpu.CompilerParams(vmem_limit_bytes=VMEM_BYTES)


VECTORS = pl.BlockSpec(memory_space=pltpu.VMEM)
SLABS = pl.BlockSpec(memory_space=pl.ANY)


def build(coupling, occupation, shift, region_map, groups, shares, momenta, energies):
    size, points = groups * shares * energies * momenta, shares * momenta
    rows = coupling.shape[0] * coupling.shape[1]
    small = jnp.pad(coupling.reshape(rows, points), ((0, 3), (0, 0)))
    for at, part in enumerate((occupation, shift, region_map)):
        part = jnp.pad(part[None, :], ((rows + at, 2 - at), (0, points - part.shape[0])))
        small = small + part.astype(jnp.float32)
    return pl.pallas_call(
        functools.partial(build_kernel, groups, shares, momenta, energies, coupling.shape[0]),
        out_shape=jax.ShapeDtypeStruct((size, size), jnp.bfloat16),
        in_specs=[VECTORS],
        out_specs=VECTORS,
        compiler_params=params(),
        cost_estimate=pl.CostEstimate(
            flops=440 * size * size * points, bytes_accessed=88 * size * size, transcendentals=0
        ),
        name="build",
    )(small)


def pack(matrix, lesser, greater, pieces, rows):
    energies, _, momenta, _, columns = lesser.shape
    size = energies * momenta * rows
    return pl.pallas_call(
        pack_kernel,
        out_shape=jax.ShapeDtypeStruct((2 * pieces, size, columns), lesser.dtype),
        in_specs=[SLABS, VECTORS, VECTORS],
        out_specs=VECTORS,
        compiler_params=params(),
        name="pack",
    )(matrix, lesser, greater)


def unpack(packed, shape, pieces, rows):
    energies, _, momenta, _, columns = shape
    out = jax.ShapeDtypeStruct(shape, packed.dtype)
    return pl.pallas_call(
        unpack_kernel,
        out_shape=(out, out),
        in_specs=[VECTORS],
        out_specs=(SLABS, SLABS),
        scratch_shapes=[
            pltpu.VMEM((2, energies, momenta, pieces * rows, columns), packed.dtype),
            pltpu.SemaphoreType.DMA((2, math.gcd(pieces, 4))),
        ],
        compiler_params=params(),
        name="unpack",
    )(packed)


def mix(matrix, received):
    return pl.pallas_call(
        mix_kernel,
        out_shape=jax.ShapeDtypeStruct(received.shape, received.dtype),
        in_specs=[VECTORS, VECTORS],
        out_specs=VECTORS,
        compiler_params=params(),
        name="mix",
    )(matrix, received)


def exchange(array):
    return lax.all_to_all(array, AXES, split_axis=0, concat_axis=0, tiled=True)


def by_rows(lesser, greater, coupling, occupation, shift, region_map, groups, shares):
    pieces = groups * shares // 2
    rows = lesser.shape[3] // pieces
    matrix = build(
        coupling, occupation, shift, region_map, groups, shares, lesser.shape[2], lesser.shape[0]
    )
    sent = pack(matrix, lesser, greater, pieces, rows)
    returned = exchange(mix(matrix, exchange(sent)))
    return unpack(returned, lesser.shape, pieces, rows)


def with_halo(shard, sides, width):
    for axis, dim in sides:
        size, length = (lax.axis_size(axis), shard.shape[dim])
        up = [(i, (i + 1) % size) for i in range(size - 1)]
        down = [(j, i) for i, j in up]
        last = lax.slice_in_dim(shard, length - width, length, axis=dim)
        first = lax.slice_in_dim(shard, 0, width, axis=dim)
        before = lax.ppermute(last, axis, up)
        after = lax.ppermute(first, axis, down)
        shard = jnp.concatenate([before, shard, after], axis=dim)
    return shard


def dft_basis(points):
    row_index = lax.broadcasted_iota(jnp.int32, (points, points), 0)
    col_index = lax.broadcasted_iota(jnp.int32, (points, points), 1)
    angles = (row_index * col_index % points).astype(jnp.float32) * (2.0 * math.pi / points)
    return jnp.concatenate([jnp.cos(angles), jnp.sin(angles)], axis=0)


def coupling_spectrum(coupling, region_map, basis):
    regions = coupling.shape[0]
    points = coupling.shape[2]
    onehot = (region_map[:, None] == jnp.arange(regions, dtype=jnp.int32)[None, :]).astype(
        jnp.float32
    )
    chosen = jnp.einsum("br,rmq->bmq", onehot, coupling, precision=lax.Precision.HIGHEST)
    spectrum = jnp.einsum("pq,bmq->bmp", basis, chosen, precision=lax.Precision.HIGHEST)
    return (spectrum[:, :, :points], -spectrum[:, :, points:])


def forward(stacked, basis_low):
    points = stacked.shape[3]
    columns = stacked.shape[5] // 2
    mixture = jnp.einsum(
        "pk,aebkxw->aebpxw", basis_low, stacked, preferred_element_type=jnp.float32
    )
    cosine = mixture[:, :, :, :points]
    sine = mixture[:, :, :, points:]
    return (
        cosine[..., :columns] + sine[..., columns:],
        cosine[..., columns:] - sine[..., :columns],
    )


def combine(hat_real, hat_imag, spec_real, spec_imag, occupation, shift, energies):
    out_shape = (2, energies) + hat_real.shape[2:]
    sigma_real = jnp.zeros(out_shape, jnp.float32)
    sigma_imag = jnp.zeros(out_shape, jnp.float32)
    points = spec_real.shape[2]
    for phonon in range(occupation.shape[0]):
        offset = shift[phonon]
        filling = occupation[phonon]
        lower_real = lax.dynamic_slice_in_dim(hat_real, SMAX - offset, energies, 1)
        lower_imag = lax.dynamic_slice_in_dim(hat_imag, SMAX - offset, energies, 1)
        upper_real = lax.dynamic_slice_in_dim(hat_real, SMAX + offset, energies, 1)
        upper_imag = lax.dynamic_slice_in_dim(hat_imag, SMAX + offset, energies, 1)
        weight_low = jnp.stack([filling, filling + 1.0]).reshape(2, 1, 1, 1, 1, 1)
        weight_high = jnp.stack([filling + 1.0, filling]).reshape(2, 1, 1, 1, 1, 1)
        mixed_real = weight_low * lower_real + weight_high * upper_real
        mixed_imag = weight_low * lower_imag + weight_high * upper_imag
        factor_real = spec_real[:, phonon, :].reshape(1, 1, -1, points, 1, 1)
        factor_imag = spec_imag[:, phonon, :].reshape(1, 1, -1, points, 1, 1)
        sigma_real = sigma_real + factor_real * mixed_real - factor_imag * mixed_imag
        sigma_imag = sigma_imag + factor_real * mixed_imag + factor_imag * mixed_real
    return (sigma_real, sigma_imag)


def inverse(sigma_real, sigma_imag, basis_low):
    points = sigma_real.shape[3]
    columns = sigma_real.shape[5]
    spectral = jnp.concatenate([sigma_real, sigma_imag], axis=-1).astype(jnp.bfloat16)
    mixture = jnp.einsum(
        "pk,aebkxw->aebpxw", basis_low, spectral, preferred_element_type=jnp.float32
    )
    cosine = mixture[:, :, :, :points]
    sine = mixture[:, :, :, points:]
    real_part = cosine[..., :columns] - sine[..., columns:]
    imag_part = cosine[..., columns:] + sine[..., :columns]
    return (jnp.concatenate([real_part, imag_part], axis=-1) * (1.0 / points)).astype(jnp.bfloat16)


def by_groups(lesser, greater, coupling, occupation, shift, region_map):
    stacked = jnp.stack([lesser, greater])
    widened = with_halo(stacked, (("grp", 1),), SMAX)
    regrouped = lax.all_to_all(widened, "mom", split_axis=4, concat_axis=3, tiled=True)
    points = regrouped.shape[3]
    basis = dft_basis(points)
    basis_low = basis.astype(jnp.bfloat16)
    spec_real, spec_imag = coupling_spectrum(coupling, region_map, basis)
    hat_real, hat_imag = forward(regrouped, basis_low)
    sigma_real, sigma_imag = combine(
        hat_real, hat_imag, spec_real, spec_imag, occupation, shift, lesser.shape[0]
    )
    result = inverse(sigma_real, sigma_imag, basis_low)
    returned = lax.all_to_all(result, "mom", split_axis=3, concat_axis=4, tiled=True)
    return (returned[0], returned[1])


def on_device(groups, shares, lesser, greater, coupling, occupation, shift, region_map):
    energies, blocks, momenta, height, columns = lesser.shape
    devices = groups * shares
    states = energies * momenta
    whole_tiles = (
        blocks == 1
        and devices >= 4
        and devices & (devices - 1) == 0
        and height % (TILE * (devices // 2)) == 0
        and TILE % states == 0
        and columns % 128 == 0
    )
    if whole_tiles:
        return by_rows(
            lesser, greater, coupling, occupation, shift, region_map, groups, shares
        )
    return by_groups(lesser, greater, coupling, occupation, shift, region_map)


def solution(mesh):
    return jax.shard_map(
        functools.partial(on_device, mesh.shape["grp"], mesh.shape["mom"]),
        mesh=mesh,
        in_specs=(
            P("grp", None, "mom", None, None),
            P("grp", None, "mom", None, None),
            P(),
            P(),
            P(),
            P(),
        ),
        out_specs=(P("grp", None, "mom", None, None), P("grp", None, "mom", None, None)),
        check_vma=False,
    )
```

```python
import functools
import math

import jax
import jax.numpy as jnp
from jax import lax
from jax.experimental import pallas as pl
from jax.experimental.pallas import tpu as pltpu
from jax.sharding import PartitionSpec as P

SMAX = 2
TILE = 16
VMEM_BYTES = 32 * 1024 * 1024
AXES = ("grp", "mom")


def turned(states, rows, back):
    size = states * rows
    down = lax.broadcasted_iota(jnp.int32, (size, size), 0)
    across = lax.broadcasted_iota(jnp.int32, (size, size), 1)
    if back:
        down, across = across, down
    bits = states.bit_length() - 1
    there = (down & (states - 1)) * rows + (down >> bits) == across
    return jnp.where(there, 1.0, 0.0).astype(jnp.bfloat16)


def mix_kernel(matrix_ref, in_ref, out_ref):
    devices, size, width = in_ref.shape
    states = matrix_ref.shape[0] // devices
    beside = math.gcd(size // states, 4)
    for first in range(0, size, beside * states):
        starts = range(first, first + beside * states, states)
        rows = [in_ref[:, at : at + states, :].reshape(devices * states, width) for at in starts]
        mixed = jnp.dot(
            matrix_ref[...], jnp.concatenate(rows, axis=1), preferred_element_type=jnp.float32
        ).astype(out_ref.dtype)
        for turn, at in enumerate(starts):
            row = mixed[:, turn * width : (turn + 1) * width]
            out_ref[:, at : at + states, :] = row.reshape(devices, states, width)


def unpack_kernel(in_ref, lesser_ref, greater_ref, held, sent):
    pieces, steps = in_ref.shape[0] // 2, sent.shape[1]
    rows = held.shape[3] // pieces
    batch = pieces // steps
    perm = turned(in_ref.shape[1] // rows, rows, True)
    copies = []
    for step in range(steps):
        span = slice(step * batch * rows, (step + 1) * batch * rows)
        for side, ref in enumerate((lesser_ref, greater_ref)):
            for piece in range(step * batch, (step + 1) * batch):
                moved = jnp.dot(
                    perm, in_ref[side * pieces + piece], preferred_element_type=jnp.float32
                )
                held[side, :, :, piece * rows : (piece + 1) * rows, :] = moved.astype(
                    held.dtype
                ).reshape(held.shape[1:3] + (rows, held.shape[4]))
            copy = pltpu.make_async_copy(
                held.at[side, :, :, span, :], ref.at[:, 0, :, span, :], sent.at[side, step]
            )
            copy.start(priority=side)
            copies.append(copy)
    for copy in copies:
        copy.wait()


def pack_kernel(matrix_ref, lesser_ref, greater_ref, out_ref):
    pieces, (size, width) = out_ref.shape[0] // 2, out_ref.shape[1:]
    rows = lesser_ref.shape[3] // pieces
    perm = turned(size // rows, rows, False)
    for side, ref in enumerate((lesser_ref, greater_ref)):
        for piece in range(pieces):
            block = ref[:, :, :, piece * rows : (piece + 1) * rows, :].reshape(size, width)
            moved = jnp.dot(perm, block, preferred_element_type=jnp.float32)
            out_ref[side * pieces + piece] = moved.astype(out_ref.dtype)


def build_kernel(groups, shares, momenta, energies, regions, small_ref, out_ref):
    points = shares * momenta
    states = energies * momenta
    size, levels = out_ref.shape[0], groups * energies
    modes = (small_ref.shape[0] - 3) // regions
    occupation, shift, region = (
        small_ref[at : at + 1, :] for at in range(regions * modes, regions * modes + 3)
    )
    place = lax.axis_index("grp") * shares + lax.axis_index("mom")
    greater = lax.div(place, jnp.int32(groups * shares // 2)).astype(jnp.float32)
    chosen = jnp.zeros((modes, points), jnp.float32)
    for at in range(regions):
        here = region[:, 0:1] == float(at)
        chosen = jnp.where(here, small_ref[at * modes : (at + 1) * modes, :], chosen)
    circles = {}
    for step in range(-SMAX, SMAX + 1):
        if step == 0:
            continue
        row = jnp.zeros((1, points), jnp.float32)
        for mode in range(modes):
            filling = occupation[:, mode : mode + 1] + (greater if step > 0 else 1.0 - greater)
            weight = jnp.where(shift[:, mode : mode + 1] == float(abs(step)), filling, 0.0)
            row = row + weight * chosen[mode : mode + 1, :]
        wide = jnp.broadcast_to(jnp.concatenate([row, row], axis=1), (points, 2 * points))
        circles[step] = pltpu.roll(wide, 0, 1, stride=1, stride_axis=0)[:, :points]
    nothing = jnp.zeros((points, points), jnp.float32)
    plain = jnp.concatenate(
        [
            jnp.concatenate([circles.get(out - level, nothing) for out in range(levels)], axis=1)
            for level in range(levels)
        ],
        axis=0,
    ).astype(jnp.bfloat16)

    at = lax.broadcasted_iota(jnp.int32, (size, 1), 0)
    device, energy = at >> (states.bit_length() - 1), (at & (states - 1)) >> (momenta.bit_length() - 1)
    energy = (device >> (shares.bit_length() - 1)) * energies + energy
    state = (energy * shares + (device & (shares - 1))) * momenta + (at & (momenta - 1))
    pick = state == lax.broadcasted_iota(jnp.int32, (size, levels * points), 1)
    pick = jnp.where(pick, 1.0, 0.0).astype(jnp.bfloat16)
    half = jnp.dot(pick, plain, preferred_element_type=jnp.float32).astype(jnp.bfloat16)
    full = lax.dot_general(
        pick, half, (((1,), (1,)), ((), ())), preferred_element_type=jnp.float32
    )
    out_ref[...] = full.astype(out_ref.dtype)


def params():
    return pltpu.CompilerParams(vmem_limit_bytes=VMEM_BYTES)


VECTORS = pl.BlockSpec(memory_space=pltpu.VMEM)
SLABS = pl.BlockSpec(memory_space=pl.ANY)


def build(coupling, occupation, shift, region_map, groups, shares, momenta, energies):
    size, points = groups * shares * energies * momenta, shares * momenta
    rows = coupling.shape[0] * coupling.shape[1]
    small = jnp.pad(coupling.reshape(rows, points), ((0, 3), (0, 0)))
    for at, part in enumerate((occupation, shift, region_map)):
        part = jnp.pad(part[None, :], ((rows + at, 2 - at), (0, points - part.shape[0])))
        small = small + part.astype(jnp.float32)
    return pl.pallas_call(
        functools.partial(build_kernel, groups, shares, momenta, energies, coupling.shape[0]),
        out_shape=jax.ShapeDtypeStruct((size, size), jnp.bfloat16),
        in_specs=[VECTORS],
        out_specs=VECTORS,
        compiler_params=params(),
        cost_estimate=pl.CostEstimate(
            flops=440 * size * size * points, bytes_accessed=88 * size * size, transcendentals=0
        ),
        name="build",
    )(small)


def pack(matrix, lesser, greater, pieces, rows):
    energies, _, momenta, _, columns = lesser.shape
    size = energies * momenta * rows
    return pl.pallas_call(
        pack_kernel,
        out_shape=jax.ShapeDtypeStruct((2 * pieces, size, columns), lesser.dtype),
        in_specs=[SLABS, VECTORS, VECTORS],
        out_specs=VECTORS,
        compiler_params=params(),
        name="pack",
    )(matrix, lesser, greater)


def unpack(packed, shape, pieces, rows):
    energies, _, momenta, _, columns = shape
    out = jax.ShapeDtypeStruct(shape, packed.dtype)
    return pl.pallas_call(
        unpack_kernel,
        out_shape=(out, out),
        in_specs=[VECTORS],
        out_specs=(SLABS, SLABS),
        scratch_shapes=[
            pltpu.VMEM((2, energies, momenta, pieces * rows, columns), packed.dtype),
            pltpu.SemaphoreType.DMA((2, math.gcd(pieces, 4))),
        ],
        compiler_params=params(),
        name="unpack",
    )(packed)


def mix(matrix, received):
    return pl.pallas_call(
        mix_kernel,
        out_shape=jax.ShapeDtypeStruct(received.shape, received.dtype),
        in_specs=[VECTORS, VECTORS],
        out_specs=VECTORS,
        compiler_params=params(),
        name="mix",
    )(matrix, received)


def exchange(array):
    return lax.all_to_all(array, AXES, split_axis=0, concat_axis=0, tiled=True)


def by_rows(lesser, greater, coupling, occupation, shift, region_map, groups, shares):
    pieces = groups * shares // 2
    rows = lesser.shape[3] // pieces
    matrix = build(
        coupling, occupation, shift, region_map, groups, shares, lesser.shape[2], lesser.shape[0]
    )
    sent = pack(matrix, lesser, greater, pieces, rows)
    returned = exchange(mix(matrix, exchange(sent)))
    return unpack(returned, lesser.shape, pieces, rows)


def with_halo(shard, sides, width):
    for axis, dim in sides:
        size, length = (lax.axis_size(axis), shard.shape[dim])
        up = [(i, (i + 1) % size) for i in range(size - 1)]
        down = [(j, i) for i, j in up]
        last = lax.slice_in_dim(shard, length - width, length, axis=dim)
        first = lax.slice_in_dim(shard, 0, width, axis=dim)
        before = lax.ppermute(last, axis, up)
        after = lax.ppermute(first, axis, down)
        shard = jnp.concatenate([before, shard, after], axis=dim)
    return shard


def dft_basis(points):
    row_index = lax.broadcasted_iota(jnp.int32, (points, points), 0)
    col_index = lax.broadcasted_iota(jnp.int32, (points, points), 1)
    angles = (row_index * col_index % points).astype(jnp.float32) * (2.0 * math.pi / points)
    return jnp.concatenate([jnp.cos(angles), jnp.sin(angles)], axis=0)


def coupling_spectrum(coupling, region_map, basis):
    regions = coupling.shape[0]
    points = coupling.shape[2]
    onehot = (region_map[:, None] == jnp.arange(regions, dtype=jnp.int32)[None, :]).astype(
        jnp.float32
    )
    chosen = jnp.einsum("br,rmq->bmq", onehot, coupling, precision=lax.Precision.HIGHEST)
    spectrum = jnp.einsum("pq,bmq->bmp", basis, chosen, precision=lax.Precision.HIGHEST)
    return (spectrum[:, :, :points], -spectrum[:, :, points:])


def forward(stacked, basis_low):
    points = stacked.shape[3]
    columns = stacked.shape[5] // 2
    mixture = jnp.einsum(
        "pk,aebkxw->aebpxw", basis_low, stacked, preferred_element_type=jnp.float32
    )
    cosine = mixture[:, :, :, :points]
    sine = mixture[:, :, :, points:]
    return (
        cosine[..., :columns] + sine[..., columns:],
        cosine[..., columns:] - sine[..., :columns],
    )


def combine(hat_real, hat_imag, spec_real, spec_imag, occupation, shift, energies):
    out_shape = (2, energies) + hat_real.shape[2:]
    sigma_real = jnp.zeros(out_shape, jnp.float32)
    sigma_imag = jnp.zeros(out_shape, jnp.float32)
    points = spec_real.shape[2]
    for phonon in range(occupation.shape[0]):
        offset = shift[phonon]
        filling = occupation[phonon]
        lower_real = lax.dynamic_slice_in_dim(hat_real, SMAX - offset, energies, 1)
        lower_imag = lax.dynamic_slice_in_dim(hat_imag, SMAX - offset, energies, 1)
        upper_real = lax.dynamic_slice_in_dim(hat_real, SMAX + offset, energies, 1)
        upper_imag = lax.dynamic_slice_in_dim(hat_imag, SMAX + offset, energies, 1)
        weight_low = jnp.stack([filling, filling + 1.0]).reshape(2, 1, 1, 1, 1, 1)
        weight_high = jnp.stack([filling + 1.0, filling]).reshape(2, 1, 1, 1, 1, 1)
        mixed_real = weight_low * lower_real + weight_high * upper_real
        mixed_imag = weight_low * lower_imag + weight_high * upper_imag
        factor_real = spec_real[:, phonon, :].reshape(1, 1, -1, points, 1, 1)
        factor_imag = spec_imag[:, phonon, :].reshape(1, 1, -1, points, 1, 1)
        sigma_real = sigma_real + factor_real * mixed_real - factor_imag * mixed_imag
        sigma_imag = sigma_imag + factor_real * mixed_imag + factor_imag * mixed_real
    return (sigma_real, sigma_imag)


def inverse(sigma_real, sigma_imag, basis_low):
    points = sigma_real.shape[3]
    columns = sigma_real.shape[5]
    spectral = jnp.concatenate([sigma_real, sigma_imag], axis=-1).astype(jnp.bfloat16)
    mixture = jnp.einsum(
        "pk,aebkxw->aebpxw", basis_low, spectral, preferred_element_type=jnp.float32
    )
    cosine = mixture[:, :, :, :points]
    sine = mixture[:, :, :, points:]
    real_part = cosine[..., :columns] - sine[..., columns:]
    imag_part = cosine[..., columns:] + sine[..., :columns]
    return (jnp.concatenate([real_part, imag_part], axis=-1) * (1.0 / points)).astype(jnp.bfloat16)


def by_groups(lesser, greater, coupling, occupation, shift, region_map):
    stacked = jnp.stack([lesser, greater])
    widened = with_halo(stacked, (("grp", 1),), SMAX)
    regrouped = lax.all_to_all(widened, "mom", split_axis=4, concat_axis=3, tiled=True)
    points = regrouped.shape[3]
    basis = dft_basis(points)
    basis_low = basis.astype(jnp.bfloat16)
    spec_real, spec_imag = coupling_spectrum(coupling, region_map, basis)
    hat_real, hat_imag = forward(regrouped, basis_low)
    sigma_real, sigma_imag = combine(
        hat_real, hat_imag, spec_real, spec_imag, occupation, shift, lesser.shape[0]
    )
    result = inverse(sigma_real, sigma_imag, basis_low)
    returned = lax.all_to_all(result, "mom", split_axis=3, concat_axis=4, tiled=True)
    return (returned[0], returned[1])


def on_device(groups, shares, lesser, greater, coupling, occupation, shift, region_map):
    energies, blocks, momenta, height, columns = lesser.shape
    devices = groups * shares
    states = energies * momenta
    whole_tiles = (
        blocks == 1
        and devices >= 4
        and devices & (devices - 1) == 0
        and height % (TILE * (devices // 2)) == 0
        and TILE % states == 0
        and columns % 128 == 0
    )
    if whole_tiles:
        return by_rows(
            lesser, greater, coupling, occupation, shift, region_map, groups, shares
        )
    return by_groups(lesser, greater, coupling, occupation, shift, region_map)


def solution(mesh):
    return jax.shard_map(
        functools.partial(on_device, mesh.shape["grp"], mesh.shape["mom"]),
        mesh=mesh,
        in_specs=(
            P("grp", None, "mom", None, None),
            P("grp", None, "mom", None, None),
            P(),
            P(),
            P(),
            P(),
        ),
        out_specs=(P("grp", None, "mom", None, None), P("grp", None, "mom", None, None)),
        check_vma=False,
    )
```

```python
import functools
import math

import jax
import jax.numpy as jnp
from jax import lax
from jax.experimental import pallas as pl
from jax.experimental.pallas import tpu as pltpu
from jax.sharding import PartitionSpec as P

SMAX = 2
TILE = 16
VMEM_BYTES = 32 * 1024 * 1024
AXES = ("grp", "near", "half")


def turned(states, rows, back):
    size = states * rows
    down = lax.broadcasted_iota(jnp.int32, (size, size), 0)
    across = lax.broadcasted_iota(jnp.int32, (size, size), 1)
    if back:
        down, across = across, down
    bits = states.bit_length() - 1
    there = (down & (states - 1)) * rows + (down >> bits) == across
    return jnp.where(there, 1.0, 0.0).astype(jnp.bfloat16)


def mix_kernel(matrix_ref, in_ref, out_ref):
    devices, size, width = in_ref.shape
    states = matrix_ref.shape[0] // devices
    for start in range(0, size, states):
        block = in_ref[:, start : start + states, :].reshape(devices * states, width)
        mixed = jnp.dot(matrix_ref[...], block, preferred_element_type=jnp.float32)
        out_ref[:, start : start + states, :] = mixed.astype(out_ref.dtype).reshape(
            devices, states, width
        )


def unpack_kernel(in_ref, lesser_ref, greater_ref, held, sent):
    pieces, steps = in_ref.shape[0] // 2, sent.shape[1]
    rows = held.shape[3] // pieces
    batch = pieces // steps
    perm = turned(in_ref.shape[1] // rows, rows, True)
    copies = []
    for step in range(steps):
        span = slice(step * batch * rows, (step + 1) * batch * rows)
        for side, ref in enumerate((lesser_ref, greater_ref)):
            for piece in range(step * batch, (step + 1) * batch):
                moved = jnp.dot(
                    perm, in_ref[side * pieces + piece], preferred_element_type=jnp.float32
                )
                held[side, :, :, piece * rows : (piece + 1) * rows, :] = moved.astype(
                    held.dtype
                ).reshape(held.shape[1:3] + (rows, held.shape[4]))
            copy = pltpu.make_async_copy(
                held.at[side, :, :, span, :], ref.at[:, 0, :, span, :], sent.at[side, step]
            )
            copy.start(priority=side)
            copies.append(copy)
    for copy in copies:
        copy.wait()


def pack_kernel(matrix_ref, lesser_ref, greater_ref, out_ref):
    pieces, (size, width) = out_ref.shape[0] // 2, out_ref.shape[1:]
    rows = lesser_ref.shape[3] // pieces
    perm = turned(size // rows, rows, False)
    for side, ref in enumerate((lesser_ref, greater_ref)):
        for piece in range(pieces):
            block = ref[:, :, :, piece * rows : (piece + 1) * rows, :].reshape(size, width)
            moved = jnp.dot(perm, block, preferred_element_type=jnp.float32)
            out_ref[side * pieces + piece] = moved.astype(out_ref.dtype)


def build_kernel(groups, shares, momenta, energies, regions, small_ref, out_ref):
    points = shares * momenta
    states = energies * momenta
    size, levels = out_ref.shape[0], groups * energies
    modes = (small_ref.shape[0] - 3) // regions
    occupation, shift, region = (
        small_ref[at : at + 1, :] for at in range(regions * modes, regions * modes + 3)
    )
    greater = lax.axis_index("grp").astype(jnp.float32)
    chosen = jnp.zeros((modes, points), jnp.float32)
    for at in range(regions):
        here = region[:, 0:1] == float(at)
        chosen = jnp.where(here, small_ref[at * modes : (at + 1) * modes, :], chosen)
    circles = {}
    for step in range(-SMAX, SMAX + 1):
        if step == 0:
            continue
        row = jnp.zeros((1, points), jnp.float32)
        for mode in range(modes):
            filling = occupation[:, mode : mode + 1] + (greater if step > 0 else 1.0 - greater)
            weight = jnp.where(shift[:, mode : mode + 1] == float(abs(step)), filling, 0.0)
            row = row + weight * chosen[mode : mode + 1, :]
        wide = jnp.broadcast_to(jnp.concatenate([row, row], axis=1), (points, 2 * points))
        circles[step] = pltpu.roll(wide, 0, 1, stride=1, stride_axis=0)[:, :points]
    nothing = jnp.zeros((points, points), jnp.float32)
    plain = jnp.concatenate(
        [
            jnp.concatenate([circles.get(out - level, nothing) for out in range(levels)], axis=1)
            for level in range(levels)
        ],
        axis=0,
    ).astype(jnp.bfloat16)

    at = lax.broadcasted_iota(jnp.int32, (size, 1), 0)
    device, energy = at >> (states.bit_length() - 1), (at & (states - 1)) >> (momenta.bit_length() - 1)
    energy = (device >> (shares.bit_length() - 1)) * energies + energy
    share = ((device & 1) * (shares // 2)) + ((device & (shares - 1)) >> 1)
    state = (energy * shares + share) * momenta + (at & (momenta - 1))
    pick = state == lax.broadcasted_iota(jnp.int32, (size, levels * points), 1)
    pick = jnp.where(pick, 1.0, 0.0).astype(jnp.bfloat16)
    half = jnp.dot(pick, plain, preferred_element_type=jnp.float32).astype(jnp.bfloat16)
    full = lax.dot_general(
        pick, half, (((1,), (1,)), ((), ())), preferred_element_type=jnp.float32
    )
    out_ref[...] = full.astype(out_ref.dtype)


def params():
    return pltpu.CompilerParams(vmem_limit_bytes=VMEM_BYTES)


VECTORS = pl.BlockSpec(memory_space=pltpu.VMEM)
SLABS = pl.BlockSpec(memory_space=pl.ANY)


def build(coupling, occupation, shift, region_map, groups, shares, momenta, energies):
    size, points = groups * shares * energies * momenta, shares * momenta
    rows = coupling.shape[0] * coupling.shape[1]
    small = jnp.pad(coupling.reshape(rows, points), ((0, 3), (0, 0)))
    for at, part in enumerate((occupation, shift, region_map)):
        part = jnp.pad(part[None, :], ((rows + at, 2 - at), (0, points - part.shape[0])))
        small = small + part.astype(jnp.float32)
    return pl.pallas_call(
        functools.partial(build_kernel, groups, shares, momenta, energies, coupling.shape[0]),
        out_shape=jax.ShapeDtypeStruct((size, size), jnp.bfloat16),
        in_specs=[VECTORS],
        out_specs=VECTORS,
        compiler_params=params(),
        cost_estimate=pl.CostEstimate(
            flops=440 * size * size * points, bytes_accessed=88 * size * size, transcendentals=0
        ),
        name="build",
    )(small)


def pack(matrix, lesser, greater, pieces, rows):
    energies, _, momenta, _, columns = lesser.shape
    size = energies * momenta * rows
    return pl.pallas_call(
        pack_kernel,
        out_shape=jax.ShapeDtypeStruct((2 * pieces, size, columns), lesser.dtype),
        in_specs=[SLABS, VECTORS, VECTORS],
        out_specs=VECTORS,
        compiler_params=params(),
        name="pack",
    )(matrix, lesser, greater)


def unpack(packed, shape, pieces, rows):
    energies, _, momenta, _, columns = shape
    out = jax.ShapeDtypeStruct(shape, packed.dtype)
    return pl.pallas_call(
        unpack_kernel,
        out_shape=(out, out),
        in_specs=[VECTORS],
        out_specs=(SLABS, SLABS),
        scratch_shapes=[
            pltpu.VMEM((2, energies, momenta, pieces * rows, columns), packed.dtype),
            pltpu.SemaphoreType.DMA((2, math.gcd(pieces, 4))),
        ],
        compiler_params=params(),
        name="unpack",
    )(packed)


def mix(matrix, received):
    return pl.pallas_call(
        mix_kernel,
        out_shape=jax.ShapeDtypeStruct(received.shape, received.dtype),
        in_specs=[VECTORS, VECTORS],
        out_specs=VECTORS,
        compiler_params=params(),
        name="mix",
    )(matrix, received)


def exchange(array):
    return lax.all_to_all(array, AXES, split_axis=0, concat_axis=0, tiled=True)


def by_rows(lesser, greater, coupling, occupation, shift, region_map, groups, shares):
    pieces = groups * shares // 2
    rows = lesser.shape[3] // pieces
    matrix = build(
        coupling, occupation, shift, region_map, groups, shares, lesser.shape[2], lesser.shape[0]
    )
    sent = pack(matrix, lesser, greater, pieces, rows)
    returned = exchange(mix(matrix, exchange(sent)))
    return unpack(returned, lesser.shape, pieces, rows)


def with_halo(shard, sides, width):
    for axis, dim in sides:
        size, length = (lax.axis_size(axis), shard.shape[dim])
        up = [(i, (i + 1) % size) for i in range(size - 1)]
        down = [(j, i) for i, j in up]
        last = lax.slice_in_dim(shard, length - width, length, axis=dim)
        first = lax.slice_in_dim(shard, 0, width, axis=dim)
        before = lax.ppermute(last, axis, up)
        after = lax.ppermute(first, axis, down)
        shard = jnp.concatenate([before, shard, after], axis=dim)
    return shard


def dft_basis(points):
    row_index = lax.broadcasted_iota(jnp.int32, (points, points), 0)
    col_index = lax.broadcasted_iota(jnp.int32, (points, points), 1)
    angles = (row_index * col_index % points).astype(jnp.float32) * (2.0 * math.pi / points)
    return jnp.concatenate([jnp.cos(angles), jnp.sin(angles)], axis=0)


def coupling_spectrum(coupling, region_map, basis):
    regions = coupling.shape[0]
    points = coupling.shape[2]
    onehot = (region_map[:, None] == jnp.arange(regions, dtype=jnp.int32)[None, :]).astype(
        jnp.float32
    )
    chosen = jnp.einsum("br,rmq->bmq", onehot, coupling, precision=lax.Precision.HIGHEST)
    spectrum = jnp.einsum("pq,bmq->bmp", basis, chosen, precision=lax.Precision.HIGHEST)
    return (spectrum[:, :, :points], -spectrum[:, :, points:])


def forward(stacked, basis_low):
    points = stacked.shape[3]
    columns = stacked.shape[5] // 2
    mixture = jnp.einsum(
        "pk,aebkxw->aebpxw", basis_low, stacked, preferred_element_type=jnp.float32
    )
    cosine = mixture[:, :, :, :points]
    sine = mixture[:, :, :, points:]
    return (
        cosine[..., :columns] + sine[..., columns:],
        cosine[..., columns:] - sine[..., :columns],
    )


def combine(hat_real, hat_imag, spec_real, spec_imag, occupation, shift, energies):
    out_shape = (2, energies) + hat_real.shape[2:]
    sigma_real = jnp.zeros(out_shape, jnp.float32)
    sigma_imag = jnp.zeros(out_shape, jnp.float32)
    points = spec_real.shape[2]
    for phonon in range(occupation.shape[0]):
        offset = shift[phonon]
        filling = occupation[phonon]
        lower_real = lax.dynamic_slice_in_dim(hat_real, SMAX - offset, energies, 1)
        lower_imag = lax.dynamic_slice_in_dim(hat_imag, SMAX - offset, energies, 1)
        upper_real = lax.dynamic_slice_in_dim(hat_real, SMAX + offset, energies, 1)
        upper_imag = lax.dynamic_slice_in_dim(hat_imag, SMAX + offset, energies, 1)
        weight_low = jnp.stack([filling, filling + 1.0]).reshape(2, 1, 1, 1, 1, 1)
        weight_high = jnp.stack([filling + 1.0, filling]).reshape(2, 1, 1, 1, 1, 1)
        mixed_real = weight_low * lower_real + weight_high * upper_real
        mixed_imag = weight_low * lower_imag + weight_high * upper_imag
        factor_real = spec_real[:, phonon, :].reshape(1, 1, -1, points, 1, 1)
        factor_imag = spec_imag[:, phonon, :].reshape(1, 1, -1, points, 1, 1)
        sigma_real = sigma_real + factor_real * mixed_real - factor_imag * mixed_imag
        sigma_imag = sigma_imag + factor_real * mixed_imag + factor_imag * mixed_real
    return (sigma_real, sigma_imag)


def inverse(sigma_real, sigma_imag, basis_low):
    points = sigma_real.shape[3]
    columns = sigma_real.shape[5]
    spectral = jnp.concatenate([sigma_real, sigma_imag], axis=-1).astype(jnp.bfloat16)
    mixture = jnp.einsum(
        "pk,aebkxw->aebpxw", basis_low, spectral, preferred_element_type=jnp.float32
    )
    cosine = mixture[:, :, :, :points]
    sine = mixture[:, :, :, points:]
    real_part = cosine[..., :columns] - sine[..., columns:]
    imag_part = cosine[..., columns:] + sine[..., :columns]
    return (jnp.concatenate([real_part, imag_part], axis=-1) * (1.0 / points)).astype(jnp.bfloat16)


def by_groups(lesser, greater, coupling, occupation, shift, region_map, momentum):
    stacked = jnp.stack([lesser, greater])
    widened = with_halo(stacked, (("grp", 1),), SMAX)
    regrouped = lax.all_to_all(widened, momentum, split_axis=4, concat_axis=3, tiled=True)
    points = regrouped.shape[3]
    basis = dft_basis(points)
    basis_low = basis.astype(jnp.bfloat16)
    spec_real, spec_imag = coupling_spectrum(coupling, region_map, basis)
    hat_real, hat_imag = forward(regrouped, basis_low)
    sigma_real, sigma_imag = combine(
        hat_real, hat_imag, spec_real, spec_imag, occupation, shift, lesser.shape[0]
    )
    result = inverse(sigma_real, sigma_imag, basis_low)
    returned = lax.all_to_all(result, momentum, split_axis=3, concat_axis=4, tiled=True)
    return (returned[0], returned[1])


def whole_tiles(shape, groups, shares):
    energies, blocks, momenta, height, columns = shape
    return (
        groups == 2
        and shares >= 8
        and shares & (shares - 1) == 0
        and blocks == 1
        and height == TILE * shares
        and TILE % (energies * momenta) == 0
        and columns % 128 == 0
    )


def solution(mesh):
    groups, shares = mesh.shape["grp"], mesh.shape["mom"]
    momentum = ("half", "near")
    split = jax.sharding.Mesh(mesh.devices.reshape(groups, 2, shares // 2), ("grp",) + momentum)

    def on_device(lesser, *rest):
        if whole_tiles(lesser.shape, groups, shares):
            return by_rows(lesser, *rest, groups, shares)
        return by_groups(lesser, *rest, momentum)

    slab = P("grp", None, momentum, None, None)
    return jax.shard_map(
        on_device,
        mesh=split,
        in_specs=(slab, slab, P(), P(), P(), P()),
        out_specs=(slab, slab),
        check_vma=False,
    )
```

```python
import functools
import math

import jax
import jax.numpy as jnp
from jax import lax
from jax.experimental import pallas as pl
from jax.experimental.pallas import tpu as pltpu
from jax.sharding import PartitionSpec as P

SMAX = 2
TILE = 16
VMEM_BYTES = 32 * 1024 * 1024
AXES = ("grp", "mom")


def turned(states, rows, back):
    size = states * rows
    down = lax.broadcasted_iota(jnp.int32, (size, size), 0)
    across = lax.broadcasted_iota(jnp.int32, (size, size), 1)
    if back:
        down, across = across, down
    bits = states.bit_length() - 1
    there = (down & (states - 1)) * rows + (down >> bits) == across
    return jnp.where(there, 1.0, 0.0).astype(jnp.bfloat16)


def mix_kernel(matrix_ref, in_ref, out_ref):
    devices, size, width = in_ref.shape
    states = matrix_ref.shape[0] // devices
    for start in range(0, size, states):
        block = in_ref[:, start : start + states, :].reshape(devices * states, width)
        mixed = jnp.dot(matrix_ref[...], block, preferred_element_type=jnp.float32)
        out_ref[:, start : start + states, :] = mixed.astype(out_ref.dtype).reshape(
            devices, states, width
        )


def unpack_kernel(in_ref, lesser_ref, greater_ref, held, sent):
    pieces, steps = in_ref.shape[0] // 2, sent.shape[1]
    rows = held.shape[3] // pieces
    batch = pieces // steps
    perm = turned(in_ref.shape[1] // rows, rows, True)
    copies = []
    for step in range(steps):
        span = slice(step * batch * rows, (step + 1) * batch * rows)
        for side, ref in enumerate((lesser_ref, greater_ref)):
            for piece in range(step * batch, (step + 1) * batch):
                moved = jnp.dot(
                    perm, in_ref[side * pieces + piece], preferred_element_type=jnp.float32
                )
                held[side, :, :, piece * rows : (piece + 1) * rows, :] = moved.astype(
                    held.dtype
                ).reshape(held.shape[1:3] + (rows, held.shape[4]))
            copy = pltpu.make_async_copy(
                held.at[side, :, :, span, :], ref.at[:, 0, :, span, :], sent.at[side, step]
            )
            copy.start(priority=side)
            copies.append(copy)
    for copy in copies:
        copy.wait()


def pack_kernel(matrix_ref, lesser_ref, greater_ref, out_ref):
    pieces, (size, width) = out_ref.shape[0] // 2, out_ref.shape[1:]
    rows = lesser_ref.shape[3] // pieces
    perm = turned(size // rows, rows, False)
    for side, ref in enumerate((lesser_ref, greater_ref)):
        for piece in range(pieces):
            block = ref[:, :, :, piece * rows : (piece + 1) * rows, :].reshape(size, width)
            moved = jnp.dot(perm, block, preferred_element_type=jnp.float32)
            out_ref[side * pieces + piece] = moved.astype(out_ref.dtype)


def build_kernel(groups, shares, momenta, energies, regions, small_ref, out_ref):
    points = shares * momenta
    states = energies * momenta
    size, levels = out_ref.shape[0], groups * energies
    modes = (small_ref.shape[0] - 3) // regions
    occupation, shift, region = (
        small_ref[at : at + 1, :] for at in range(regions * modes, regions * modes + 3)
    )
    place = lax.axis_index("grp") * shares + lax.axis_index("mom")
    greater = lax.div(place, jnp.int32(groups * shares // 2)).astype(jnp.float32)
    chosen = jnp.zeros((modes, points), jnp.float32)
    for at in range(regions):
        here = region[:, 0:1] == float(at)
        chosen = jnp.where(here, small_ref[at * modes : (at + 1) * modes, :], chosen)
    circles = {}
    for step in range(-SMAX, SMAX + 1):
        if step == 0:
            continue
        row = jnp.zeros((1, points), jnp.float32)
        for mode in range(modes):
            filling = occupation[:, mode : mode + 1] + (greater if step > 0 else 1.0 - greater)
            weight = jnp.where(shift[:, mode : mode + 1] == float(abs(step)), filling, 0.0)
            row = row + weight * chosen[mode : mode + 1, :]
        wide = jnp.broadcast_to(jnp.concatenate([row, row], axis=1), (points, 2 * points))
        circles[step] = pltpu.roll(wide, 0, 1, stride=1, stride_axis=0)[:, :points]
    nothing = jnp.zeros((points, points), jnp.float32)
    plain = jnp.concatenate(
        [
            jnp.concatenate([circles.get(out - level, nothing) for out in range(levels)], axis=1)
            for level in range(levels)
        ],
        axis=0,
    ).astype(jnp.bfloat16)

    at = lax.broadcasted_iota(jnp.int32, (size, 1), 0)
    device, energy = at >> (states.bit_length() - 1), (at & (states - 1)) >> (momenta.bit_length() - 1)
    energy = (device >> (shares.bit_length() - 1)) * energies + energy
    state = (energy * shares + (device & (shares - 1))) * momenta + (at & (momenta - 1))
    pick = state == lax.broadcasted_iota(jnp.int32, (size, levels * points), 1)
    pick = jnp.where(pick, 1.0, 0.0).astype(jnp.bfloat16)
    half = jnp.dot(pick, plain, preferred_element_type=jnp.float32).astype(jnp.bfloat16)
    full = lax.dot_general(
        pick, half, (((1,), (1,)), ((), ())), preferred_element_type=jnp.float32
    )
    out_ref[...] = full.astype(out_ref.dtype)


def params():
    return pltpu.CompilerParams(vmem_limit_bytes=VMEM_BYTES)


VECTORS = pl.BlockSpec(memory_space=pltpu.VMEM)
SLABS = pl.BlockSpec(memory_space=pl.ANY)


def build(coupling, occupation, shift, region_map, groups, shares, momenta, energies):
    size, points = groups * shares * energies * momenta, shares * momenta
    rows = coupling.shape[0] * coupling.shape[1]
    small = jnp.pad(coupling.reshape(rows, points), ((0, 3), (0, 0)))
    for at, part in enumerate((occupation, shift, region_map)):
        part = jnp.pad(part[None, :], ((rows + at, 2 - at), (0, points - part.shape[0])))
        small = small + part.astype(jnp.float32)
    return pl.pallas_call(
        functools.partial(build_kernel, groups, shares, momenta, energies, coupling.shape[0]),
        out_shape=jax.ShapeDtypeStruct((size, size), jnp.bfloat16),
        in_specs=[VECTORS],
        out_specs=VECTORS,
        compiler_params=params(),
        cost_estimate=pl.CostEstimate(
            flops=440 * size * size * points, bytes_accessed=88 * size * size, transcendentals=0
        ),
        name="build",
    )(small)


def pack(matrix, lesser, greater, pieces, rows):
    energies, _, momenta, _, columns = lesser.shape
    size = energies * momenta * rows
    return pl.pallas_call(
        pack_kernel,
        out_shape=jax.ShapeDtypeStruct((2 * pieces, size, columns), lesser.dtype),
        in_specs=[SLABS, VECTORS, VECTORS],
        out_specs=VECTORS,
        compiler_params=params(),
        name="pack",
    )(matrix, lesser, greater)


def unpack(packed, shape, pieces, rows):
    energies, _, momenta, _, columns = shape
    out = jax.ShapeDtypeStruct(shape, packed.dtype)
    return pl.pallas_call(
        unpack_kernel,
        out_shape=(out, out),
        in_specs=[VECTORS],
        out_specs=(SLABS, SLABS),
        scratch_shapes=[
            pltpu.VMEM((2, energies, momenta, pieces * rows, columns), packed.dtype),
            pltpu.SemaphoreType.DMA((2, math.gcd(pieces, 8))),
        ],
        compiler_params=params(),
        name="unpack",
    )(packed)


def mix(matrix, received):
    return pl.pallas_call(
        mix_kernel,
        out_shape=jax.ShapeDtypeStruct(received.shape, received.dtype),
        in_specs=[VECTORS, VECTORS],
        out_specs=VECTORS,
        compiler_params=params(),
        name="mix",
    )(matrix, received)


def exchange(array):
    return lax.all_to_all(array, AXES, split_axis=0, concat_axis=0, tiled=True)


def by_rows(lesser, greater, coupling, occupation, shift, region_map, groups, shares):
    pieces = groups * shares // 2
    rows = lesser.shape[3] // pieces
    matrix = build(
        coupling, occupation, shift, region_map, groups, shares, lesser.shape[2], lesser.shape[0]
    )
    sent = pack(matrix, lesser, greater, pieces, rows)
    returned = exchange(mix(matrix, exchange(sent)))
    return unpack(returned, lesser.shape, pieces, rows)


def with_halo(shard, sides, width):
    for axis, dim in sides:
        size, length = (lax.axis_size(axis), shard.shape[dim])
        up = [(i, (i + 1) % size) for i in range(size - 1)]
        down = [(j, i) for i, j in up]
        last = lax.slice_in_dim(shard, length - width, length, axis=dim)
        first = lax.slice_in_dim(shard, 0, width, axis=dim)
        before = lax.ppermute(last, axis, up)
        after = lax.ppermute(first, axis, down)
        shard = jnp.concatenate([before, shard, after], axis=dim)
    return shard


def dft_basis(points):
    row_index = lax.broadcasted_iota(jnp.int32, (points, points), 0)
    col_index = lax.broadcasted_iota(jnp.int32, (points, points), 1)
    angles = (row_index * col_index % points).astype(jnp.float32) * (2.0 * math.pi / points)
    return jnp.concatenate([jnp.cos(angles), jnp.sin(angles)], axis=0)


def coupling_spectrum(coupling, region_map, basis):
    regions = coupling.shape[0]
    points = coupling.shape[2]
    onehot = (region_map[:, None] == jnp.arange(regions, dtype=jnp.int32)[None, :]).astype(
        jnp.float32
    )
    chosen = jnp.einsum("br,rmq->bmq", onehot, coupling, precision=lax.Precision.HIGHEST)
    spectrum = jnp.einsum("pq,bmq->bmp", basis, chosen, precision=lax.Precision.HIGHEST)
    return (spectrum[:, :, :points], -spectrum[:, :, points:])


def forward(stacked, basis_low):
    points = stacked.shape[3]
    columns = stacked.shape[5] // 2
    mixture = jnp.einsum(
        "pk,aebkxw->aebpxw", basis_low, stacked, preferred_element_type=jnp.float32
    )
    cosine = mixture[:, :, :, :points]
    sine = mixture[:, :, :, points:]
    return (
        cosine[..., :columns] + sine[..., columns:],
        cosine[..., columns:] - sine[..., :columns],
    )


def combine(hat_real, hat_imag, spec_real, spec_imag, occupation, shift, energies):
    out_shape = (2, energies) + hat_real.shape[2:]
    sigma_real = jnp.zeros(out_shape, jnp.float32)
    sigma_imag = jnp.zeros(out_shape, jnp.float32)
    points = spec_real.shape[2]
    for phonon in range(occupation.shape[0]):
        offset = shift[phonon]
        filling = occupation[phonon]
        lower_real = lax.dynamic_slice_in_dim(hat_real, SMAX - offset, energies, 1)
        lower_imag = lax.dynamic_slice_in_dim(hat_imag, SMAX - offset, energies, 1)
        upper_real = lax.dynamic_slice_in_dim(hat_real, SMAX + offset, energies, 1)
        upper_imag = lax.dynamic_slice_in_dim(hat_imag, SMAX + offset, energies, 1)
        weight_low = jnp.stack([filling, filling + 1.0]).reshape(2, 1, 1, 1, 1, 1)
        weight_high = jnp.stack([filling + 1.0, filling]).reshape(2, 1, 1, 1, 1, 1)
        mixed_real = weight_low * lower_real + weight_high * upper_real
        mixed_imag = weight_low * lower_imag + weight_high * upper_imag
        factor_real = spec_real[:, phonon, :].reshape(1, 1, -1, points, 1, 1)
        factor_imag = spec_imag[:, phonon, :].reshape(1, 1, -1, points, 1, 1)
        sigma_real = sigma_real + factor_real * mixed_real - factor_imag * mixed_imag
        sigma_imag = sigma_imag + factor_real * mixed_imag + factor_imag * mixed_real
    return (sigma_real, sigma_imag)


def inverse(sigma_real, sigma_imag, basis_low):
    points = sigma_real.shape[3]
    columns = sigma_real.shape[5]
    spectral = jnp.concatenate([sigma_real, sigma_imag], axis=-1).astype(jnp.bfloat16)
    mixture = jnp.einsum(
        "pk,aebkxw->aebpxw", basis_low, spectral, preferred_element_type=jnp.float32
    )
    cosine = mixture[:, :, :, :points]
    sine = mixture[:, :, :, points:]
    real_part = cosine[..., :columns] - sine[..., columns:]
    imag_part = cosine[..., columns:] + sine[..., :columns]
    return (jnp.concatenate([real_part, imag_part], axis=-1) * (1.0 / points)).astype(jnp.bfloat16)


def by_groups(lesser, greater, coupling, occupation, shift, region_map):
    stacked = jnp.stack([lesser, greater])
    widened = with_halo(stacked, (("grp", 1),), SMAX)
    regrouped = lax.all_to_all(widened, "mom", split_axis=4, concat_axis=3, tiled=True)
    points = regrouped.shape[3]
    basis = dft_basis(points)
    basis_low = basis.astype(jnp.bfloat16)
    spec_real, spec_imag = coupling_spectrum(coupling, region_map, basis)
    hat_real, hat_imag = forward(regrouped, basis_low)
    sigma_real, sigma_imag = combine(
        hat_real, hat_imag, spec_real, spec_imag, occupation, shift, lesser.shape[0]
    )
    result = inverse(sigma_real, sigma_imag, basis_low)
    returned = lax.all_to_all(result, "mom", split_axis=3, concat_axis=4, tiled=True)
    return (returned[0], returned[1])


def on_device(groups, shares, lesser, greater, coupling, occupation, shift, region_map):
    energies, blocks, momenta, height, columns = lesser.shape
    devices = groups * shares
    states = energies * momenta
    whole_tiles = (
        blocks == 1
        and devices >= 4
        and devices & (devices - 1) == 0
        and height % (TILE * (devices // 2)) == 0
        and TILE % states == 0
        and columns % 128 == 0
    )
    if whole_tiles:
        return by_rows(
            lesser, greater, coupling, occupation, shift, region_map, groups, shares
        )
    return by_groups(lesser, greater, coupling, occupation, shift, region_map)


def solution(mesh):
    return jax.shard_map(
        functools.partial(on_device, mesh.shape["grp"], mesh.shape["mom"]),
        mesh=mesh,
        in_specs=(
            P("grp", None, "mom", None, None),
            P("grp", None, "mom", None, None),
            P(),
            P(),
            P(),
            P(),
        ),
        out_specs=(P("grp", None, "mom", None, None), P("grp", None, "mom", None, None)),
        check_vma=False,
    )
```
